128 devices in a mesh: dp: 32 (over x, z, core), mp: 4 (over y).
Axes of the slice: x: 4, y: 4, z: 4, core: 2. Of those that a mesh axis runs over, the one named last changes fastest.
Arguments:
- tokens: bfloat16 [73728, 768], P('dp'), may hold values from -6 to 6
- qkv_weight: bfloat16 [3, 768, 768], P(None, None, 'mp'), may hold values from -0.21875 to 0.21875
- qkv_bias: bfloat16 [2, 768], P(None, 'mp'), may hold values from -0.59765625 to 0.59765625
- out_weight: bfloat16 [768, 768], P('mp'), may hold values from -0.4375 to 0.4375
- out_bias: bfloat16 [768], replicated, may hold values from -2 to 2
- up_weight: bfloat16 [768, 3072], P(None, 'mp'), may hold values from -0.21875 to 0.21875
- up_bias: bfloat16 [3072], P('mp'), may hold values from -2 to 2
- down_weight: bfloat16 [3072, 768], P('mp'), may hold values from -0.109375 to 0.109375
- down_bias: bfloat16 [768], replicated, may hold values from -2 to 2
- norm_gains: float32 [2, 768], replicated, may hold values from 0.25 to 1.75
- norm_biases: float32 [2, 768], replicated, may hold values from -2 to 2
- cotangent: bfloat16 [73728, 768], P('dp'), may hold values from -6 to 6
- band_masks: int32 [128, 4], P('dp'), may hold values from 0 to 1, as said below
Outputs:
- result: bfloat16 [73728, 768], P('dp')
- input_grad: float32 [73728, 768], P('dp')
- qkv_weight_grad: float32 [3, 768, 768], P(None, None, 'mp')
- qkv_bias_grad: float32 [2, 768], P(None, 'mp')
- out_weight_grad: float32 [768, 768], P('mp')
- out_bias_grad: float32 [768], replicated
- up_weight_grad: float32 [768, 3072], P(None, 'mp')
- up_bias_grad: float32 [3072], P('mp')
- down_weight_grad: float32 [3072, 768], P('mp')
- down_bias_grad: float32 [768], replicated
- norm_gains_grad: float32 [2, 768], replicated
- norm_biases_grad: float32 [2, 768], replicated
The draws below stay inside these ranges and needn't reach their ends.
Inputs may be any that keep to these rules, and one draw needn't show every extreme that they name: `band_masks`: each sample has 2 to 4 groups marked 1.
All inputs are finite; a program needn't handle non-finite values.
Results may differ from the reference program's by a relative error of at most 0.0095.
Values may be sent and summed in bfloat16 or wider, within the bound.
No kernel may reach another device: no remote copies, remote signals or barrier semaphores. Data moves between devices by JAX's collectives and lax.ppermute only.
A program may use at most 192 MiB of HBM per device.

```python
import jax
import jax.numpy as jnp
from jax import lax

D = 768
HEADS = 12
HEAD = 64
FF = 3072
SPATIAL = 144
GROUPS = 4
SEQ = 576
SAMPLES = 128
TOKENS = 73728


def draw_band_masks(key, part):
    key = jax.random.fold_in(key, 7)
    missing_key, order_key = jax.random.split(key)
    missing = jax.random.randint(missing_key, (SAMPLES, 1), 0, 3)
    scores = jax.random.randint(order_key, (SAMPLES, GROUPS), 0, 1000) * GROUPS + jnp.arange(GROUPS)[None, :]
    ranking = jnp.argsort(jnp.argsort(scores, axis=1), axis=1)
    return (ranking >= missing).astype(jnp.int32)


def shard_levels(own_key, shape, pieces, low, high):
    loudness = 1.0
    for dim, shards_of in pieces:
        draws = jax.random.uniform(jax.random.fold_in(jax.random.fold_in(own_key, 6), dim), (shards_of,), jnp.float32, low / len(pieces), high / len(pieces))
        loudness = loudness * jnp.repeat(jnp.exp(draws), shape[dim] // shards_of).reshape((-1,) + (1,) * (len(shape) - 1 - dim))
    return loudness


def scatter_about(own_key, extent, deviation, reach, cuts=(), kind=jnp.bfloat16):
    level = shard_levels(own_key, extent, cuts, -0.22, 0.18) if cuts else 1.0
    array = jax.random.normal(own_key, extent, jnp.float32) * deviation * level
    return jnp.minimum(jnp.maximum(array, -reach), reach).astype(kind)


def setup_inputs(seed: int = 0) -> dict:
    key_of = jax.random.split(jax.random.key(seed), 14)
    return {
        "tokens": scatter_about(key_of[0], (TOKENS, D), 1.0, 6.0, ((0, 32),)),
        "qkv_weight": scatter_about(key_of[1], (3, D, D), D ** -0.5, 0.21875, ((2, 4),)),
        "qkv_bias": scatter_about(key_of[2], (2, D), 0.1, 0.59765625, ((1, 4),)),
        "out_weight": scatter_about(key_of[3], (D, D), (D // 4) ** -0.5, 0.4375, ((0, 4),)),
        "out_bias": scatter_about(key_of[4], (D,), 0.3, 2.0),
        "up_weight": scatter_about(key_of[5], (D, FF), D ** -0.5, 0.21875, ((1, 4),)),
        "up_bias": scatter_about(key_of[6], (FF,), 0.3, 2.0, ((0, 4),)),
        "down_weight": scatter_about(key_of[7], (FF, D), FF ** -0.5, 0.109375, ((0, 4),)),
        "down_bias": scatter_about(key_of[8], (D,), 0.3, 2.0),
        "norm_gains": jnp.clip(1.0 + 0.15 * jax.random.normal(key_of[9], (2, D), jnp.float32), 0.25, 1.75),
        "norm_biases": scatter_about(key_of[10], (2, D), 0.3, 2.0, (), jnp.float32),
        "cotangent": scatter_about(key_of[11], (TOKENS, D), 1.0, 6.0, ((0, 32),)),
        "band_masks": draw_band_masks(jax.random.fold_in(key_of[13], 71), 0),
    }


@jax.custom_vjp
def low(v):
    return lax.optimization_barrier(v.astype(jnp.bfloat16)).astype(jnp.float32)

@jax.custom_vjp
def low_back(v):
    return v

def low_keep(v):
    return (low(v), None)

def low_pass(kept, grad):
    return (grad,)

def back_keep(v):
    return (v, None)

def back_low(kept, grad):
    return (low(grad),)
low.defvjp(low_keep, low_pass)
low_back.defvjp(back_keep, back_low)
highest = lax.Precision.HIGHEST

def round_both(value):
    return low_back(low(value))

def matmul(left, right):
    return jnp.dot(left, right, precision=highest)

def layer_norm(value, gain, shift):
    centred = value - lax.optimization_barrier(jnp.mean(value, axis=-1, keepdims=True))
    scaled = centred * lax.rsqrt(lax.optimization_barrier(jnp.mean(centred * centred, axis=-1, keepdims=True)) + 1e-05)
    return scaled * gain + shift

def attend_sample(packed):
    queries, key_rows, value_rows, key_valid = packed
    scores = jnp.einsum('qhd,khd->hqk', queries, key_rows, precision=highest) * HEAD ** (-0.5)
    scores = low_back(scores)
    scores = jnp.where(key_valid[None, None, :] > 0, scores, -1e+30)
    peak = lax.optimization_barrier(jnp.max(scores, axis=-1, keepdims=True))
    expos = jnp.exp(scores - peak)
    weights = low(expos / lax.optimization_barrier(jnp.sum(expos, axis=-1, keepdims=True)))
    return jnp.einsum('hqk,khd->qhd', weights, value_rows, precision=highest)

def forward(token_f, qkv_w, qkv_b, out_w, out_b, up_w, up_b, down_w, down_b, gains, shifts, keep_rows):
    rows = token_f.shape[0]
    samples = rows // SEQ
    first_in = low(layer_norm(token_f, gains[0], shifts[0]))
    queries = round_both(matmul(first_in, qkv_w[0]) + qkv_b[0])
    key_rows = round_both(matmul(first_in, qkv_w[1]))
    value_rows = round_both(matmul(first_in, qkv_w[2]) + qkv_b[1])
    shaped = (samples, SEQ, HEADS, HEAD)
    mixed = lax.map(jax.checkpoint(attend_sample), (queries.reshape(shaped), key_rows.reshape(shaped), value_rows.reshape(shaped), keep_rows.reshape(samples, SEQ)))
    heads_out = round_both(mixed.reshape(rows, D))
    branch = low_back(matmul(heads_out, out_w) + out_b)
    middle = token_f + branch
    second_in = low(layer_norm(middle, gains[1], shifts[1]))
    hidden = low_back(matmul(second_in, up_w) + up_b)
    active = low(jax.nn.gelu(hidden, approximate=False))
    feed = low_back(matmul(active, down_w) + down_b)
    return keep_rows[:, None] * (middle + feed)

def reference(tokens, qkv_weight, qkv_bias, out_weight, out_bias, up_weight, up_bias, down_weight, down_bias, norm_gains, norm_biases, cotangent, band_masks):
    keep_rows = jnp.repeat(band_masks, SPATIAL, axis=1).reshape(-1).astype(jnp.float32)
    primals = (tokens.astype(jnp.float32), qkv_weight.astype(jnp.float32), qkv_bias.astype(jnp.float32), out_weight.astype(jnp.float32), out_bias.astype(jnp.float32), up_weight.astype(jnp.float32), up_bias.astype(jnp.float32), down_weight.astype(jnp.float32), down_bias.astype(jnp.float32), norm_gains.astype(jnp.float32), norm_biases.astype(jnp.float32))

    def wrapped(*params):
        return forward(*params, keep_rows)
    output, pullback = jax.vjp(wrapped, *primals)
    grads = pullback(cotangent.astype(jnp.float32))
    return (output.astype(jnp.bfloat16), grads[0], grads[1], grads[2], grads[3], grads[4], grads[5], grads[6], grads[7], grads[8], grads[9], grads[10])
```

```python
import functools

import jax
import jax.numpy as jnp
import numpy as np
from jax import lax
from jax.experimental import pallas as pl
from jax.experimental.pallas import tpu as pltpu
from jax.sharding import Mesh, PartitionSpec as P

BF = jnp.bfloat16
F32 = jnp.float32
SEQ = 576
SPATIAL = 144
D = 768
HD = 64
LH = 3
LW = 192
HALF_FF = 384
ROWS = 192
VMEM = 56 * 2**20
NEG = -1e30
SCALE = HD**-0.5
ORDER = (0, 1, 3, 2)


def nt(a, b):
    return lax.dot_general(a, b, (((1,), (1,)), ((), ())), preferred_element_type=F32)


def nn(a, b):
    return lax.dot_general(a, b, (((1,), (0,)), ((), ())), preferred_element_type=F32)


def tn(a, b):
    return lax.dot_general(a, b, (((0,), (0,)), ((), ())), preferred_element_type=F32)


def normalize(value):
    centred = value - jnp.mean(value, axis=-1, keepdims=True)
    inverse = lax.rsqrt(jnp.mean(centred * centred, axis=-1, keepdims=True) + 1e-05)
    return centred * inverse, inverse


def norm_back(grad_out, scaled, inverse, gain):
    scaled_grad = grad_out * gain
    centre = jnp.mean(scaled_grad, axis=-1, keepdims=True)
    along = jnp.mean(scaled_grad * scaled, axis=-1, keepdims=True)
    return inverse * (scaled_grad - centre - scaled * along)


def colsum(value):
    return jnp.sum(value, axis=0, keepdims=True)


def call(body, outs, *args, scratch=(), specs=None, flops=0, name=None):
    shapes = [jax.ShapeDtypeStruct(s, d) for s, d in outs]
    moved = sum(int(np.prod(a.shape)) * a.dtype.itemsize for a in list(args) + shapes)
    return pl.pallas_call(
        body,
        grid=(1,),
        out_shape=shapes,
        in_specs=[
            (specs or {}).get(i, pl.BlockSpec(memory_space=pltpu.VMEM)) for i in range(len(args))
        ],
        out_specs=[pl.BlockSpec(memory_space=pltpu.VMEM) for _ in shapes],
        scratch_shapes=list(scratch),
        compiler_params=pltpu.CompilerParams(vmem_limit_bytes=VMEM),
        cost_estimate=pl.CostEstimate(flops=flops, bytes_accessed=moved, transcendentals=0),
        name=name,
    )(*args)


def attend_forward_body(first, *refs):
    if first:
        x, gain, shift, wm, wp, mrow, h1, w, qkv, o, lrow, lcol = refs
        for r in range(0, SEQ, 96):
            scaled, _ = normalize(x[r : r + 96, :].astype(F32))
            h1[r : r + 96, :] = (scaled * gain[0:1, :] + shift[0:1, :]).astype(BF)
    else:
        h1, wm, wp, mrow, w, qkv, o, lrow, lcol = refs
    for g in range(12):
        w[64 * g : 64 * g + 32, :] = wm[32 * g : 32 * g + 32, :]
        w[64 * g + 32 : 64 * g + 64, :] = wp[32 * g : 32 * g + 32, :]
    bias = (wm[384:385, :] + wp[385:386, :])[:, : 3 * LW].astype(F32)
    for r in range(0, SEQ, ROWS):
        qkv[r : r + ROWS, :] = (nt(h1[r : r + ROWS, :], w[0 : 3 * LW, :]) + bias).astype(BF)
    for h in range(LH):
        a = HD * h
        keys = qkv[:, LW + a : LW + a + HD]
        vals = qkv[:, 2 * LW + a : 2 * LW + a + HD]
        for r in range(0, SEQ, ROWS):
            queries = qkv[r : r + ROWS, a : a + HD] * jnp.asarray(SCALE, BF)
            scores = nt(queries, keys) + mrow[...]
            peak = jnp.max(scores, axis=-1, keepdims=True)
            expos = jnp.exp(scores - peak)
            total = jnp.sum(expos, axis=-1, keepdims=True)
            probs = (expos * (1.0 / total)).astype(BF)
            o[r : r + ROWS, a : a + HD] = nn(probs, vals).astype(BF)
            lcol[r : r + ROWS, h : h + 1] = peak + jnp.log(total)
    lrow[...] = lcol[...].T[0:8, 0:SEQ]


def attend_forward(first, lead, wm, wp, mrow):
    outs = [((D, D), BF), ((SEQ, 3 * LW), BF), ((SEQ, LW), BF), ((8, SEQ), F32)]
    if first:
        outs = [((SEQ, D), BF)] + outs
    return call(
        functools.partial(attend_forward_body, first),
        outs,
        *lead,
        wm,
        wp,
        mrow,
        scratch=[pltpu.VMEM((640, 128), F32)],
        flops=int(2e9),
        name="attend_forward",
    )


def middle_body(*refs):
    x, bias, gain, shift = refs[:4]
    outs_of = refs[4:8]
    weights = refs[8:12]
    mid, h2 = refs[12:]
    for r in range(0, SEQ, ROWS):
        total = x[r : r + ROWS, :].astype(F32) + bias[...].astype(F32)
        for k in range(4):
            total = total + nn(outs_of[k][r : r + ROWS, :], weights[k][...])
        mid[r : r + ROWS, :] = total
        scaled, _ = normalize(total)
        h2[r : r + ROWS, :] = (scaled * gain[1:2, :] + shift[1:2, :]).astype(BF)


OUT_ROWS = pl.BlockSpec((LW, D), lambda i: (3, 0))
QKV_ROWS = pl.BlockSpec((3 * LW, D), lambda i: (0, 0))


def feed_body(*refs):
    h2o, h2p, dyo, dyp = refs[:4]
    uds = refs[4:8]
    grads, mo, mp, dho, dhp, ubias = refs[8:14]
    h2, dy, wu, wd, act, dhid, accm, acch = refs[14:]
    h2[0:SEQ, :] = h2o[...]
    h2[SEQ:, :] = h2p[...]
    dy[0:SEQ, :] = dyo[...]
    dy[SEQ:, :] = dyp[...]
    block = 288
    for pair in range(2):
        one, two = uds[2 * pair], uds[2 * pair + 1]
        wu[0:HALF_FF, :] = one[0:HALF_FF, :]
        wu[HALF_FF:, :] = two[0:HALF_FF, :]
        wd[0:HALF_FF, :] = one[HALF_FF : 2 * HALF_FF, :]
        wd[HALF_FF:, :] = two[HALF_FF : 2 * HALF_FF, :]
        bias = jnp.concatenate(
            [one[768:769, 0:HALF_FF], two[768:769, 0:HALF_FF]], axis=1
        ).astype(F32)
        ubias[pair] = jnp.zeros((8, D), F32)

        @pl.loop(0, 2 * SEQ // block)
        def _(i):
            at = pl.ds(pl.multiple_of(i * block, block), block)
            hid = nt(h2[at, :], wu[...]) + bias
            cdf = 0.5 + 0.5 * lax.erf(hid * np.float32(0.7071067811865476))
            active = (hid * cdf).astype(BF)
            slope = cdf + hid * (
                jnp.exp(hid * hid * np.float32(-0.5)) * np.float32(0.3989422804014327)
            )
            act[at, :] = active
            hid_grad = (nt(dy[at, :], wd[...]) * slope).astype(BF)
            dhid[at, :] = hid_grad
            ubias[pair, 0:1, :] += colsum(hid_grad.astype(F32))
            down = nn(active, wd[...])
            back = nn(hid_grad, wu[...])
            if pair == 0:
                accm[at, :] = down
                acch[at, :] = back
            else:
                accm[at, :] += down
                acch[at, :] += back

        for s in range(2):
            k = ORDER[2 * pair + s]
            cols = slice(s * HALF_FF, (s + 1) * HALF_FF)
            up_grad = tn(dhid[:, cols], h2[...]).astype(BF)
            down_grad = tn(act[:, cols], dy[...]).astype(BF)
            for q in range(8):
                grads[q, k] = up_grad[48 * q : 48 * q + 48, :]
                grads[8 + q, k] = down_grad[48 * q : 48 * q + 48, :]
    mo[...] = accm[0:SEQ, :]
    mp[...] = accm[SEQ:, :]
    dho[...] = acch[0:SEQ, :]
    dhp[...] = acch[SEQ:, :].astype(BF)


def feed(h2o, h2p, dyo, dyp, uds):
    big = (2 * SEQ, D)
    return call(
        feed_body,
        [
            ((16, 4, 48, D), BF),
            ((SEQ, D), F32),
            ((SEQ, D), F32),
            ((SEQ, D), F32),
            ((SEQ, D), BF),
            ((2, 8, D), F32),
        ],
        h2o,
        h2p,
        dyo,
        dyp,
        *[uds[k] for k in ORDER],
        scratch=[
            pltpu.VMEM(big, BF),
            pltpu.VMEM(big, BF),
            pltpu.VMEM((D, D), BF),
            pltpu.VMEM((D, D), BF),
            pltpu.VMEM(big, BF),
            pltpu.VMEM(big, BF),
            pltpu.VMEM(big, F32),
            pltpu.VMEM(big, F32),
        ],
        flops=int(17e9),
        name="feed",
    )


def middle_back_body(*refs):
    dho, dhp, mid, gain, dy = refs[:5]
    outs_of = refs[5:9]
    weights = refs[9:13]
    dmid, gm, gp, small = refs[13:17]
    outs_grad = refs[17:21]
    da = refs[21]
    gain_sum = shift_sum = bias_sum = down_sum = jnp.zeros((1, D), F32)
    for r in range(0, SEQ, ROWS):
        at = slice(r, r + ROWS)
        grad = dho[at, :] + dhp[at, :].astype(F32)
        scaled, inverse = normalize(mid[at, :])
        out_grad = dy[at, :].astype(F32)
        total = out_grad + norm_back(grad, scaled, inverse, gain[1:2, :])
        dmid[at, :] = total
        low = total.astype(BF)
        da[at, :] = low
        gain_sum += colsum(grad * scaled)
        shift_sum += colsum(grad)
        bias_sum += colsum(low.astype(F32))
        down_sum += colsum(out_grad)
        for k in range(4):
            outs_grad[k][at, :] = nt(low, weights[k][...]).astype(BF)
    for k in range(4):
        weight_grad = tn(outs_of[k][...], da[...]).astype(BF)
        for h in range(LH):
            gm[k, 32 * h : 32 * h + 32, :] = weight_grad[64 * h : 64 * h + 32, :]
            gp[k, 32 * h : 32 * h + 32, :] = weight_grad[64 * h + 32 : 64 * h + 64, :]
    small[...] = jnp.concatenate(
        [gain_sum, shift_sum, bias_sum, down_sum, jnp.zeros((4, D), F32)], axis=0
    )


def attend_backward_body(qkv, lrow, o, do, mcol, h1, dqkv, gm, gp, bias, dcol, dq):
    for h in range(LH):
        a = HD * h
        dcol[0:SEQ, h : h + 1] = jnp.sum(
            do[:, a : a + HD].astype(F32) * o[:, a : a + HD].astype(F32), axis=-1, keepdims=True
        )
    drow = dcol[...].T[0:8, 0:SEQ]
    for h in range(LH):
        a = HD * h
        queries = qkv[:, a : a + HD] * jnp.asarray(SCALE, BF)
        heads_grad = do[:, a : a + HD]
        for r in range(0, SEQ, ROWS):
            at = slice(r, r + ROWS)
            keys = qkv[at, LW + a : LW + a + HD]
            vals = qkv[at, 2 * LW + a : 2 * LW + a + HD]
            scores = nt(keys, queries) + mcol[at, :]
            probs = jnp.exp(scores - lrow[h : h + 1, :])
            prob_grad = nt(vals, heads_grad)
            score_grad = (probs * (prob_grad - drow[h : h + 1, :])).astype(BF)
            dqkv[at, 2 * LW + a : 2 * LW + a + HD] = nn(probs.astype(BF), heads_grad).astype(BF)
            dqkv[at, LW + a : LW + a + HD] = nn(score_grad, queries).astype(BF)
            part = tn(score_grad, keys)
            if r == 0:
                dq[...] = part
            else:
                dq[...] += part
        dqkv[:, a : a + HD] = (dq[...] * SCALE).astype(BF)
    bias[...] = jnp.broadcast_to(colsum(dqkv[...].astype(F32)), (8, 3 * LW))
    for t in range(3):
        weight_grad = tn(dqkv[:, LW * t : LW * t + LW], h1[...]).astype(BF)
        for h in range(LH):
            g = 3 * t + h
            gm[32 * g : 32 * g + 32, :] = weight_grad[64 * h : 64 * h + 32, :]
            gp[32 * g : 32 * g + 32, :] = weight_grad[64 * h + 32 : 64 * h + 64, :]


def attend_backward(qkv, lrow, o, do, mcol, h1):
    return call(
        attend_backward_body,
        [((SEQ, 3 * LW), BF), ((288, D), BF), ((288, D), BF), ((8, 3 * LW), F32)],
        qkv,
        lrow,
        o,
        do,
        mcol,
        h1,
        scratch=[pltpu.VMEM((640, 128), F32), pltpu.VMEM((SEQ, HD), F32)],
        flops=int(3e9),
        name="attend_backward",
    )


def first_back_body(*refs):
    x, gain, dmid = refs[:3]
    dqkvs = refs[3:7]
    weights = refs[7:11]
    grad_in, small = refs[11:]
    gain_sum = shift_sum = jnp.zeros((1, D), F32)
    for r in range(0, SEQ, ROWS):
        at = slice(r, r + ROWS)
        grad = nn(dqkvs[0][at, :], weights[0][...])
        for k in range(1, 4):
            grad += nn(dqkvs[k][at, :], weights[k][...])
        scaled, inverse = normalize(x[at, :].astype(F32))
        total = dmid[at, :] + norm_back(grad, scaled, inverse, gain[0:1, :])
        grad_in[at, :] = total.astype(BF)
        gain_sum += colsum(grad * scaled)
        shift_sum += colsum(grad)
    small[...] = jnp.concatenate([gain_sum, shift_sum, jnp.zeros((6, D), F32)], axis=0)


def place_body(at, *refs):
    out = refs[4]
    for i in range(4):

        @pl.when(pl.program_id(0) == i)
        def _():
            out[...] = refs[i][...].astype(out.dtype)


def place(places, blocks, dtype):
    whole = pl.BlockSpec((SEQ, D), lambda i, at: (0, 0))
    return pl.pallas_call(
        place_body,
        grid_spec=pltpu.PrefetchScalarGridSpec(
            num_scalar_prefetch=1,
            grid=(4,),
            in_specs=[whole] * 4,
            out_specs=pl.BlockSpec((SEQ, D), lambda i, at: (at[i], 0)),
        ),
        out_shape=jax.ShapeDtypeStruct((4 * SEQ, D), dtype),
        compiler_params=pltpu.CompilerParams(vmem_limit_bytes=VMEM),
        name="place",
    )(places, *blocks)


def along_y(value, step):
    return lax.ppermute(value, "y", [(i, (i + step) % 4) for i in range(4)])


def other_core(value):
    return lax.ppermute(value, "c", [(0, 1), (1, 0)])


def exchange_xz(value):
    return lax.all_to_all(value, ("x", "z"), 0, 0, tiled=True)


def spread_xz(piece):
    copies = jnp.broadcast_to(piece[None], (16,) + piece.shape)
    out = exchange_xz(copies)
    return out.reshape((-1,) + piece.shape[1:])


def per_device(
    tokens,
    qkv_weight,
    qkv_bias,
    out_weight,
    out_bias,
    up_weight,
    up_bias,
    down_weight,
    down_bias,
    norm_gains,
    norm_biases,
    cotangent,
    band_masks,
):
    core = lax.axis_index("c")
    here = lax.axis_index("y")
    places = ((here - jnp.arange(4)) % 4).astype(jnp.int32)

    def own(block):
        return lax.dynamic_slice_in_dim(block, here * SEQ, SEQ, 0)

    groups = jnp.concatenate(
        [jnp.swapaxes(qkv_weight, 1, 2), out_weight[None]], axis=0
    ).reshape(12, 2, 32, D)
    halves = jnp.swapaxes(groups, 0, 1).reshape(2, 384, D)
    bias_halves = jnp.swapaxes(qkv_bias.reshape(6, 2, 32), 0, 1)

    def heads_pack(c):
        values = lax.dynamic_index_in_dim(bias_halves, c, 0, False).reshape(2, 3, 32)
        padded = jnp.pad(values[jnp.array([0, 0, 1])] * jnp.array([1, 0, 1], BF)[:, None, None], ((0, 0), (0, 0), (0, 32)))
        mine = padded.reshape(1, 576)
        theirs = jnp.roll(mine, 32, axis=1)
        rows = jnp.pad(jnp.concatenate([mine, theirs], axis=0), ((0, 14), (0, D - 576)))
        return jnp.concatenate([lax.dynamic_index_in_dim(halves, c, 0, False), rows], axis=0)

    heads_mine = {0: heads_pack(core)}
    heads_theirs = {0: heads_pack(1 - core)}
    at = core * HALF_FF
    hidden_mine = {
        0: jnp.concatenate(
            [
                lax.dynamic_slice_in_dim(up_weight, at, HALF_FF, 1).T,
                lax.dynamic_slice_in_dim(down_weight, at, HALF_FF, 0),
                jnp.pad(
                    lax.dynamic_slice_in_dim(up_bias, at, HALF_FF, 0)[None],
                    ((0, 15), (0, D - HALF_FF)),
                ),
            ],
            axis=0,
        )
    }
    for s in ORDER[1:]:
        heads_mine[s] = along_y(heads_mine[0], s)
        heads_theirs[s] = other_core(heads_mine[s])
    for s in ORDER[1:]:
        hidden_mine[s] = along_y(hidden_mine[0], s)

    token_own = own(tokens)
    keep = jnp.repeat(lax.dynamic_index_in_dim(band_masks, here, 0, False), SPATIAL)
    keep_col = keep.astype(F32)[:, None]
    mask_col = jnp.where(keep_col > 0, 0.0, NEG)
    mask_row = mask_col.reshape(1, SEQ)
    out_grad = jnp.where(keep_col > 0, own(cotangent), jnp.asarray(0, BF))
    out_grad_other = other_core(out_grad)

    weights, qkvs, outs_of, logs = {}, {}, {}, {}
    first_in, *rest = attend_forward(
        True, (token_own, norm_gains, norm_biases), heads_mine[0], heads_theirs[0], mask_row
    )
    weights[0], qkvs[0], outs_of[0], logs[0] = rest
    for s in ORDER[1:]:
        weights[s], qkvs[s], outs_of[s], logs[s] = attend_forward(
            False, (first_in,), heads_mine[s], heads_theirs[s], mask_row
        )
    four = range(4)
    middle, second_in = call(
        middle_body,
        [((SEQ, D), F32), ((SEQ, D), BF)],
        token_own,
        out_bias[None],
        norm_gains,
        norm_biases,
        *[outs_of[k] for k in four],
        *[weights[k] for k in four],
        specs={8 + k: OUT_ROWS for k in four},
        flops=int(1e9),
        name="middle",
    )
    second_other = other_core(second_in)
    hidden_grads, down_own, down_other, back_own, back_other, up_sums = feed(
        second_in, second_other, out_grad, out_grad_other, hidden_mine
    )
    back_received = other_core(back_other)
    down_received = other_core(down_other)
    result_own = (
        keep_col * (middle + (down_own + down_received + down_bias.astype(F32)))
    ).astype(BF)

    pieces = jnp.sum(exchange_xz(hidden_grads).astype(F32), axis=0)
    hidden_piece = pieces[0]
    for s in ORDER[1:]:
        hidden_piece = hidden_piece + along_y(pieces[s], -s)
    hidden_half = spread_xz(hidden_piece.astype(BF))
    hidden_half_other = other_core(hidden_half)

    results = [result_own] + [along_y(result_own, s) for s in (1, 2, 3)]
    result = place(places, results, BF)

    middle_grad, out_gm, out_gp, small_two, *outs_grad = call(
        middle_back_body,
        [((SEQ, D), F32), ((4, 96, D), BF), ((4, 96, D), BF), ((8, D), F32)]
        + [((SEQ, LW), BF)] * 4,
        back_own,
        back_received,
        middle,
        norm_gains,
        out_grad,
        *[outs_of[k] for k in four],
        *[weights[k] for k in four],
        specs={9 + k: OUT_ROWS for k in four},
        scratch=[pltpu.VMEM((SEQ, D), BF)],
        flops=int(2e9),
        name="middle_back",
    )
    dqkvs, gms, gps, bias_sums = {}, {}, {}, {}
    for s in ORDER:
        dqkvs[s], gms[s], gps[s], bias_sums[s] = attend_backward(
            qkvs[s], logs[s], outs_of[s], outs_grad[s], mask_col, first_in
        )
    grad_own, small_one = call(
        first_back_body,
        [((SEQ, D), BF), ((8, D), F32)],
        token_own,
        norm_gains,
        middle_grad,
        *[dqkvs[k] for k in four],
        *[weights[k] for k in four],
        specs={7 + k: QKV_ROWS for k in four},
        flops=int(2e9),
        name="first_back",
    )
    grads_in = [grad_own] + [along_y(grad_own, s) for s in (1, 2, 3)]
    input_grad = place(places, grads_in, F32)

    both = [jnp.stack([bias_sums[k][0] for k in four]).reshape(4, 3, 3, 2, 32)[:, ::2]]
    bias_mine = both[0][:, :, :, 0].reshape(4, 192)
    bias_theirs = both[0][:, :, :, 1].reshape(4, 192)
    common = jnp.concatenate([small_one[0:2], small_two[0:4]], axis=0)

    def split_low(v):
        high = v.astype(BF)
        return high, (v - high.astype(F32)).astype(BF)

    def with_small(c_rows, k_rows):
        rows = jnp.concatenate(
            [c_rows, jnp.pad(k_rows, ((0, 0), (0, D - k_rows.shape[1])))], axis=0
        )
        high, low = split_low(rows)
        return jnp.pad(jnp.concatenate([high, low], axis=0), ((0, 12), (0, 0)))

    def from_small(v):
        return v[..., 0:10, :].astype(F32) + v[..., 10:20, :].astype(F32)

    mine = jnp.concatenate([jnp.stack([gms[k] for k in four]), out_gm], axis=1)
    theirs = jnp.concatenate([jnp.stack([gps[k] for k in four]), out_gp], axis=1)
    message = jnp.concatenate(
        [theirs.reshape(4 * 384, D), with_small(common, bias_theirs)], axis=0
    )
    received = other_core(message)
    heads_sum = mine.astype(F32) + received[: 4 * 384].reshape(4, 384, D).astype(F32)
    small_sum = from_small(received[4 * 384 :])
    common_sum = common + small_sum[0:6]
    bias_sum = bias_mine + small_sum[6:10, 0:192]
    up_rows = up_sums[:, 0, :].reshape(4, HALF_FF)
    up_rows = jnp.stack([up_rows[ORDER.index(k)] for k in four])
    k_rows = jnp.concatenate([up_rows, bias_sum], axis=1)
    send = jnp.swapaxes(heads_sum.reshape(4, 16, 24, D), 0, 1).reshape(16, 96, D).astype(BF)
    tail = with_small(common_sum, k_rows)
    send = jnp.concatenate([send, jnp.broadcast_to(tail[None], (16, 32, D))], axis=1)
    got = exchange_xz(send)
    heads_pieces = jnp.sum(got[:, 0:96].astype(F32), axis=0).reshape(4, 24, D)
    small_pieces = jnp.sum(from_small(got[:, 96:]), axis=0)
    common_row, k_row = small_pieces[0:6], small_pieces[6:10]

    def y_pack(k):
        return jnp.concatenate(
            [heads_pieces[k], common_row, k_row[k : k + 1], jnp.zeros((1, D), F32)], axis=0
        )

    total = y_pack(0)
    for s in ORDER[1:]:
        total = total + along_y(y_pack(s), -s)
    heads_half = spread_xz(total[0:24].astype(BF))
    common_total, k_total = total[24:30], total[30]
    k_high, k_low = split_low(k_total[None])
    heads_half_other = other_core(
        jnp.concatenate([heads_half, k_high, k_low, jnp.zeros((14, D), BF)], axis=0)
    )
    k_other = heads_half_other[384].astype(F32) + heads_half_other[385].astype(F32)
    heads_half_other = heads_half_other[0:384]

    def in_order(a, b, axis):
        return jnp.stack([jnp.where(core == 0, a, b), jnp.where(core == 0, b, a)], axis=axis)

    heads_full = in_order(heads_half.reshape(12, 32, D), heads_half_other.reshape(12, 32, D), 1)
    heads_full = heads_full.reshape(4, LW, D).astype(F32)
    qkv_weight_grad = jnp.swapaxes(heads_full[0:3], 1, 2)
    out_weight_grad = heads_full[3]
    hidden_full = in_order(hidden_half, hidden_half_other, 0).astype(F32)
    up_weight_grad = hidden_full[:, 0:HALF_FF].reshape(D, D).T
    down_weight_grad = hidden_full[:, HALF_FF:].reshape(D, D)
    up_bias_grad = in_order(k_total[0:HALF_FF], k_other[0:HALF_FF], 0).reshape(D)
    qkv_bias_grad = in_order(
        k_total[HALF_FF : HALF_FF + 192].reshape(2, 3, 32),
        k_other[HALF_FF : HALF_FF + 192].reshape(2, 3, 32),
        2,
    ).reshape(2, LW)
    return (
        result,
        input_grad,
        qkv_weight_grad,
        qkv_bias_grad,
        out_weight_grad,
        common_total[4],
        up_weight_grad,
        up_bias_grad,
        down_weight_grad,
        common_total[5],
        jnp.stack([common_total[0], common_total[2]]),
        jnp.stack([common_total[1], common_total[3]]),
    )


def solution(mesh):
    inner = Mesh(np.array(mesh.devices).reshape(4, 4, 2, 4), ("x", "z", "c", "y"))
    dp = ("x", "z", "c")
    in_specs = (
        P(dp, None),
        P(None, None, "y"),
        P(None, "y"),
        P("y", None),
        P(),
        P(None, "y"),
        P("y"),
        P("y", None),
        P(),
        P(),
        P(),
        P(dp, None),
        P(dp, None),
    )
    out_specs = (
        P(dp, None),
        P(dp, None),
        P(None, None, "y"),
        P(None, "y"),
        P("y", None),
        P(),
        P(None, "y"),
        P("y"),
        P("y", None),
        P(),
        P(),
        P(),
    )
    return jax.shard_map(
        per_device, mesh=inner, in_specs=in_specs, out_specs=out_specs, check_vma=False
    )
```

```python
import functools

import jax
import jax.numpy as jnp
import numpy as np
from jax import lax
from jax.experimental import pallas as pl
from jax.experimental.pallas import tpu as pltpu
from jax.sharding import Mesh, PartitionSpec as P

BF = jnp.bfloat16
F32 = jnp.float32
SEQ = 576
SPATIAL = 144
D = 768
HD = 64
LH = 3
LW = 192
HALF_FF = 384
ROWS = 192
VMEM = 56 * 2**20
NEG = -1e30
PER_MICRO = 1e6
SCALE = HD**-0.5
ORDER = (0, 1, 3, 2)


def nt(a, b):
    return lax.dot_general(a, b, (((1,), (1,)), ((), ())), preferred_element_type=F32)


def nn(a, b):
    return lax.dot_general(a, b, (((1,), (0,)), ((), ())), preferred_element_type=F32)


def tn(a, b):
    return lax.dot_general(a, b, (((0,), (0,)), ((), ())), preferred_element_type=F32)


def normalize(value):
    centred = value - jnp.mean(value, axis=-1, keepdims=True)
    inverse = lax.rsqrt(jnp.mean(centred * centred, axis=-1, keepdims=True) + 1e-05)
    return centred * inverse, inverse


def norm_back(grad_out, scaled, inverse, gain):
    scaled_grad = grad_out * gain
    centre = jnp.mean(scaled_grad, axis=-1, keepdims=True)
    along = jnp.mean(scaled_grad * scaled, axis=-1, keepdims=True)
    return inverse * (scaled_grad - centre - scaled * along)


def colsum(value):
    return jnp.sum(value, axis=0, keepdims=True)


def call(body, outs, scalars, *args, scratch=(), specs=None, micros=1.0, name=None):
    shapes = [jax.ShapeDtypeStruct(s, d) for s, d in outs]
    moved = sum(int(np.prod(a.shape)) * a.dtype.itemsize for a in list(args) + shapes)
    return pl.pallas_call(
        body,
        grid_spec=pltpu.PrefetchScalarGridSpec(
            num_scalar_prefetch=1,
            grid=(1,),
            in_specs=[
                (specs or {}).get(i, pl.BlockSpec(memory_space=pltpu.VMEM))
                for i in range(len(args))
            ],
            out_specs=[pl.BlockSpec(memory_space=pltpu.VMEM) for _ in shapes],
            scratch_shapes=list(scratch),
        ),
        out_shape=shapes,
        compiler_params=pltpu.CompilerParams(vmem_limit_bytes=VMEM),
        cost_estimate=pl.CostEstimate(
            flops=int(micros * PER_MICRO), bytes_accessed=moved // 1024, transcendentals=0
        ),
        name=name,
    )(scalars, *args)


OWN_ROWS = pl.BlockSpec((SEQ, D), lambda i, at: (at[3], 0))
OUT_ROWS = pl.BlockSpec((LW, D), lambda i, at: (3, 0))
QKV_ROWS = pl.BlockSpec((3 * LW, D), lambda i, at: (0, 0))
CORE, X_AT, Z_AT, Y_AT, MASKS = 0, 1, 2, 3, 4


def pack_body(
    at,
    qkv_weight,
    out_weight,
    qkv_bias,
    up_weight,
    down_weight,
    up_bias,
    mine,
    theirs,
    hidden,
    rows,
):
    core = lax.axis_index("c")
    for t in range(3):
        rows[LW * t : LW * t + LW, :] = qkv_weight[t]
    rows[3 * LW :, :] = out_weight[...]
    lane = lax.broadcasted_iota(jnp.int32, (8, D), 1)
    low = (lane % HD) < 32
    given = qkv_bias[...].astype(F32)
    none = jnp.zeros((1, LW), F32)
    bias = jnp.concatenate([given[0:1], none, given[1:2], none], axis=1)
    bias = jnp.broadcast_to(bias, (8, D))
    parts = (
        jnp.where(low, bias, 0.0),
        jnp.where(low, pltpu.roll(bias, D - 32, 1), 0.0),
    )

    def fill(ref, half):
        for g in range(12):
            ref[32 * g : 32 * g + 32, :] = rows[64 * g + 32 * half : 64 * g + 32 * half + 32, :]
        part = parts[half]
        shifted = pltpu.roll(part, 32, 1)
        ref[384:400, :] = jnp.concatenate(
            [part[0:1], shifted[0:1], jnp.zeros((14, D), F32)], axis=0
        ).astype(BF)

    @pl.when(core == 0)
    def _():
        fill(mine, 0)
        fill(theirs, 1)

    @pl.when(core != 0)
    def _():
        fill(mine, 1)
        fill(theirs, 0)

    start = pl.multiple_of(core * HALF_FF, HALF_FF)
    hidden[0:HALF_FF, :] = up_weight[:, pl.ds(start, HALF_FF)].T
    hidden[HALF_FF : 2 * HALF_FF, :] = down_weight[pl.ds(start, HALF_FF), :]
    up_row = up_bias[...].astype(F32).reshape(1, D)
    up_part = jnp.where(core == 0, up_row[:, 0:HALF_FF], up_row[:, HALF_FF:])
    hidden[2 * HALF_FF : 2 * HALF_FF + 16, :] = jnp.concatenate(
        [
            jnp.concatenate([up_part, jnp.zeros((1, D - HALF_FF), F32)], axis=1),
            jnp.zeros((15, D), F32),
        ],
        axis=0,
    ).astype(BF)


def masks_body(at, cot, dy, keep_col):
    kept = [at[MASKS + 4 * at[Y_AT] + g].astype(F32) for g in range(4)]
    for g in range(4):
        rows = slice(g * SPATIAL, (g + 1) * SPATIAL)
        dy[rows, :] = (cot[rows, :].astype(F32) * kept[g]).astype(BF)
        keep_col[rows, :] = jnp.full((SPATIAL, 1), kept[g])


def attend_forward_body(first, at, *refs):
    if first:
        x, gain, shift, wm, wp, keep, h1, w, qkv, o, logs = refs
        for r in range(0, SEQ, 96):
            scaled, _ = normalize(x[r : r + 96, :].astype(F32))
            h1[r : r + 96, :] = (scaled * gain[0:1, :] + shift[0:1, :]).astype(BF)
    else:
        h1, wm, wp, keep, w, qkv, o, logs = refs
    for g in range(12):
        w[64 * g : 64 * g + 32, :] = wm[32 * g : 32 * g + 32, :]
        w[64 * g + 32 : 64 * g + 64, :] = wp[32 * g : 32 * g + 32, :]
    bias = (wm[384:385, :] + wp[385:386, :])[:, : 3 * LW].astype(F32)
    for r in range(0, SEQ, ROWS):
        qkv[r : r + ROWS, :] = (nt(h1[r : r + ROWS, :], w[0 : 3 * LW, :]) + bias).astype(BF)
    mask = ((1.0 - keep[...]) * NEG).astype(BF)
    ones = jnp.ones((SEQ, 1), BF)
    rest = jnp.zeros((SEQ, HD - 1), BF)
    for h in range(LH):
        a = HD * h
        keys = jnp.concatenate([qkv[:, LW + a : LW + a + HD], mask, rest], axis=1)
        queries = jnp.concatenate(
            [qkv[:, a : a + HD] * jnp.asarray(SCALE, BF), ones, rest], axis=1
        )
        scores = nt(queries, keys)
        peak = jnp.max(scores, axis=-1, keepdims=True)
        expos = jnp.exp(scores - peak)
        total = jnp.sum(expos, axis=-1, keepdims=True)
        probs = (expos * (1.0 / total)).astype(BF)
        o[:, a : a + HD] = nn(probs, qkv[:, 2 * LW + a : 2 * LW + a + HD]).astype(BF)
        logs[:, h : h + 1] = peak + jnp.log(total)


def attend_forward(first, scalars, lead, wm, wp, keep):
    outs = [((D, D), BF), ((SEQ, 3 * LW), BF), ((SEQ, LW), BF), ((SEQ, 128), F32)]
    if first:
        outs = [((SEQ, D), BF)] + outs
    return call(
        functools.partial(attend_forward_body, first),
        outs,
        scalars,
        *lead,
        wm,
        wp,
        keep,
        specs={0: OWN_ROWS} if first else None,
        micros=8,
        name="attend_forward",
    )


def middle_body(at, *refs):
    x, bias, gain, shift = refs[:4]
    outs_of = refs[4:8]
    weights = refs[8:12]
    mid, h2 = refs[12:]
    for r in range(0, SEQ, ROWS):
        total = x[r : r + ROWS, :].astype(F32) + bias[...].astype(F32)
        for k in range(4):
            total = total + nn(outs_of[k][r : r + ROWS, :], weights[k][...])
        mid[r : r + ROWS, :] = total
        scaled, _ = normalize(total)
        h2[r : r + ROWS, :] = (scaled * gain[1:2, :] + shift[1:2, :]).astype(BF)


def feed_body(at, h2o, h2p, dyo, dyp, shards, grads, mo, mp, dho, dhp, ubias, *scratch):
    h2, dy, wu, wd, act, dhid, accm, acch = scratch
    owners = [lax.rem(at[Y_AT] + 4 - k, 4) for k in range(4)]
    h2[0:SEQ, :] = h2o[...]
    h2[SEQ:, :] = h2p[...]
    dy[0:SEQ, :] = dyo[...]
    dy[SEQ:, :] = dyp[...]
    block = 288
    for pair in range(2):
        one, two = (shards.at[owners[ORDER[2 * pair + s]]] for s in range(2))
        wu[0:HALF_FF, :] = one[0:HALF_FF, :]
        wu[HALF_FF:, :] = two[0:HALF_FF, :]
        wd[0:HALF_FF, :] = one[HALF_FF : 2 * HALF_FF, :]
        wd[HALF_FF:, :] = two[HALF_FF : 2 * HALF_FF, :]
        bias = jnp.concatenate(
            [one[768:784, 0:HALF_FF][0:1], two[768:784, 0:HALF_FF][0:1]], axis=1
        ).astype(F32)
        ubias[pair] = jnp.zeros((8, D), F32)

        @pl.loop(0, 2 * SEQ // block)
        def _(i):
            rows = pl.ds(pl.multiple_of(i * block, block), block)
            hid = nt(h2[rows, :], wu[...]) + bias
            cdf = 0.5 + 0.5 * lax.erf(hid * np.float32(0.7071067811865476))
            active = (hid * cdf).astype(BF)
            slope = cdf + hid * (
                jnp.exp(hid * hid * np.float32(-0.5)) * np.float32(0.3989422804014327)
            )
            act[rows, :] = active
            hid_grad = (nt(dy[rows, :], wd[...]) * slope).astype(BF)
            dhid[rows, :] = hid_grad
            ubias[pair, 0:1, :] += colsum(hid_grad.astype(F32))
            down = nn(active, wd[...])
            back = nn(hid_grad, wu[...])
            if pair == 0:
                accm[rows, :] = down
                acch[rows, :] = back
            else:
                accm[rows, :] += down
                acch[rows, :] += back

        for s in range(2):
            k = ORDER[2 * pair + s]
            cols = slice(s * HALF_FF, (s + 1) * HALF_FF)
            up_grad = tn(dhid[:, cols], h2[...])
            down_grad = tn(act[:, cols], dy[...])
            for q in range(8):
                rows = slice(48 * q, 48 * q + 48)
                grads[q, k] = up_grad[rows, :]
                grads[8 + q, k] = down_grad[rows, :]
    mo[...] = accm[0:SEQ, :]
    mp[...] = accm[SEQ:, :]
    dho[...] = acch[0:SEQ, :]
    dhp[...] = acch[SEQ:, :].astype(BF)


def feed(scalars, h2o, h2p, dyo, dyp, shards):
    big = (2 * SEQ, D)
    return call(
        feed_body,
        [
            ((16, 4, 48, D), F32),
            ((SEQ, D), F32),
            ((SEQ, D), F32),
            ((SEQ, D), F32),
            ((SEQ, D), BF),
            ((2, 8, D), F32),
        ],
        scalars,
        h2o,
        h2p,
        dyo,
        dyp,
        shards,
        scratch=[
            pltpu.VMEM(big, BF),
            pltpu.VMEM(big, BF),
            pltpu.VMEM((D, D), BF),
            pltpu.VMEM((D, D), BF),
            pltpu.VMEM(big, BF),
            pltpu.VMEM(big, BF),
            pltpu.VMEM(big, F32),
            pltpu.VMEM(big, F32),
        ],
        micros=30,
        name="feed",
    )


def result_body(at, middle, down, other, bias, keep, out):
    total = middle[...] + (down[...] + other[...] + bias[...].astype(F32))
    low = (keep[...] * total).astype(BF)
    for q in range(4):
        out[q] = low


def spread_body(at, a, b, c, d, out):
    total = ((a[...] + b[...]) + (c[...] + d[...])).astype(out.dtype)
    for q in range(16):
        out[q] = total


def hidden_out_body(at, mine, theirs, up, down):
    for ref, core in ((mine, at[CORE]), (theirs, 1 - at[CORE])):
        start = pl.multiple_of(core * HALF_FF, HALF_FF)
        half = jnp.concatenate([ref[q] for q in range(8)], axis=0).astype(F32)
        up[:, pl.ds(start, HALF_FF)] = half.T
        for q in range(8):
            row = pl.multiple_of(start + 48 * q, 16)
            down[pl.ds(row, 48), :] = ref[8 + q].astype(F32)


def middle_back_body(at, *refs):
    dho, dhp, mid, gain, dy = refs[:5]
    outs_of = refs[5:9]
    weights = refs[9:13]
    dmid, gm, gp, small = refs[13:17]
    outs_grad = refs[17:21]
    da = refs[21]
    gain_sum = shift_sum = bias_sum = down_sum = jnp.zeros((1, D), F32)
    for r in range(0, SEQ, ROWS):
        at = slice(r, r + ROWS)
        grad = dho[at, :] + dhp[at, :].astype(F32)
        scaled, inverse = normalize(mid[at, :])
        out_grad = dy[at, :].astype(F32)
        total = out_grad + norm_back(grad, scaled, inverse, gain[1:2, :])
        dmid[at, :] = total
        low = total.astype(BF)
        da[at, :] = low
        gain_sum += colsum(grad * scaled)
        shift_sum += colsum(grad)
        bias_sum += colsum(low.astype(F32))
        down_sum += colsum(out_grad)
        for k in range(4):
            outs_grad[k][at, :] = nt(low, weights[k][...]).astype(BF)
    for k in range(4):
        weight_grad = tn(outs_of[k][...], da[...])
        for h in range(LH):
            gm[k, 32 * h : 32 * h + 32, :] = weight_grad[64 * h : 64 * h + 32, :]
            gp[k, 32 * h : 32 * h + 32, :] = weight_grad[64 * h + 32 : 64 * h + 64, :]
    small[...] = jnp.concatenate(
        [gain_sum, shift_sum, bias_sum, down_sum, jnp.zeros((4, D), F32)], axis=0
    )


def in_three(value):
    one = value.astype(BF)
    left = value - one.astype(F32)
    two = left.astype(BF)
    return [one, two, (left - two.astype(F32)).astype(BF)]


def attend_backward_body(sc, qkv, logs, o, do, keep, h1, dqkv, gm, gp, bias):
    mask = ((1.0 - keep[...]) * NEG).astype(BF)
    ones = jnp.ones((SEQ, 3), BF)
    rest = jnp.zeros((SEQ, HD - 4), BF)
    for h in range(LH):
        a = HD * h
        heads_grad = do[:, a : a + HD]
        inner = jnp.sum(
            heads_grad.astype(F32) * o[:, a : a + HD].astype(F32), axis=-1, keepdims=True
        )
        keys = qkv[:, LW + a : LW + a + HD]
        vals = qkv[:, 2 * LW + a : 2 * LW + a + HD]
        queries = qkv[:, a : a + HD] * jnp.asarray(SCALE, BF)
        logits = nt(
            jnp.concatenate([keys, ones, mask, rest], axis=1),
            jnp.concatenate(
                [queries] + in_three(-logs[:, h : h + 1]) + [ones[:, 0:1], rest], axis=1
            ),
        )
        probs = jnp.exp(logits)
        centred = nt(
            jnp.concatenate([vals, ones, ones[:, 0:1], rest], axis=1),
            jnp.concatenate(
                [heads_grad] + in_three(-inner) + [jnp.zeros((SEQ, 1), BF), rest], axis=1
            ),
        )
        score_grad = (probs * centred).astype(BF)
        dqkv[:, 2 * LW + a : 2 * LW + a + HD] = nn(probs.astype(BF), heads_grad).astype(BF)
        dqkv[:, LW + a : LW + a + HD] = nn(score_grad, queries).astype(BF)
        dqkv[:, a : a + HD] = (tn(score_grad, keys) * SCALE).astype(BF)
    bias[...] = jnp.broadcast_to(colsum(dqkv[...].astype(F32)), (8, 3 * LW))
    for t in range(3):
        weight_grad = tn(dqkv[:, LW * t : LW * t + LW], h1[...])
        for h in range(LH):
            g = 3 * t + h
            gm[32 * g : 32 * g + 32, :] = weight_grad[64 * h : 64 * h + 32, :]
            gp[32 * g : 32 * g + 32, :] = weight_grad[64 * h + 32 : 64 * h + 64, :]


def attend_backward(scalars, qkv, logs, o, do, keep, h1):
    return call(
        attend_backward_body,
        [((SEQ, 3 * LW), BF), ((288, D), F32), ((288, D), F32), ((8, 3 * LW), F32)],
        scalars,
        qkv,
        logs,
        o,
        do,
        keep,
        h1,
        micros=8,
        name="attend_backward",
    )


def first_back_body(sc, *refs):
    x, gain, dmid, small_two = refs[:4]
    dqkvs = refs[4:8]
    weights = refs[8:12]
    biases = refs[12:16]
    grad_in, small = refs[16:]
    gain_sum = shift_sum = jnp.zeros((1, D), F32)
    for r in range(0, SEQ, ROWS):
        at = slice(r, r + ROWS)
        grad = nn(dqkvs[0][at, :], weights[0][...])
        for k in range(1, 4):
            grad += nn(dqkvs[k][at, :], weights[k][...])
        scaled, inverse = normalize(x[at, :].astype(F32))
        total = dmid[at, :] + norm_back(grad, scaled, inverse, gain[0:1, :])
        grad_in[at, :] = total.astype(BF)
        gain_sum += colsum(grad * scaled)
        shift_sum += colsum(grad)
    rest = jnp.zeros((1, D - 3 * LW), F32)
    small[...] = jnp.concatenate(
        [gain_sum, shift_sum, small_two[0:4, :]]
        + [jnp.concatenate([biases[k][0:1, :], rest], axis=1) for k in range(4)]
        + [jnp.zeros((6, D), F32)],
        axis=0,
    )


def heads_send_body(ks, sc, *refs):
    mine, theirs = refs[0:2], refs[2:4]
    out_mine, out_theirs, send = refs[4:7]
    for p in range(16):
        parts = []
        for j, k in enumerate(ks):
            if p < 12:
                rows = slice(24 * p, 24 * p + 24)
                parts.append(mine[j][rows, :] + theirs[j][rows, :])
            else:
                rows = slice(24 * (p - 12), 24 * (p - 12) + 24)
                parts.append(out_mine[k, rows, :] + out_theirs[k, rows, :])
        send[p] = jnp.concatenate(parts, axis=0).astype(BF)


def heads_fold_body(sc, got_one, got_two, small, small_other, sums, *to_y):
    parts = []
    for got in (got_one, got_two):
        total = got[0].astype(F32)
        for q in range(1, 16):
            total += got[q].astype(F32)
        parts += [total[0:24], total[24:48]]
    common = small[0:6, :] + small_other[0:6, :]
    crossed = pltpu.roll(small_other[...], D - 32, 1)
    rest = jnp.zeros((1, D - HALF_FF), F32)
    for k in range(4):
        place = ORDER.index(k)
        lanes = slice((place % 2) * HALF_FF, (place % 2 + 1) * HALF_FF)
        hidden = jnp.concatenate([sums[place // 2, 0:1, lanes], rest], axis=1)
        heads_bias = small[6 + k : 7 + k, :] + crossed[6 + k : 7 + k, :]
        to_y[k][0:24, :] = parts[place]
        to_y[k][24:32, :] = jnp.concatenate([common, heads_bias, hidden], axis=0)


def heads_out_body(
    sc, mine, theirs, qkv_grad, out_grad, out_sum, down_sum, gains, biases, up_sum, qkv_sum, rows
):
    sums = []
    for ref, core in ((mine, sc[CORE]), (theirs, 1 - sc[CORE])):
        for p in range(16):
            for g in range(3):
                at = 24 * p + 8 * g
                row = pl.multiple_of(64 * (at // 32) + 32 * core + at % 32, 8)
                rows[pl.ds(row, 8), :] = ref[p, 8 * g : 8 * g + 8, :]
        total = ref[0, 24:32, :]
        for p in range(1, 16):
            total += ref[p, 24:32, :]
        sums.append(total)
    for t in range(3):
        qkv_grad[t] = rows[LW * t : LW * t + LW, :]
    out_grad[...] = rows[3 * LW :, :]
    own, other = sums
    gains[...] = jnp.concatenate([own[0:1], own[2:3]], axis=0)
    biases[...] = jnp.concatenate([own[1:2], own[3:4]], axis=0)
    out_sum[...] = own[4:5].reshape(D)
    down_sum[...] = own[5:6].reshape(D)
    low = (lax.broadcasted_iota(jnp.int32, (8, D), 1) % HD) < 32
    swap = sc[CORE] != 0
    hidden = (own[7:8, 0:HALF_FF], other[7:8, 0:HALF_FF])
    up_sum[...] = jnp.concatenate(
        [jnp.where(swap, hidden[1], hidden[0]), jnp.where(swap, hidden[0], hidden[1])], axis=1
    ).reshape(D)
    first = jnp.where(sc[CORE] == 0, own, other)
    second = jnp.where(sc[CORE] == 0, other, own)
    natural = jnp.where(low, first, pltpu.roll(second, 32, 1))[6:7]
    qkv_sum[...] = jnp.concatenate([natural[:, 0:LW], natural[:, 2 * LW : 3 * LW]], axis=0)


def along_y(value, step):
    return lax.ppermute(value, "y", [(i, (i + step) % 4) for i in range(4)])


def after(value, *done):
    return lax.optimization_barrier((value, *done))[0]


def other_core(value):
    return lax.ppermute(value, "c", [(0, 1), (1, 0)])


def per_device(
    tokens,
    qkv_weight,
    qkv_bias,
    out_weight,
    out_bias,
    up_weight,
    up_bias,
    down_weight,
    down_bias,
    norm_gains,
    norm_biases,
    cotangent,
    band_masks,
):
    core = lax.axis_index("c")
    here = lax.axis_index("y")
    at = jnp.concatenate(
        [
            jnp.stack([core, lax.axis_index("x"), lax.axis_index("z"), here]).astype(jnp.int32),
            band_masks.reshape(16),
        ]
    )
    four = range(4)
    mine, theirs, hidden = call(
        pack_body,
        [((400, D), BF), ((400, D), BF), ((784, D), BF)],
        jnp.zeros((1,), jnp.int32),
        jnp.swapaxes(qkv_weight, 1, 2),
        out_weight,
        qkv_bias,
        up_weight,
        down_weight,
        up_bias,
        scratch=[pltpu.VMEM((D, D), BF)],
        micros=5,
        name="pack",
    )
    heads_mine, heads_theirs = {0: mine}, {0: theirs}
    for s in (1, 3):
        heads_mine[s] = along_y(mine, s)
    relayed = [along_y(heads_mine[1][:200], 1), along_y(heads_mine[3][200:], 3)]
    shards = lax.all_gather(hidden, "y", axis=0, tiled=False)
    out_grad, keep_col = call(
        masks_body,
        [((SEQ, D), BF), ((SEQ, 1), F32)],
        at,
        cotangent,
        specs={0: OWN_ROWS},
        micros=2,
        name="masks",
    )
    out_grad_other = other_core(out_grad)

    weights, qkvs, outs_of, logs = {}, {}, {}, {}
    first_in, *rest = attend_forward(
        True, at, (tokens, norm_gains, norm_biases), heads_mine[0], heads_theirs[0], keep_col
    )
    weights[0], qkvs[0], outs_of[0], logs[0] = rest
    def forward(s, *done):
        weights[s], qkvs[s], outs_of[s], logs[s] = attend_forward(
            False, at, (after(first_in, *done),), heads_mine[s], heads_theirs[s], keep_col
        )

    for s in (1, 3):
        heads_theirs[s] = other_core(after(heads_mine[s], qkvs[0]))
    forward(1, qkvs[0])
    forward(3, qkvs[1])
    heads_mine[2] = jnp.concatenate(after(relayed, qkvs[1]), axis=0)
    heads_theirs[2] = other_core(heads_mine[2])
    forward(2, qkvs[3])
    middle, second_in = call(
        middle_body,
        [((SEQ, D), F32), ((SEQ, D), BF)],
        at,
        tokens,
        out_bias[None],
        norm_gains,
        norm_biases,
        *[outs_of[k] for k in four],
        *[weights[k] for k in four],
        specs={0: OWN_ROWS} | {8 + k: OUT_ROWS for k in four},
        micros=4,
        name="middle",
    )
    second_other = other_core(second_in)
    hidden_grads, down_own, down_other, back_own, back_other, up_sums = feed(
        at, second_in, second_other, out_grad, out_grad_other, shards
    )
    back_received = other_core(back_other)
    hidden_pieces = lax.psum_scatter(
        hidden_grads.reshape(16, 4 * 48, D), ("x", "z"), scatter_dimension=0, tiled=False
    ).reshape(4, 48, D)
    down_received = other_core(down_other)

    middle_grad, out_gm, out_gp, small_two, *outs_grad = call(
        middle_back_body,
        [((SEQ, D), F32), ((4, 96, D), F32), ((4, 96, D), F32), ((8, D), F32)]
        + [((SEQ, LW), BF)] * 4,
        at,
        back_own,
        back_received,
        middle,
        norm_gains,
        out_grad,
        *[outs_of[k] for k in four],
        *[weights[k] for k in four],
        specs={9 + k: OUT_ROWS for k in four},
        scratch=[pltpu.VMEM((SEQ, D), BF)],
        micros=7,
        name="middle_back",
    )
    out_received = other_core(out_gp)
    (result_copies,) = call(
        result_body,
        [((4, SEQ, D), BF)],
        at,
        middle,
        down_own,
        down_received,
        down_bias[None],
        keep_col,
        micros=2,
        name="result_rows",
    )
    result = lax.all_to_all(result_copies, "y", 0, 0, tiled=True).reshape(4 * SEQ, D)
    dqkvs, gms, gps, bias_sums = {}, {}, {}, {}

    def backward(s, *done):
        heads_grad = after(outs_grad[s], *done)
        dqkvs[s], gms[s], gp, bias_sums[s] = attend_backward(
            at, qkvs[s], logs[s], outs_of[s], heads_grad, keep_col, first_in
        )
        gps[s] = other_core(gp)

    def heads_send(ks, *done):
        (send,) = call(
            functools.partial(heads_send_body, ks),
            [((16, 48, D), BF)],
            at,
            *[gms[k] for k in ks],
            *[gps[k] for k in ks],
            after(out_gm, *done),
            out_received,
            micros=4,
            name="heads_send",
        )
        return send

    backward(0, result_copies)
    backward(1, dqkvs[0])
    backward(3, dqkvs[1], gps[0])
    send_one = heads_send(ORDER[0:2], dqkvs[3])
    heads_one = lax.all_to_all(after(send_one, result), ("x", "z"), 0, 0, tiled=True)
    backward(2, dqkvs[3], send_one)
    send_two = heads_send(ORDER[2:4], dqkvs[2])
    heads_two = lax.all_to_all(after(send_two, heads_one), ("x", "z"), 0, 0, tiled=True)
    grad_own, small = call(
        first_back_body,
        [((SEQ, D), BF), ((16, D), F32)],
        at,
        tokens,
        norm_gains,
        after(middle_grad, send_two, heads_one),
        small_two,
        *[dqkvs[k] for k in four],
        *[weights[k] for k in four],
        *[bias_sums[k] for k in four],
        specs={0: OWN_ROWS} | {8 + k: QKV_ROWS for k in four},
        micros=8,
        name="first_back",
    )
    hidden_pieces = after(hidden_pieces, small)
    (hidden_copies,) = call(
        spread_body,
        [((16, 48, D), BF)],
        at,
        hidden_pieces[0],
        *[along_y(hidden_pieces[s], -s) for s in (1, 2, 3)],
        micros=2,
        name="hidden_spread",
    )
    input_grad = lax.all_gather(grad_own, "y", axis=0, tiled=True).astype(F32)
    to_y = call(
        heads_fold_body,
        [((32, D), F32)] * 4,
        at,
        heads_one,
        heads_two,
        small,
        other_core(small),
        up_sums,
        micros=3,
        name="heads_fold",
    )
    hidden_half = lax.all_to_all(after(hidden_copies, to_y[0]), ("x", "z"), 0, 0, tiled=True)
    (heads_copies,) = call(
        spread_body,
        [((16, 32, D), F32)],
        at,
        to_y[0],
        *[along_y(to_y[s], -s) for s in (1, 2, 3)],
        micros=2,
        name="heads_spread",
    )
    heads_half = lax.all_to_all(heads_copies, ("x", "z"), 0, 0, tiled=True)
    up_weight_grad, down_weight_grad = call(
        hidden_out_body,
        [((D, D), F32), ((D, D), F32)],
        at,
        hidden_half,
        other_core(hidden_half),
        micros=4,
        name="hidden_out",
    )
    heads_half_sent, input_grad, up_weight_grad, down_weight_grad = lax.optimization_barrier(
        (heads_half, input_grad, up_weight_grad, down_weight_grad)
    )
    heads_half_other = other_core(heads_half_sent)
    qkv_grad, out_weight_grad, out_sum, down_sum, gains, biases, up_sum, qkv_sum = call(
        heads_out_body,
        [
            ((3, LW, D), F32),
            ((LW, D), F32),
            ((D,), F32),
            ((D,), F32),
            ((2, D), F32),
            ((2, D), F32),
            ((D,), F32),
            ((2, LW), F32),
        ],
        at,
        heads_half,
        heads_half_other,
        scratch=[pltpu.VMEM((D, D), F32)],
        micros=4,
        name="heads_out",
    )
    return (
        result,
        input_grad,
        jnp.swapaxes(qkv_grad, 1, 2),
        qkv_sum,
        out_weight_grad,
        out_sum,
        up_weight_grad,
        up_sum,
        down_weight_grad,
        down_sum,
        gains,
        biases,
    )


def solution(mesh):
    inner = Mesh(np.array(mesh.devices).reshape(4, 4, 2, 4), ("x", "z", "c", "y"))
    dp = ("x", "z", "c")
    in_specs = (
        P(dp, None),
        P(None, None, "y"),
        P(None, "y"),
        P("y", None),
        P(),
        P(None, "y"),
        P("y"),
        P("y", None),
        P(),
        P(),
        P(),
        P(dp, None),
        P(dp, None),
    )
    out_specs = (
        P(dp, None),
        P(dp, None),
        P(None, None, "y"),
        P(None, "y"),
        P("y", None),
        P(),
        P(None, "y"),
        P("y"),
        P("y", None),
        P(),
        P(),
        P(),
    )
    return jax.shard_map(
        per_device, mesh=inner, in_specs=in_specs, out_specs=out_specs, check_vma=False
    )
```

```python
import functools

import jax
import jax.numpy as jnp
import numpy as np
from jax import lax
from jax.experimental import pallas as pl
from jax.experimental.pallas import tpu as pltpu
from jax.sharding import Mesh, PartitionSpec as P

BF = jnp.bfloat16
F32 = jnp.float32
SEQ = 576
SPATIAL = 144
D = 768
HD = 64
LH = 3
LW = 192
HALF_FF = 384
ROWS = 576
VMEM = 56 * 2**20
NEG = -1e30
PER_MICRO = 1e6
SCALE = HD**-0.5
ORDER = (0, 1, 3, 2)


def nt(a, b):
    return lax.dot_general(a, b, (((1,), (1,)), ((), ())), preferred_element_type=F32)


def nn(a, b):
    return lax.dot_general(a, b, (((1,), (0,)), ((), ())), preferred_element_type=F32)


def tn(a, b):
    return lax.dot_general(a, b, (((0,), (0,)), ((), ())), preferred_element_type=F32)


def normalize(value):
    centred = value - jnp.mean(value, axis=-1, keepdims=True)
    inverse = lax.rsqrt(jnp.mean(centred * centred, axis=-1, keepdims=True) + 1e-05)
    return centred * inverse, inverse


def norm_back(grad_out, scaled, inverse, gain):
    scaled_grad = grad_out * gain
    centre = jnp.mean(scaled_grad, axis=-1, keepdims=True)
    along = jnp.mean(scaled_grad * scaled, axis=-1, keepdims=True)
    return inverse * (scaled_grad - centre - scaled * along)


def colsum(value):
    return jnp.sum(value, axis=0, keepdims=True)


def call(body, outs, scalars, *args, scratch=(), specs=None, micros=1.0, name=None):
    shapes = [jax.ShapeDtypeStruct(s, d) for s, d in outs]
    moved = sum(int(np.prod(a.shape)) * a.dtype.itemsize for a in list(args) + shapes)
    return pl.pallas_call(
        body,
        grid_spec=pltpu.PrefetchScalarGridSpec(
            num_scalar_prefetch=1,
            grid=(1,),
            in_specs=[
                (specs or {}).get(i, pl.BlockSpec(memory_space=pltpu.VMEM))
                for i in range(len(args))
            ],
            out_specs=[pl.BlockSpec(memory_space=pltpu.VMEM) for _ in shapes],
            scratch_shapes=list(scratch),
        ),
        out_shape=shapes,
        compiler_params=pltpu.CompilerParams(vmem_limit_bytes=VMEM),
        cost_estimate=pl.CostEstimate(
            flops=int(micros * PER_MICRO), bytes_accessed=moved // 1024, transcendentals=0
        ),
        name=name,
    )(scalars, *args)


OWN_ROWS = pl.BlockSpec((SEQ, D), lambda i, at: (at[3], 0))
OUT_ROWS = pl.BlockSpec((LW, D), lambda i, at: (3, 0))
QKV_ROWS = pl.BlockSpec((3 * LW, D), lambda i, at: (0, 0))
CORE, X_AT, Z_AT, Y_AT, MASKS = 0, 1, 2, 3, 4


def pack_body(
    at,
    qkv_weight,
    out_weight,
    qkv_bias,
    up_weight,
    down_weight,
    up_bias,
    mine,
    theirs,
    hidden,
    rows,
):
    core = lax.axis_index("c")
    for t in range(3):
        rows[LW * t : LW * t + LW, :] = qkv_weight[t]
    rows[3 * LW :, :] = out_weight[...]
    lane = lax.broadcasted_iota(jnp.int32, (8, D), 1)
    low = (lane % HD) < 32
    given = qkv_bias[...].astype(F32)
    none = jnp.zeros((1, LW), F32)
    bias = jnp.concatenate([given[0:1], none, given[1:2], none], axis=1)
    bias = jnp.broadcast_to(bias, (8, D))
    parts = (
        jnp.where(low, bias, 0.0),
        jnp.where(low, pltpu.roll(bias, D - 32, 1), 0.0),
    )

    def fill(ref, half):
        for g in range(12):
            ref[32 * g : 32 * g + 32, :] = rows[64 * g + 32 * half : 64 * g + 32 * half + 32, :]
        part = parts[half]
        shifted = pltpu.roll(part, 32, 1)
        ref[384:400, :] = jnp.concatenate(
            [part[0:1], shifted[0:1], jnp.zeros((14, D), F32)], axis=0
        ).astype(BF)

    @pl.when(core == 0)
    def _():
        fill(mine, 0)
        fill(theirs, 1)

    @pl.when(core != 0)
    def _():
        fill(mine, 1)
        fill(theirs, 0)

    start = pl.multiple_of(core * HALF_FF, HALF_FF)
    hidden[0:HALF_FF, :] = up_weight[:, pl.ds(start, HALF_FF)].T
    hidden[HALF_FF : 2 * HALF_FF, :] = down_weight[pl.ds(start, HALF_FF), :]
    up_row = up_bias[...].astype(F32).reshape(1, D)
    up_part = jnp.where(core == 0, up_row[:, 0:HALF_FF], up_row[:, HALF_FF:])
    hidden[2 * HALF_FF : 2 * HALF_FF + 16, :] = jnp.concatenate(
        [
            jnp.concatenate([up_part, jnp.zeros((1, D - HALF_FF), F32)], axis=1),
            jnp.zeros((15, D), F32),
        ],
        axis=0,
    ).astype(BF)


def masks_body(at, cot, dy, keep_col):
    kept = [at[MASKS + 4 * at[Y_AT] + g].astype(F32) for g in range(4)]
    for g in range(4):
        rows = slice(g * SPATIAL, (g + 1) * SPATIAL)
        dy[rows, :] = (cot[rows, :].astype(F32) * kept[g]).astype(BF)
        keep_col[rows, :] = jnp.full((SPATIAL, 1), kept[g])


def attend_forward_body(first, at, *refs):
    if first:
        x, gain, shift, wm, wp, keep, h1, w, qkv, o, logs = refs
        for r in range(0, SEQ, 96):
            scaled, _ = normalize(x[r : r + 96, :].astype(F32))
            h1[r : r + 96, :] = (scaled * gain[0:1, :] + shift[0:1, :]).astype(BF)
    else:
        h1, wm, wp, keep, w, qkv, o, logs = refs
    for g in range(12):
        w[64 * g : 64 * g + 32, :] = wm[32 * g : 32 * g + 32, :]
        w[64 * g + 32 : 64 * g + 64, :] = wp[32 * g : 32 * g + 32, :]
    bias = (wm[384:385, :] + wp[385:386, :])[:, : 3 * LW].astype(F32)
    for r in range(0, SEQ, ROWS):
        qkv[r : r + ROWS, :] = (nt(h1[r : r + ROWS, :], w[0 : 3 * LW, :]) + bias).astype(BF)
    mask = ((1.0 - keep[...]) * NEG).astype(BF)
    ones = jnp.ones((SEQ, 1), BF)
    rest = jnp.zeros((SEQ, HD - 1), BF)
    for h in range(LH):
        a = HD * h
        keys = jnp.concatenate([qkv[:, LW + a : LW + a + HD], mask, rest], axis=1)
        queries = jnp.concatenate(
            [qkv[:, a : a + HD] * jnp.asarray(SCALE, BF), ones, rest], axis=1
        )
        scores = nt(queries, keys)
        peak = jnp.max(scores, axis=-1, keepdims=True)
        expos = jnp.exp(scores - peak)
        total = jnp.sum(expos, axis=-1, keepdims=True)
        probs = (expos * (1.0 / total)).astype(BF)
        o[:, a : a + HD] = nn(probs, qkv[:, 2 * LW + a : 2 * LW + a + HD]).astype(BF)
        logs[:, h : h + 1] = peak + jnp.log(total)


def attend_forward(first, scalars, lead, wm, wp, keep):
    outs = [((D, D), BF), ((SEQ, 3 * LW), BF), ((SEQ, LW), BF), ((SEQ, 128), F32)]
    if first:
        outs = [((SEQ, D), BF)] + outs
    return call(
        functools.partial(attend_forward_body, first),
        outs,
        scalars,
        *lead,
        wm,
        wp,
        keep,
        specs={0: OWN_ROWS} if first else None,
        micros=8,
        name="attend_forward",
    )


def middle_body(at, *refs):
    x, bias, gain, shift = refs[:4]
    outs_of = refs[4:8]
    weights = refs[8:12]
    mid, h2 = refs[12:]
    for r in range(0, SEQ, ROWS):
        total = x[r : r + ROWS, :].astype(F32) + bias[...].astype(F32)
        for k in range(4):
            total = total + nn(outs_of[k][r : r + ROWS, :], weights[k][...])
        mid[r : r + ROWS, :] = total
        scaled, _ = normalize(total)
        h2[r : r + ROWS, :] = (scaled * gain[1:2, :] + shift[1:2, :]).astype(BF)


def feed_body(at, h2o, h2p, dyo, dyp, shards, grads, mo, mp, dho, dhp, ubias, *scratch):
    h2, dy, wu, wd, act, dhid, accm, acch = scratch
    owners = [lax.rem(at[Y_AT] + 4 - k, 4) for k in range(4)]
    h2[0:SEQ, :] = h2o[...]
    h2[SEQ:, :] = h2p[...]
    dy[0:SEQ, :] = dyo[...]
    dy[SEQ:, :] = dyp[...]
    block = 2 * SEQ
    for pair in range(2):
        one, two = (shards.at[owners[ORDER[2 * pair + s]]] for s in range(2))
        wu[0:HALF_FF, :] = one[0:HALF_FF, :]
        wu[HALF_FF:, :] = two[0:HALF_FF, :]
        wd[0:HALF_FF, :] = one[HALF_FF : 2 * HALF_FF, :]
        wd[HALF_FF:, :] = two[HALF_FF : 2 * HALF_FF, :]
        bias = jnp.concatenate(
            [one[768:784, 0:HALF_FF][0:1], two[768:784, 0:HALF_FF][0:1]], axis=1
        ).astype(F32)
        ubias[pair] = jnp.zeros((8, D), F32)

        @pl.loop(0, 2 * SEQ // block)
        def _(i):
            rows = pl.ds(pl.multiple_of(i * block, block), block)
            hid = nt(h2[rows, :], wu[...]) + bias
            cdf = 0.5 + 0.5 * lax.erf(hid * np.float32(0.7071067811865476))
            active = (hid * cdf).astype(BF)
            slope = cdf + hid * (
                jnp.exp(hid * hid * np.float32(-0.5)) * np.float32(0.3989422804014327)
            )
            act[rows, :] = active
            hid_grad = (nt(dy[rows, :], wd[...]) * slope).astype(BF)
            dhid[rows, :] = hid_grad
            ubias[pair, 0:1, :] += colsum(hid_grad.astype(F32))
            down = nn(active, wd[...])
            back = nn(hid_grad, wu[...])
            if pair == 0:
                accm[rows, :] = down
                acch[rows, :] = back
            else:
                accm[rows, :] += down
                acch[rows, :] += back

        for s in range(2):
            k = ORDER[2 * pair + s]
            cols = slice(s * HALF_FF, (s + 1) * HALF_FF)
            up_grad = tn(dhid[:, cols], h2[...])
            down_grad = tn(act[:, cols], dy[...])
            for q in range(8):
                rows = slice(48 * q, 48 * q + 48)
                grads[q, k] = up_grad[rows, :]
                grads[8 + q, k] = down_grad[rows, :]
    mo[...] = accm[0:SEQ, :]
    mp[...] = accm[SEQ:, :]
    dho[...] = acch[0:SEQ, :]
    dhp[...] = acch[SEQ:, :].astype(BF)


def feed(scalars, h2o, h2p, dyo, dyp, shards):
    big = (2 * SEQ, D)
    return call(
        feed_body,
        [
            ((16, 4, 48, D), F32),
            ((SEQ, D), F32),
            ((SEQ, D), F32),
            ((SEQ, D), F32),
            ((SEQ, D), BF),
            ((2, 8, D), F32),
        ],
        scalars,
        h2o,
        h2p,
        dyo,
        dyp,
        shards,
        scratch=[
            pltpu.VMEM(big, BF),
            pltpu.VMEM(big, BF),
            pltpu.VMEM((D, D), BF),
            pltpu.VMEM((D, D), BF),
            pltpu.VMEM(big, BF),
            pltpu.VMEM(big, BF),
            pltpu.VMEM(big, F32),
            pltpu.VMEM(big, F32),
        ],
        micros=30,
        name="feed",
    )


def result_body(at, middle, down, other, bias, keep, out):
    total = middle[...] + (down[...] + other[...] + bias[...].astype(F32))
    low = (keep[...] * total).astype(BF)
    for q in range(4):
        out[q] = low


def spread_body(at, a, b, c, d, out):
    total = ((a[...] + b[...]) + (c[...] + d[...])).astype(out.dtype)
    for q in range(16):
        out[q] = total


def hidden_out_body(at, mine, theirs, up, down):
    for ref, core in ((mine, at[CORE]), (theirs, 1 - at[CORE])):
        start = pl.multiple_of(core * HALF_FF, HALF_FF)
        half = jnp.concatenate([ref[q] for q in range(8)], axis=0).astype(F32)
        up[:, pl.ds(start, HALF_FF)] = half.T
        for q in range(8):
            row = pl.multiple_of(start + 48 * q, 16)
            down[pl.ds(row, 48), :] = ref[8 + q].astype(F32)


def middle_back_body(at, *refs):
    dho, dhp, mid, gain, dy = refs[:5]
    outs_of = refs[5:9]
    weights = refs[9:13]
    dmid, gm, gp, small = refs[13:17]
    outs_grad = refs[17:21]
    da = refs[21]
    gain_sum = shift_sum = bias_sum = down_sum = jnp.zeros((1, D), F32)
    for r in range(0, SEQ, ROWS):
        at = slice(r, r + ROWS)
        grad = dho[at, :] + dhp[at, :].astype(F32)
        scaled, inverse = normalize(mid[at, :])
        out_grad = dy[at, :].astype(F32)
        total = out_grad + norm_back(grad, scaled, inverse, gain[1:2, :])
        dmid[at, :] = total
        low = total.astype(BF)
        da[at, :] = low
        gain_sum += colsum(grad * scaled)
        shift_sum += colsum(grad)
        bias_sum += colsum(low.astype(F32))
        down_sum += colsum(out_grad)
        for k in range(4):
            outs_grad[k][at, :] = nt(low, weights[k][...]).astype(BF)
    for k in range(4):
        weight_grad = tn(outs_of[k][...], da[...])
        for h in range(LH):
            gm[k, 32 * h : 32 * h + 32, :] = weight_grad[64 * h : 64 * h + 32, :]
            gp[k, 32 * h : 32 * h + 32, :] = weight_grad[64 * h + 32 : 64 * h + 64, :]
    small[...] = jnp.concatenate(
        [gain_sum, shift_sum, bias_sum, down_sum, jnp.zeros((4, D), F32)], axis=0
    )


def in_three(value):
    one = value.astype(BF)
    left = value - one.astype(F32)
    two = left.astype(BF)
    return [one, two, (left - two.astype(F32)).astype(BF)]


def attend_backward_body(sc, qkv, logs, o, do, keep, h1, dqkv, gm, gp, bias):
    mask = ((1.0 - keep[...]) * NEG).astype(BF)
    ones = jnp.ones((SEQ, 3), BF)
    rest = jnp.zeros((SEQ, HD - 4), BF)
    for h in range(LH):
        a = HD * h
        heads_grad = do[:, a : a + HD]
        inner = jnp.sum(
            heads_grad.astype(F32) * o[:, a : a + HD].astype(F32), axis=-1, keepdims=True
        )
        keys = qkv[:, LW + a : LW + a + HD]
        vals = qkv[:, 2 * LW + a : 2 * LW + a + HD]
        queries = qkv[:, a : a + HD] * jnp.asarray(SCALE, BF)
        logits = nt(
            jnp.concatenate([keys, ones, mask, rest], axis=1),
            jnp.concatenate(
                [queries] + in_three(-logs[:, h : h + 1]) + [ones[:, 0:1], rest], axis=1
            ),
        )
        probs = jnp.exp(logits)
        centred = nt(
            jnp.concatenate([vals, ones, ones[:, 0:1], rest], axis=1),
            jnp.concatenate(
                [heads_grad] + in_three(-inner) + [jnp.zeros((SEQ, 1), BF), rest], axis=1
            ),
        )
        score_grad = (probs * centred).astype(BF)
        dqkv[:, 2 * LW + a : 2 * LW + a + HD] = nn(probs.astype(BF), heads_grad).astype(BF)
        dqkv[:, LW + a : LW + a + HD] = nn(score_grad, queries).astype(BF)
        dqkv[:, a : a + HD] = (tn(score_grad, keys) * SCALE).astype(BF)
    bias[...] = jnp.broadcast_to(colsum(dqkv[...].astype(F32)), (8, 3 * LW))
    for t in range(3):
        weight_grad = tn(dqkv[:, LW * t : LW * t + LW], h1[...])
        for h in range(LH):
            g = 3 * t + h
            gm[32 * g : 32 * g + 32, :] = weight_grad[64 * h : 64 * h + 32, :]
            gp[32 * g : 32 * g + 32, :] = weight_grad[64 * h + 32 : 64 * h + 64, :]


def attend_backward(scalars, qkv, logs, o, do, keep, h1):
    return call(
        attend_backward_body,
        [((SEQ, 3 * LW), BF), ((288, D), F32), ((288, D), F32), ((8, 3 * LW), F32)],
        scalars,
        qkv,
        logs,
        o,
        do,
        keep,
        h1,
        micros=8,
        name="attend_backward",
    )


def first_back_body(sc, *refs):
    x, gain, dmid, small_two = refs[:4]
    dqkvs = refs[4:8]
    weights = refs[8:12]
    biases = refs[12:16]
    grad_in, small = refs[16:]
    gain_sum = shift_sum = jnp.zeros((1, D), F32)
    for r in range(0, SEQ, ROWS):
        at = slice(r, r + ROWS)
        grad = nn(dqkvs[0][at, :], weights[0][...])
        for k in range(1, 4):
            grad += nn(dqkvs[k][at, :], weights[k][...])
        scaled, inverse = normalize(x[at, :].astype(F32))
        total = dmid[at, :] + norm_back(grad, scaled, inverse, gain[0:1, :])
        grad_in[at, :] = total.astype(BF)
        gain_sum += colsum(grad * scaled)
        shift_sum += colsum(grad)
    rest = jnp.zeros((1, D - 3 * LW), F32)
    small[...] = jnp.concatenate(
        [gain_sum, shift_sum, small_two[0:4, :]]
        + [jnp.concatenate([biases[k][0:1, :], rest], axis=1) for k in range(4)]
        + [jnp.zeros((6, D), F32)],
        axis=0,
    )


def heads_send_body(ks, sc, *refs):
    mine, theirs = refs[0:2], refs[2:4]
    out_mine, out_theirs, send = refs[4:7]
    for p in range(16):
        parts = []
        for j, k in enumerate(ks):
            if p < 12:
                rows = slice(24 * p, 24 * p + 24)
                parts.append(mine[j][rows, :] + theirs[j][rows, :])
            else:
                rows = slice(24 * (p - 12), 24 * (p - 12) + 24)
                parts.append(out_mine[k, rows, :] + out_theirs[k, rows, :])
        send[p] = jnp.concatenate(parts, axis=0).astype(BF)


def heads_fold_body(sc, got_one, got_two, small, small_other, sums, *to_y):
    parts = []
    for got in (got_one, got_two):
        total = got[0].astype(F32)
        for q in range(1, 16):
            total += got[q].astype(F32)
        parts += [total[0:24], total[24:48]]
    common = small[0:6, :] + small_other[0:6, :]
    crossed = pltpu.roll(small_other[...], D - 32, 1)
    rest = jnp.zeros((1, D - HALF_FF), F32)
    for k in range(4):
        place = ORDER.index(k)
        lanes = slice((place % 2) * HALF_FF, (place % 2 + 1) * HALF_FF)
        hidden = jnp.concatenate([sums[place // 2, 0:1, lanes], rest], axis=1)
        heads_bias = small[6 + k : 7 + k, :] + crossed[6 + k : 7 + k, :]
        to_y[k][0:24, :] = parts[place]
        to_y[k][24:32, :] = jnp.concatenate([common, heads_bias, hidden], axis=0)


def heads_out_body(
    sc, mine, theirs, qkv_grad, out_grad, out_sum, down_sum, gains, biases, up_sum, qkv_sum, rows
):
    sums = []
    for ref, core in ((mine, sc[CORE]), (theirs, 1 - sc[CORE])):
        for p in range(16):
            for g in range(3):
                at = 24 * p + 8 * g
                row = pl.multiple_of(64 * (at // 32) + 32 * core + at % 32, 8)
                rows[pl.ds(row, 8), :] = ref[p, 8 * g : 8 * g + 8, :]
        total = ref[0, 24:32, :]
        for p in range(1, 16):
            total += ref[p, 24:32, :]
        sums.append(total)
    for t in range(3):
        qkv_grad[t] = rows[LW * t : LW * t + LW, :]
    out_grad[...] = rows[3 * LW :, :]
    own, other = sums
    gains[...] = jnp.concatenate([own[0:1], own[2:3]], axis=0)
    biases[...] = jnp.concatenate([own[1:2], own[3:4]], axis=0)
    out_sum[...] = own[4:5].reshape(D)
    down_sum[...] = own[5:6].reshape(D)
    low = (lax.broadcasted_iota(jnp.int32, (8, D), 1) % HD) < 32
    swap = sc[CORE] != 0
    hidden = (own[7:8, 0:HALF_FF], other[7:8, 0:HALF_FF])
    up_sum[...] = jnp.concatenate(
        [jnp.where(swap, hidden[1], hidden[0]), jnp.where(swap, hidden[0], hidden[1])], axis=1
    ).reshape(D)
    first = jnp.where(sc[CORE] == 0, own, other)
    second = jnp.where(sc[CORE] == 0, other, own)
    natural = jnp.where(low, first, pltpu.roll(second, 32, 1))[6:7]
    qkv_sum[...] = jnp.concatenate([natural[:, 0:LW], natural[:, 2 * LW : 3 * LW]], axis=0)


def along_y(value, step):
    return lax.ppermute(value, "y", [(i, (i + step) % 4) for i in range(4)])


def after(value, *done):
    return lax.optimization_barrier((value, *done))[0]


def other_core(value):
    return lax.ppermute(value, "c", [(0, 1), (1, 0)])


def per_device(
    tokens,
    qkv_weight,
    qkv_bias,
    out_weight,
    out_bias,
    up_weight,
    up_bias,
    down_weight,
    down_bias,
    norm_gains,
    norm_biases,
    cotangent,
    band_masks,
):
    core = lax.axis_index("c")
    here = lax.axis_index("y")
    at = jnp.concatenate(
        [
            jnp.stack([core, lax.axis_index("x"), lax.axis_index("z"), here]).astype(jnp.int32),
            band_masks.reshape(16),
        ]
    )
    four = range(4)
    mine, theirs, hidden = call(
        pack_body,
        [((400, D), BF), ((400, D), BF), ((784, D), BF)],
        jnp.zeros((1,), jnp.int32),
        jnp.swapaxes(qkv_weight, 1, 2),
        out_weight,
        qkv_bias,
        up_weight,
        down_weight,
        up_bias,
        scratch=[pltpu.VMEM((D, D), BF)],
        micros=5,
        name="pack",
    )
    heads_mine, heads_theirs = {0: mine}, {0: theirs}
    for s in (1, 3):
        heads_mine[s] = along_y(mine, s)
    relayed = [along_y(heads_mine[1][:200], 1), along_y(heads_mine[3][200:], 3)]
    shards = lax.all_gather(hidden, "y", axis=0, tiled=False)
    out_grad, keep_col = call(
        masks_body,
        [((SEQ, D), BF), ((SEQ, 1), F32)],
        at,
        cotangent,
        specs={0: OWN_ROWS},
        micros=2,
        name="masks",
    )
    out_grad_other = other_core(out_grad)

    weights, qkvs, outs_of, logs = {}, {}, {}, {}
    first_in, *rest = attend_forward(
        True, at, (tokens, norm_gains, norm_biases), heads_mine[0], heads_theirs[0], keep_col
    )
    weights[0], qkvs[0], outs_of[0], logs[0] = rest
    def forward(s, *done):
        weights[s], qkvs[s], outs_of[s], logs[s] = attend_forward(
            False, at, (after(first_in, *done),), heads_mine[s], heads_theirs[s], keep_col
        )

    for s in (1, 3):
        heads_theirs[s] = other_core(after(heads_mine[s], qkvs[0]))
    forward(1, qkvs[0])
    forward(3, qkvs[1])
    heads_mine[2] = jnp.concatenate(after(relayed, qkvs[1]), axis=0)
    heads_theirs[2] = other_core(heads_mine[2])
    forward(2, qkvs[3])
    middle, second_in = call(
        middle_body,
        [((SEQ, D), F32), ((SEQ, D), BF)],
        at,
        tokens,
        out_bias[None],
        norm_gains,
        norm_biases,
        *[outs_of[k] for k in four],
        *[weights[k] for k in four],
        specs={0: OWN_ROWS} | {8 + k: OUT_ROWS for k in four},
        micros=4,
        name="middle",
    )
    second_other = other_core(second_in)
    hidden_grads, down_own, down_other, back_own, back_other, up_sums = feed(
        at, second_in, second_other, out_grad, out_grad_other, shards
    )
    back_received = other_core(back_other)
    hidden_pieces = lax.psum_scatter(
        hidden_grads.reshape(16, 4 * 48, D), ("x", "z"), scatter_dimension=0, tiled=False
    ).reshape(4, 48, D)
    down_received = other_core(down_other)

    middle_grad, out_gm, out_gp, small_two, *outs_grad = call(
        middle_back_body,
        [((SEQ, D), F32), ((4, 96, D), F32), ((4, 96, D), F32), ((8, D), F32)]
        + [((SEQ, LW), BF)] * 4,
        at,
        back_own,
        back_received,
        middle,
        norm_gains,
        out_grad,
        *[outs_of[k] for k in four],
        *[weights[k] for k in four],
        specs={9 + k: OUT_ROWS for k in four},
        scratch=[pltpu.VMEM((SEQ, D), BF)],
        micros=7,
        name="middle_back",
    )
    out_received = other_core(out_gp)
    (result_copies,) = call(
        result_body,
        [((4, SEQ, D), BF)],
        at,
        middle,
        down_own,
        down_received,
        down_bias[None],
        keep_col,
        micros=2,
        name="result_rows",
    )
    result = lax.all_to_all(result_copies, "y", 0, 0, tiled=True).reshape(4 * SEQ, D)
    dqkvs, gms, gps, bias_sums = {}, {}, {}, {}

    def backward(s, *done):
        heads_grad = after(outs_grad[s], *done)
        dqkvs[s], gms[s], gp, bias_sums[s] = attend_backward(
            at, qkvs[s], logs[s], outs_of[s], heads_grad, keep_col, first_in
        )
        gps[s] = other_core(gp)

    def heads_send(ks, *done):
        (send,) = call(
            functools.partial(heads_send_body, ks),
            [((16, 48, D), BF)],
            at,
            *[gms[k] for k in ks],
            *[gps[k] for k in ks],
            after(out_gm, *done),
            out_received,
            micros=4,
            name="heads_send",
        )
        return send

    backward(0, result_copies)
    backward(1, dqkvs[0])
    backward(3, dqkvs[1], gps[0])
    backward(2, dqkvs[3])
    send_one = heads_send(ORDER[0:2], dqkvs[2])
    send_one, result = lax.optimization_barrier((send_one, result))
    heads_one = lax.all_to_all(send_one, ("x", "z"), 0, 0, tiled=True)
    send_two = heads_send(ORDER[2:4], send_one)
    heads_two = lax.all_to_all(after(send_two, heads_one), ("x", "z"), 0, 0, tiled=True)
    grad_own, small = call(
        first_back_body,
        [((SEQ, D), BF), ((16, D), F32)],
        at,
        tokens,
        norm_gains,
        after(middle_grad, send_two),
        small_two,
        *[dqkvs[k] for k in four],
        *[weights[k] for k in four],
        *[bias_sums[k] for k in four],
        specs={0: OWN_ROWS} | {8 + k: QKV_ROWS for k in four},
        micros=8,
        name="first_back",
    )
    hidden_pieces = after(hidden_pieces, small)
    (hidden_copies,) = call(
        spread_body,
        [((16, 48, D), BF)],
        at,
        hidden_pieces[0],
        *[along_y(hidden_pieces[s], -s) for s in (1, 2, 3)],
        micros=2,
        name="hidden_spread",
    )
    input_grad = lax.all_gather(grad_own, "y", axis=0, tiled=True).astype(F32)
    to_y = call(
        heads_fold_body,
        [((32, D), F32)] * 4,
        at,
        heads_one,
        heads_two,
        small,
        other_core(small),
        up_sums,
        micros=3,
        name="heads_fold",
    )
    hidden_half = lax.all_to_all(after(hidden_copies, to_y[0]), ("x", "z"), 0, 0, tiled=True)
    (heads_copies,) = call(
        spread_body,
        [((16, 32, D), F32)],
        at,
        to_y[0],
        *[along_y(to_y[s], -s) for s in (1, 2, 3)],
        micros=2,
        name="heads_spread",
    )
    heads_half = lax.all_to_all(heads_copies, ("x", "z"), 0, 0, tiled=True)
    up_weight_grad, down_weight_grad = call(
        hidden_out_body,
        [((D, D), F32), ((D, D), F32)],
        at,
        hidden_half,
        other_core(hidden_half),
        micros=4,
        name="hidden_out",
    )
    heads_half_sent, input_grad, up_weight_grad, down_weight_grad = lax.optimization_barrier(
        (heads_half, input_grad, up_weight_grad, down_weight_grad)
    )
    heads_half_other = other_core(heads_half_sent)
    qkv_grad, out_weight_grad, out_sum, down_sum, gains, biases, up_sum, qkv_sum = call(
        heads_out_body,
        [
            ((3, LW, D), F32),
            ((LW, D), F32),
            ((D,), F32),
            ((D,), F32),
            ((2, D), F32),
            ((2, D), F32),
            ((D,), F32),
            ((2, LW), F32),
        ],
        at,
        heads_half,
        heads_half_other,
        scratch=[pltpu.VMEM((D, D), F32)],
        micros=4,
        name="heads_out",
    )
    return (
        result,
        input_grad,
        jnp.swapaxes(qkv_grad, 1, 2),
        qkv_sum,
        out_weight_grad,
        out_sum,
        up_weight_grad,
        up_sum,
        down_weight_grad,
        down_sum,
        gains,
        biases,
    )


def solution(mesh):
    inner = Mesh(np.array(mesh.devices).reshape(4, 4, 2, 4), ("x", "z", "c", "y"))
    dp = ("x", "z", "c")
    in_specs = (
        P(dp, None),
        P(None, None, "y"),
        P(None, "y"),
        P("y", None),
        P(),
        P(None, "y"),
        P("y"),
        P("y", None),
        P(),
        P(),
        P(),
        P(dp, None),
        P(dp, None),
    )
    out_specs = (
        P(dp, None),
        P(dp, None),
        P(None, None, "y"),
        P(None, "y"),
        P("y", None),
        P(),
        P(None, "y"),
        P("y"),
        P("y", None),
        P(),
        P(),
        P(),
    )
    return jax.shard_map(
        per_device, mesh=inner, in_specs=in_specs, out_specs=out_specs, check_vma=False
    )
```

```python
import functools

import jax
import jax.numpy as jnp
import numpy as np
from jax import lax
from jax.experimental import pallas as pl
from jax.experimental.pallas import tpu as pltpu
from jax.sharding import Mesh, PartitionSpec as P

BF = jnp.bfloat16
F32 = jnp.float32
SEQ = 576
SPATIAL = 144
D = 768
HD = 64
LH = 3
LW = 192
HALF_FF = 384
ROWS = 192
VMEM = 56 * 2**20
NEG = -1e30
PER_MICRO = 1e6
SCALE = HD**-0.5
ORDER = (0, 1, 3, 2)


def nt(a, b):
    return lax.dot_general(a, b, (((1,), (1,)), ((), ())), preferred_element_type=F32)


def nn(a, b):
    return lax.dot_general(a, b, (((1,), (0,)), ((), ())), preferred_element_type=F32)


def tn(a, b):
    return lax.dot_general(a, b, (((0,), (0,)), ((), ())), preferred_element_type=F32)


def normalize(value):
    centred = value - jnp.mean(value, axis=-1, keepdims=True)
    inverse = lax.rsqrt(jnp.mean(centred * centred, axis=-1, keepdims=True) + 1e-05)
    return centred * inverse, inverse


def norm_back(grad_out, scaled, inverse, gain):
    scaled_grad = grad_out * gain
    centre = jnp.mean(scaled_grad, axis=-1, keepdims=True)
    along = jnp.mean(scaled_grad * scaled, axis=-1, keepdims=True)
    return inverse * (scaled_grad - centre - scaled * along)


def colsum(value):
    return jnp.sum(value, axis=0, keepdims=True)


def call(body, outs, scalars, *args, scratch=(), specs=None, micros=1.0, name=None):
    shapes = [jax.ShapeDtypeStruct(s, d) for s, d in outs]
    moved = sum(int(np.prod(a.shape)) * a.dtype.itemsize for a in list(args) + shapes)
    return pl.pallas_call(
        body,
        grid_spec=pltpu.PrefetchScalarGridSpec(
            num_scalar_prefetch=1,
            grid=(1,),
            in_specs=[
                (specs or {}).get(i, pl.BlockSpec(memory_space=pltpu.VMEM))
                for i in range(len(args))
            ],
            out_specs=[pl.BlockSpec(memory_space=pltpu.VMEM) for _ in shapes],
            scratch_shapes=list(scratch),
        ),
        out_shape=shapes,
        compiler_params=pltpu.CompilerParams(vmem_limit_bytes=VMEM),
        cost_estimate=pl.CostEstimate(
            flops=int(micros * PER_MICRO), bytes_accessed=moved // 1024, transcendentals=0
        ),
        name=name,
    )(scalars, *args)


OWN_ROWS = pl.BlockSpec((SEQ, D), lambda i, at: (at[3], 0))
OUT_ROWS = pl.BlockSpec((LW, D), lambda i, at: (3, 0))
QKV_ROWS = pl.BlockSpec((3 * LW, D), lambda i, at: (0, 0))
CORE, X_AT, Z_AT, Y_AT, MASKS = 0, 1, 2, 3, 4


def pack_body(
    at,
    qkv_weight,
    out_weight,
    qkv_bias,
    up_weight,
    down_weight,
    up_bias,
    mine,
    theirs,
    hidden,
    rows,
):
    core = lax.axis_index("c")
    for t in range(3):
        rows[LW * t : LW * t + LW, :] = qkv_weight[t]
    rows[3 * LW :, :] = out_weight[...]
    lane = lax.broadcasted_iota(jnp.int32, (8, D), 1)
    low = (lane % HD) < 32
    given = qkv_bias[...].astype(F32)
    none = jnp.zeros((1, LW), F32)
    bias = jnp.concatenate([given[0:1], none, given[1:2], none], axis=1)
    bias = jnp.broadcast_to(bias, (8, D))
    parts = (
        jnp.where(low, bias, 0.0),
        jnp.where(low, pltpu.roll(bias, D - 32, 1), 0.0),
    )

    def fill(ref, half):
        for g in range(12):
            ref[32 * g : 32 * g + 32, :] = rows[64 * g + 32 * half : 64 * g + 32 * half + 32, :]
        part = parts[half]
        shifted = pltpu.roll(part, 32, 1)
        ref[384:400, :] = jnp.concatenate(
            [part[0:1], shifted[0:1], jnp.zeros((14, D), F32)], axis=0
        ).astype(BF)

    @pl.when(core == 0)
    def _():
        fill(mine, 0)
        fill(theirs, 1)

    @pl.when(core != 0)
    def _():
        fill(mine, 1)
        fill(theirs, 0)

    start = pl.multiple_of(core * HALF_FF, HALF_FF)
    hidden[0:HALF_FF, :] = up_weight[:, pl.ds(start, HALF_FF)].T
    hidden[HALF_FF : 2 * HALF_FF, :] = down_weight[pl.ds(start, HALF_FF), :]
    up_row = up_bias[...].astype(F32).reshape(1, D)
    up_part = jnp.where(core == 0, up_row[:, 0:HALF_FF], up_row[:, HALF_FF:])
    hidden[2 * HALF_FF : 2 * HALF_FF + 16, :] = jnp.concatenate(
        [
            jnp.concatenate([up_part, jnp.zeros((1, D - HALF_FF), F32)], axis=1),
            jnp.zeros((15, D), F32),
        ],
        axis=0,
    ).astype(BF)


def masks_body(at, cot, dy, keep_col):
    kept = [at[MASKS + 4 * at[Y_AT] + g].astype(F32) for g in range(4)]
    for g in range(4):
        rows = slice(g * SPATIAL, (g + 1) * SPATIAL)
        dy[rows, :] = (cot[rows, :].astype(F32) * kept[g]).astype(BF)
        keep_col[rows, :] = jnp.full((SPATIAL, 1), kept[g])


def attend_forward_body(first, at, *refs):
    if first:
        x, gain, shift, wm, wp, keep, h1, w, qkv, o, logs = refs
        for r in range(0, SEQ, 96):
            scaled, _ = normalize(x[r : r + 96, :].astype(F32))
            h1[r : r + 96, :] = (scaled * gain[0:1, :] + shift[0:1, :]).astype(BF)
    else:
        h1, wm, wp, keep, w, qkv, o, logs = refs
    for g in range(12):
        w[64 * g : 64 * g + 32, :] = wm[32 * g : 32 * g + 32, :]
        w[64 * g + 32 : 64 * g + 64, :] = wp[32 * g : 32 * g + 32, :]
    bias = (wm[384:385, :] + wp[385:386, :])[:, : 3 * LW].astype(F32)
    for r in range(0, SEQ, ROWS):
        qkv[r : r + ROWS, :] = (nt(h1[r : r + ROWS, :], w[0 : 3 * LW, :]) + bias).astype(BF)
    mask = ((1.0 - keep[...]) * NEG).astype(BF)
    ones = jnp.ones((SEQ, 1), BF)
    rest = jnp.zeros((SEQ, HD - 1), BF)
    for h in range(LH):
        a = HD * h
        keys = jnp.concatenate([qkv[:, LW + a : LW + a + HD], mask, rest], axis=1)
        queries = jnp.concatenate(
            [qkv[:, a : a + HD] * jnp.asarray(SCALE, BF), ones, rest], axis=1
        )
        scores = nt(queries, keys)
        peak = jnp.max(scores, axis=-1, keepdims=True)
        expos = jnp.exp(scores - peak)
        total = jnp.sum(expos, axis=-1, keepdims=True)
        probs = (expos * (1.0 / total)).astype(BF)
        o[:, a : a + HD] = nn(probs, qkv[:, 2 * LW + a : 2 * LW + a + HD]).astype(BF)
        logs[:, h : h + 1] = peak + jnp.log(total)


def attend_forward(first, scalars, lead, wm, wp, keep):
    outs = [((D, D), BF), ((SEQ, 3 * LW), BF), ((SEQ, LW), BF), ((SEQ, 128), F32)]
    if first:
        outs = [((SEQ, D), BF)] + outs
    return call(
        functools.partial(attend_forward_body, first),
        outs,
        scalars,
        *lead,
        wm,
        wp,
        keep,
        specs={0: OWN_ROWS} if first else None,
        micros=8,
        name="attend_forward",
    )


def middle_body(at, *refs):
    x, bias, gain, shift = refs[:4]
    outs_of = refs[4:8]
    weights = refs[8:12]
    mid, h2 = refs[12:]
    for r in range(0, SEQ, ROWS):
        total = x[r : r + ROWS, :].astype(F32) + bias[...].astype(F32)
        for k in range(4):
            total = total + nn(outs_of[k][r : r + ROWS, :], weights[k][...])
        mid[r : r + ROWS, :] = total
        scaled, _ = normalize(total)
        h2[r : r + ROWS, :] = (scaled * gain[1:2, :] + shift[1:2, :]).astype(BF)


def feed_body(at, h2o, h2p, dyo, dyp, shards, grads, mo, mp, dho, dhp, ubias, *scratch):
    h2, dy, wu, wd, act, dhid, accm, acch = scratch
    owners = [lax.rem(at[Y_AT] + 4 - k, 4) for k in range(4)]
    h2[0:SEQ, :] = h2o[...]
    h2[SEQ:, :] = h2p[...]
    dy[0:SEQ, :] = dyo[...]
    dy[SEQ:, :] = dyp[...]
    block = 2 * SEQ
    for pair in range(2):
        one, two = (shards.at[owners[ORDER[2 * pair + s]]] for s in range(2))
        wu[0:HALF_FF, :] = one[0:HALF_FF, :]
        wu[HALF_FF:, :] = two[0:HALF_FF, :]
        wd[0:HALF_FF, :] = one[HALF_FF : 2 * HALF_FF, :]
        wd[HALF_FF:, :] = two[HALF_FF : 2 * HALF_FF, :]
        bias = jnp.concatenate(
            [one[768:784, 0:HALF_FF][0:1], two[768:784, 0:HALF_FF][0:1]], axis=1
        ).astype(F32)
        ubias[pair] = jnp.zeros((8, D), F32)

        @pl.loop(0, 2 * SEQ // block)
        def _(i):
            rows = pl.ds(pl.multiple_of(i * block, block), block)
            hid = nt(h2[rows, :], wu[...]) + bias
            cdf = 0.5 + 0.5 * lax.erf(hid * np.float32(0.7071067811865476))
            active = (hid * cdf).astype(BF)
            slope = cdf + hid * (
                jnp.exp(hid * hid * np.float32(-0.5)) * np.float32(0.3989422804014327)
            )
            act[rows, :] = active
            hid_grad = (nt(dy[rows, :], wd[...]) * slope).astype(BF)
            dhid[rows, :] = hid_grad
            ubias[pair, 0:1, :] += colsum(hid_grad.astype(F32))
            down = nn(active, wd[...])
            back = nn(hid_grad, wu[...])
            if pair == 0:
                accm[rows, :] = down
                acch[rows, :] = back
            else:
                accm[rows, :] += down
                acch[rows, :] += back

        for s in range(2):
            k = ORDER[2 * pair + s]
            cols = slice(s * HALF_FF, (s + 1) * HALF_FF)
            up_grad = tn(dhid[:, cols], h2[...])
            down_grad = tn(act[:, cols], dy[...])
            for q in range(8):
                rows = slice(48 * q, 48 * q + 48)
                grads[q, k] = up_grad[rows, :]
                grads[8 + q, k] = down_grad[rows, :]
    mo[...] = accm[0:SEQ, :]
    mp[...] = accm[SEQ:, :]
    dho[...] = acch[0:SEQ, :]
    dhp[...] = acch[SEQ:, :].astype(BF)


def feed(scalars, h2o, h2p, dyo, dyp, shards):
    big = (2 * SEQ, D)
    return call(
        feed_body,
        [
            ((16, 4, 48, D), F32),
            ((SEQ, D), F32),
            ((SEQ, D), F32),
            ((SEQ, D), F32),
            ((SEQ, D), BF),
            ((2, 8, D), F32),
        ],
        scalars,
        h2o,
        h2p,
        dyo,
        dyp,
        shards,
        scratch=[
            pltpu.VMEM(big, BF),
            pltpu.VMEM(big, BF),
            pltpu.VMEM((D, D), BF),
            pltpu.VMEM((D, D), BF),
            pltpu.VMEM(big, BF),
            pltpu.VMEM(big, BF),
            pltpu.VMEM(big, F32),
            pltpu.VMEM(big, F32),
        ],
        micros=30,
        name="feed",
    )


def result_body(at, middle, down, other, bias, out):
    total = middle[...] + (down[...] + other[...] + bias[...].astype(F32))
    low = total.astype(BF)
    for q in range(4):
        out[q] = low


def spread_body(at, a, b, c, d, out):
    total = ((a[...] + b[...]) + (c[...] + d[...])).astype(out.dtype)
    for q in range(16):
        out[q] = total


def hidden_out_body(at, mine, theirs, up, down):
    for ref, core in ((mine, at[CORE]), (theirs, 1 - at[CORE])):
        start = pl.multiple_of(core * HALF_FF, HALF_FF)
        half = jnp.concatenate([ref[q] for q in range(8)], axis=0).astype(F32)
        up[:, pl.ds(start, HALF_FF)] = half.T
        for q in range(8):
            row = pl.multiple_of(start + 48 * q, 16)
            down[pl.ds(row, 48), :] = ref[8 + q].astype(F32)


def middle_back_body(at, *refs):
    dho, dhp, mid, gain, dy = refs[:5]
    outs_of = refs[5:9]
    weights = refs[9:13]
    dmid, gm, gp, small = refs[13:17]
    outs_grad = refs[17:21]
    da = refs[21]
    gain_sum = shift_sum = bias_sum = down_sum = jnp.zeros((1, D), F32)
    for r in range(0, SEQ, ROWS):
        at = slice(r, r + ROWS)
        grad = dho[at, :] + dhp[at, :].astype(F32)
        scaled, inverse = normalize(mid[at, :])
        out_grad = dy[at, :].astype(F32)
        total = out_grad + norm_back(grad, scaled, inverse, gain[1:2, :])
        dmid[at, :] = total
        low = total.astype(BF)
        da[at, :] = low
        gain_sum += colsum(grad * scaled)
        shift_sum += colsum(grad)
        bias_sum += colsum(low.astype(F32))
        down_sum += colsum(out_grad)
        for k in range(4):
            outs_grad[k][at, :] = nt(low, weights[k][...]).astype(BF)
    for k in range(4):
        weight_grad = tn(outs_of[k][...], da[...])
        for h in range(LH):
            gm[k, 32 * h : 32 * h + 32, :] = weight_grad[64 * h : 64 * h + 32, :]
            gp[k, 32 * h : 32 * h + 32, :] = weight_grad[64 * h + 32 : 64 * h + 64, :]
    small[...] = jnp.concatenate(
        [gain_sum, shift_sum, bias_sum, down_sum, jnp.zeros((4, D), F32)], axis=0
    )


def in_three(value):
    one = value.astype(BF)
    left = value - one.astype(F32)
    two = left.astype(BF)
    return [one, two, (left - two.astype(F32)).astype(BF)]


def attend_backward_body(sc, qkv, logs, o, do, keep, h1, dqkv, gm, gp, bias):
    mask = ((1.0 - keep[...]) * NEG).astype(BF)
    ones = jnp.ones((SEQ, 3), BF)
    rest = jnp.zeros((SEQ, HD - 4), BF)
    for h in range(LH):
        a = HD * h
        heads_grad = do[:, a : a + HD]
        inner = jnp.sum(
            heads_grad.astype(F32) * o[:, a : a + HD].astype(F32), axis=-1, keepdims=True
        )
        keys = qkv[:, LW + a : LW + a + HD]
        vals = qkv[:, 2 * LW + a : 2 * LW + a + HD]
        queries = qkv[:, a : a + HD] * jnp.asarray(SCALE, BF)
        logits = nt(
            jnp.concatenate([keys, ones, mask, rest], axis=1),
            jnp.concatenate(
                [queries] + in_three(-logs[:, h : h + 1]) + [ones[:, 0:1], rest], axis=1
            ),
        )
        probs = jnp.exp(logits)
        centred = nt(
            jnp.concatenate([vals, ones, ones[:, 0:1], rest], axis=1),
            jnp.concatenate(
                [heads_grad] + in_three(-inner) + [jnp.zeros((SEQ, 1), BF), rest], axis=1
            ),
        )
        score_grad = (probs * centred).astype(BF)
        dqkv[:, 2 * LW + a : 2 * LW + a + HD] = nn(probs.astype(BF), heads_grad).astype(BF)
        dqkv[:, LW + a : LW + a + HD] = nn(score_grad, queries).astype(BF)
        dqkv[:, a : a + HD] = (tn(score_grad, keys) * SCALE).astype(BF)
    bias[...] = jnp.broadcast_to(colsum(dqkv[...].astype(F32)), (8, 3 * LW))
    for t in range(3):
        weight_grad = tn(dqkv[:, LW * t : LW * t + LW], h1[...])
        for h in range(LH):
            g = 3 * t + h
            gm[32 * g : 32 * g + 32, :] = weight_grad[64 * h : 64 * h + 32, :]
            gp[32 * g : 32 * g + 32, :] = weight_grad[64 * h + 32 : 64 * h + 64, :]


def attend_backward(scalars, qkv, logs, o, do, keep, h1):
    return call(
        attend_backward_body,
        [((SEQ, 3 * LW), BF), ((288, D), F32), ((288, D), F32), ((8, 3 * LW), F32)],
        scalars,
        qkv,
        logs,
        o,
        do,
        keep,
        h1,
        micros=8,
        name="attend_backward",
    )


def first_back_body(sc, *refs):
    x, gain, dmid, small_two = refs[:4]
    dqkvs = refs[4:8]
    weights = refs[8:12]
    biases = refs[12:16]
    grad_in, small = refs[16:]
    gain_sum = shift_sum = jnp.zeros((1, D), F32)
    for r in range(0, SEQ, ROWS):
        at = slice(r, r + ROWS)
        grad = nn(dqkvs[0][at, :], weights[0][...])
        for k in range(1, 4):
            grad += nn(dqkvs[k][at, :], weights[k][...])
        scaled, inverse = normalize(x[at, :].astype(F32))
        total = dmid[at, :] + norm_back(grad, scaled, inverse, gain[0:1, :])
        grad_in[at, :] = total.astype(BF)
        gain_sum += colsum(grad * scaled)
        shift_sum += colsum(grad)
    rest = jnp.zeros((1, D - 3 * LW), F32)
    small[...] = jnp.concatenate(
        [gain_sum, shift_sum, small_two[0:4, :]]
        + [jnp.concatenate([biases[k][0:1, :], rest], axis=1) for k in range(4)]
        + [jnp.zeros((6, D), F32)],
        axis=0,
    )


def heads_send_body(ks, sc, *refs):
    mine, theirs = refs[0:2], refs[2:4]
    out_mine, out_theirs, send = refs[4:7]
    for p in range(16):
        parts = []
        for j, k in enumerate(ks):
            if p < 12:
                rows = slice(24 * p, 24 * p + 24)
                parts.append(mine[j][rows, :] + theirs[j][rows, :])
            else:
                rows = slice(24 * (p - 12), 24 * (p - 12) + 24)
                parts.append(out_mine[k, rows, :] + out_theirs[k, rows, :])
        send[p] = jnp.concatenate(parts, axis=0).astype(BF)


def heads_fold_body(sc, got_one, got_two, small, small_other, sums, *to_y):
    parts = []
    for got in (got_one, got_two):
        total = got[0].astype(F32)
        for q in range(1, 16):
            total += got[q].astype(F32)
        parts += [total[0:24], total[24:48]]
    common = small[0:6, :] + small_other[0:6, :]
    crossed = pltpu.roll(small_other[...], D - 32, 1)
    rest = jnp.zeros((1, D - HALF_FF), F32)
    for k in range(4):
        place = ORDER.index(k)
        lanes = slice((place % 2) * HALF_FF, (place % 2 + 1) * HALF_FF)
        hidden = jnp.concatenate([sums[place // 2, 0:1, lanes], rest], axis=1)
        heads_bias = small[6 + k : 7 + k, :] + crossed[6 + k : 7 + k, :]
        to_y[k][0:24, :] = parts[place]
        to_y[k][24:32, :] = jnp.concatenate([common, heads_bias, hidden], axis=0)


def heads_out_body(
    sc, mine, theirs, qkv_grad, out_grad, out_sum, down_sum, gains, biases, up_sum, qkv_sum, rows
):
    sums = []
    for ref, core in ((mine, sc[CORE]), (theirs, 1 - sc[CORE])):
        for p in range(16):
            for g in range(3):
                at = 24 * p + 8 * g
                row = pl.multiple_of(64 * (at // 32) + 32 * core + at % 32, 8)
                rows[pl.ds(row, 8), :] = ref[p, 8 * g : 8 * g + 8, :]
        total = ref[0, 24:32, :]
        for p in range(1, 16):
            total += ref[p, 24:32, :]
        sums.append(total)
    for t in range(3):
        qkv_grad[t] = rows[LW * t : LW * t + LW, :]
    out_grad[...] = rows[3 * LW :, :]
    own, other = sums
    gains[...] = jnp.concatenate([own[0:1], own[2:3]], axis=0)
    biases[...] = jnp.concatenate([own[1:2], own[3:4]], axis=0)
    out_sum[...] = own[4:5].reshape(D)
    down_sum[...] = own[5:6].reshape(D)
    low = (lax.broadcasted_iota(jnp.int32, (8, D), 1) % HD) < 32
    swap = sc[CORE] != 0
    hidden = (own[7:8, 0:HALF_FF], other[7:8, 0:HALF_FF])
    up_sum[...] = jnp.concatenate(
        [jnp.where(swap, hidden[1], hidden[0]), jnp.where(swap, hidden[0], hidden[1])], axis=1
    ).reshape(D)
    first = jnp.where(sc[CORE] == 0, own, other)
    second = jnp.where(sc[CORE] == 0, other, own)
    natural = jnp.where(low, first, pltpu.roll(second, 32, 1))[6:7]
    qkv_sum[...] = jnp.concatenate([natural[:, 0:LW], natural[:, 2 * LW : 3 * LW]], axis=0)


def along_y(value, step):
    return lax.ppermute(value, "y", [(i, (i + step) % 4) for i in range(4)])


def after(value, *done):
    return lax.optimization_barrier((value, *done))[0]


def other_core(value):
    return lax.ppermute(value, "c", [(0, 1), (1, 0)])


def per_device(
    tokens,
    qkv_weight,
    qkv_bias,
    out_weight,
    out_bias,
    up_weight,
    up_bias,
    down_weight,
    down_bias,
    norm_gains,
    norm_biases,
    cotangent,
    band_masks,
):
    core = lax.axis_index("c")
    here = lax.axis_index("y")
    at = jnp.concatenate(
        [
            jnp.stack([core, lax.axis_index("x"), lax.axis_index("z"), here]).astype(jnp.int32),
            band_masks.reshape(16),
        ]
    )
    four = range(4)
    mine, theirs, hidden = call(
        pack_body,
        [((400, D), BF), ((400, D), BF), ((784, D), BF)],
        jnp.zeros((1,), jnp.int32),
        jnp.swapaxes(qkv_weight, 1, 2),
        out_weight,
        qkv_bias,
        up_weight,
        down_weight,
        up_bias,
        scratch=[pltpu.VMEM((D, D), BF)],
        micros=5,
        name="pack",
    )
    heads_mine, heads_theirs = {0: mine}, {0: theirs}
    for s in (1, 3):
        heads_mine[s] = along_y(mine, s)
    relayed = [along_y(heads_mine[1][:200], 1), along_y(heads_mine[3][200:], 3)]
    shards = lax.all_gather(hidden, "y", axis=0, tiled=False)
    out_grad, keep_col = call(
        masks_body,
        [((SEQ, D), BF), ((SEQ, 1), F32)],
        at,
        cotangent,
        specs={0: OWN_ROWS},
        micros=2,
        name="masks",
    )
    out_grad_other = other_core(out_grad)

    weights, qkvs, outs_of, logs = {}, {}, {}, {}
    first_in, *rest = attend_forward(
        True, at, (tokens, norm_gains, norm_biases), heads_mine[0], heads_theirs[0], keep_col
    )
    weights[0], qkvs[0], outs_of[0], logs[0] = rest
    def forward(s, *done):
        weights[s], qkvs[s], outs_of[s], logs[s] = attend_forward(
            False, at, (after(first_in, *done),), heads_mine[s], heads_theirs[s], keep_col
        )

    for s in (1, 3):
        heads_theirs[s] = other_core(after(heads_mine[s], qkvs[0]))
    forward(1, qkvs[0])
    forward(3, qkvs[1])
    heads_mine[2] = jnp.concatenate(after(relayed, qkvs[1]), axis=0)
    heads_theirs[2] = other_core(heads_mine[2])
    forward(2, qkvs[3])
    middle, second_in = call(
        middle_body,
        [((SEQ, D), F32), ((SEQ, D), BF)],
        at,
        tokens,
        out_bias[None],
        norm_gains,
        norm_biases,
        *[outs_of[k] for k in four],
        *[weights[k] for k in four],
        specs={0: OWN_ROWS} | {8 + k: OUT_ROWS for k in four},
        micros=4,
        name="middle",
    )
    second_other = other_core(second_in)
    hidden_grads, down_own, down_other, back_own, back_other, up_sums = feed(
        at, second_in, second_other, out_grad, out_grad_other, shards
    )
    back_received = other_core(back_other)
    hidden_pieces = lax.psum_scatter(
        hidden_grads.reshape(16, 4 * 48, D), ("x", "z"), scatter_dimension=0, tiled=False
    ).reshape(4, 48, D)
    down_received = other_core(down_other)

    middle_grad, out_gm, out_gp, small_two, *outs_grad = call(
        middle_back_body,
        [((SEQ, D), F32), ((4, 96, D), F32), ((4, 96, D), F32), ((8, D), F32)]
        + [((SEQ, LW), BF)] * 4,
        at,
        back_own,
        back_received,
        middle,
        norm_gains,
        out_grad,
        *[outs_of[k] for k in four],
        *[weights[k] for k in four],
        specs={9 + k: OUT_ROWS for k in four},
        scratch=[pltpu.VMEM((SEQ, D), BF)],
        micros=7,
        name="middle_back",
    )
    out_received = other_core(out_gp)
    (result_copies,) = call(
        result_body,
        [((4, SEQ, D), BF)],
        at,
        middle,
        down_own,
        down_received,
        down_bias[None],
        micros=2,
        name="result_rows",
    )
    result = lax.all_to_all(result_copies, "y", 0, 0, tiled=True).reshape(4 * SEQ, D)
    dqkvs, gms, gps, bias_sums = {}, {}, {}, {}

    def backward(s, *done):
        heads_grad = after(outs_grad[s], *done)
        dqkvs[s], gms[s], gp, bias_sums[s] = attend_backward(
            at, qkvs[s], logs[s], outs_of[s], heads_grad, keep_col, first_in
        )
        gps[s] = other_core(gp)

    def heads_send(ks, *done):
        (send,) = call(
            functools.partial(heads_send_body, ks),
            [((16, 48, D), BF)],
            at,
            *[gms[k] for k in ks],
            *[gps[k] for k in ks],
            after(out_gm, *done),
            out_received,
            micros=4,
            name="heads_send",
        )
        return send

    backward(0, result_copies)
    backward(1, dqkvs[0])
    backward(3, dqkvs[1], gps[0])
    send_one = heads_send(ORDER[0:2], dqkvs[3])
    send_one, result = lax.optimization_barrier((send_one, result))
    heads_one = lax.all_to_all(send_one, ("x", "z"), 0, 0, tiled=True)
    backward(2, dqkvs[3], send_one)
    grad_own, small = call(
        first_back_body,
        [((SEQ, D), BF), ((16, D), F32)],
        at,
        tokens,
        norm_gains,
        after(middle_grad, dqkvs[2]),
        small_two,
        *[dqkvs[k] for k in four],
        *[weights[k] for k in four],
        *[bias_sums[k] for k in four],
        specs={0: OWN_ROWS} | {8 + k: QKV_ROWS for k in four},
        micros=8,
        name="first_back",
    )
    hidden_pieces = after(hidden_pieces, small)
    (hidden_copies,) = call(
        spread_body,
        [((16, 48, D), BF)],
        at,
        hidden_pieces[0],
        *[along_y(hidden_pieces[s], -s) for s in (1, 2, 3)],
        micros=2,
        name="hidden_spread",
    )
    send_two = heads_send(ORDER[2:4], small)
    heads_two = lax.all_to_all(after(send_two, heads_one), ("x", "z"), 0, 0, tiled=True)
    input_grad = lax.all_gather(grad_own, "y", axis=0, tiled=True).astype(F32)
    to_y = call(
        heads_fold_body,
        [((32, D), F32)] * 4,
        at,
        heads_one,
        heads_two,
        small,
        other_core(small),
        up_sums,
        micros=3,
        name="heads_fold",
    )
    hidden_half = lax.all_to_all(after(hidden_copies, to_y[0]), ("x", "z"), 0, 0, tiled=True)
    (heads_copies,) = call(
        spread_body,
        [((16, 32, D), F32)],
        at,
        to_y[0],
        *[along_y(to_y[s], -s) for s in (1, 2, 3)],
        micros=2,
        name="heads_spread",
    )
    heads_half = lax.all_to_all(heads_copies, ("x", "z"), 0, 0, tiled=True)
    up_weight_grad, down_weight_grad = call(
        hidden_out_body,
        [((D, D), F32), ((D, D), F32)],
        at,
        hidden_half,
        other_core(hidden_half),
        micros=4,
        name="hidden_out",
    )
    keep_rows = jnp.repeat(band_masks, SPATIAL, axis=1).reshape(-1, 1)
    heads_half_sent, input_grad, up_weight_grad, down_weight_grad, result = (
        lax.optimization_barrier(
            (
                heads_half,
                input_grad,
                up_weight_grad,
                down_weight_grad,
                jnp.where(keep_rows > 0, result, jnp.asarray(0, BF)),
            )
        )
    )
    heads_half_other = other_core(heads_half_sent)
    qkv_grad, out_weight_grad, out_sum, down_sum, gains, biases, up_sum, qkv_sum = call(
        heads_out_body,
        [
            ((3, LW, D), F32),
            ((LW, D), F32),
            ((D,), F32),
            ((D,), F32),
            ((2, D), F32),
            ((2, D), F32),
            ((D,), F32),
            ((2, LW), F32),
        ],
        at,
        heads_half,
        heads_half_other,
        scratch=[pltpu.VMEM((D, D), F32)],
        micros=4,
        name="heads_out",
    )
    return (
        result,
        input_grad,
        jnp.swapaxes(qkv_grad, 1, 2),
        qkv_sum,
        out_weight_grad,
        out_sum,
        up_weight_grad,
        up_sum,
        down_weight_grad,
        down_sum,
        gains,
        biases,
    )


def solution(mesh):
    inner = Mesh(np.array(mesh.devices).reshape(4, 4, 2, 4), ("x", "z", "c", "y"))
    dp = ("x", "z", "c")
    in_specs = (
        P(dp, None),
        P(None, None, "y"),
        P(None, "y"),
        P("y", None),
        P(),
        P(None, "y"),
        P("y"),
        P("y", None),
        P(),
        P(),
        P(),
        P(dp, None),
        P(dp, None),
    )
    out_specs = (
        P(dp, None),
        P(dp, None),
        P(None, None, "y"),
        P(None, "y"),
        P("y", None),
        P(),
        P(None, "y"),
        P("y"),
        P("y", None),
        P(),
        P(),
        P(),
    )
    return jax.shard_map(
        per_device, mesh=inner, in_specs=in_specs, out_specs=out_specs, check_vma=False
    )
```

```python
import functools

import jax
import jax.numpy as jnp
import numpy as np
from jax import lax
from jax.experimental import pallas as pl
from jax.experimental.pallas import tpu as pltpu
from jax.sharding import Mesh, PartitionSpec as P

BF = jnp.bfloat16
F32 = jnp.float32
SEQ = 576
SPATIAL = 144
D = 768
HD = 64
LH = 3
LW = 192
HALF_FF = 384
ROWS = 192
VMEM = 56 * 2**20
NEG = -1e30
PER_MICRO = 1e6
SCALE = HD**-0.5
ORDER = (0, 1, 3, 2)


def nt(a, b):
    return lax.dot_general(a, b, (((1,), (1,)), ((), ())), preferred_element_type=F32)


def nn(a, b):
    return lax.dot_general(a, b, (((1,), (0,)), ((), ())), preferred_element_type=F32)


def tn(a, b):
    return lax.dot_general(a, b, (((0,), (0,)), ((), ())), preferred_element_type=F32)


def normalize(value):
    centred = value - jnp.mean(value, axis=-1, keepdims=True)
    inverse = lax.rsqrt(jnp.mean(centred * centred, axis=-1, keepdims=True) + 1e-05)
    return centred * inverse, inverse


def norm_back(grad_out, scaled, inverse, gain):
    scaled_grad = grad_out * gain
    centre = jnp.mean(scaled_grad, axis=-1, keepdims=True)
    along = jnp.mean(scaled_grad * scaled, axis=-1, keepdims=True)
    return inverse * (scaled_grad - centre - scaled * along)


def colsum(value):
    return jnp.sum(value, axis=0, keepdims=True)


def call(body, outs, scalars, *args, scratch=(), specs=None, micros=1.0, name=None):
    shapes = [jax.ShapeDtypeStruct(s, d) for s, d in outs]
    moved = sum(int(np.prod(a.shape)) * a.dtype.itemsize for a in list(args) + shapes)
    return pl.pallas_call(
        body,
        grid_spec=pltpu.PrefetchScalarGridSpec(
            num_scalar_prefetch=1,
            grid=(1,),
            in_specs=[
                (specs or {}).get(i, pl.BlockSpec(memory_space=pltpu.VMEM))
                for i in range(len(args))
            ],
            out_specs=[pl.BlockSpec(memory_space=pltpu.VMEM) for _ in shapes],
            scratch_shapes=list(scratch),
        ),
        out_shape=shapes,
        compiler_params=pltpu.CompilerParams(vmem_limit_bytes=VMEM),
        cost_estimate=pl.CostEstimate(
            flops=int(micros * PER_MICRO), bytes_accessed=moved // 1024, transcendentals=0
        ),
        name=name,
    )(scalars, *args)


OWN_ROWS = pl.BlockSpec((SEQ, D), lambda i, at: (at[3], 0))
OUT_ROWS = pl.BlockSpec((LW, D), lambda i, at: (3, 0))
QKV_ROWS = pl.BlockSpec((3 * LW, D), lambda i, at: (0, 0))
CORE, X_AT, Z_AT, Y_AT, MASKS = 0, 1, 2, 3, 4


def pack_body(
    at,
    qkv_weight,
    out_weight,
    qkv_bias,
    up_weight,
    down_weight,
    up_bias,
    mine,
    theirs,
    hidden,
    rows,
):
    core = lax.axis_index("c")
    for t in range(3):
        rows[LW * t : LW * t + LW, :] = qkv_weight[t]
    rows[3 * LW :, :] = out_weight[...]
    lane = lax.broadcasted_iota(jnp.int32, (8, D), 1)
    low = (lane % HD) < 32
    given = qkv_bias[...].astype(F32)
    none = jnp.zeros((1, LW), F32)
    bias = jnp.concatenate([given[0:1], none, given[1:2], none], axis=1)
    bias = jnp.broadcast_to(bias, (8, D))
    parts = (
        jnp.where(low, bias, 0.0),
        jnp.where(low, pltpu.roll(bias, D - 32, 1), 0.0),
    )

    def fill(ref, half):
        for g in range(12):
            ref[32 * g : 32 * g + 32, :] = rows[64 * g + 32 * half : 64 * g + 32 * half + 32, :]
        part = parts[half]
        shifted = pltpu.roll(part, 32, 1)
        ref[384:400, :] = jnp.concatenate(
            [part[0:1], shifted[0:1], jnp.zeros((14, D), F32)], axis=0
        ).astype(BF)

    @pl.when(core == 0)
    def _():
        fill(mine, 0)
        fill(theirs, 1)

    @pl.when(core != 0)
    def _():
        fill(mine, 1)
        fill(theirs, 0)

    start = pl.multiple_of(core * HALF_FF, HALF_FF)
    hidden[0:HALF_FF, :] = up_weight[:, pl.ds(start, HALF_FF)].T
    hidden[HALF_FF : 2 * HALF_FF, :] = down_weight[pl.ds(start, HALF_FF), :]
    up_row = up_bias[...].astype(F32).reshape(1, D)
    up_part = jnp.where(core == 0, up_row[:, 0:HALF_FF], up_row[:, HALF_FF:])
    hidden[2 * HALF_FF : 2 * HALF_FF + 16, :] = jnp.concatenate(
        [
            jnp.concatenate([up_part, jnp.zeros((1, D - HALF_FF), F32)], axis=1),
            jnp.zeros((15, D), F32),
        ],
        axis=0,
    ).astype(BF)


def masks_body(at, cot, dy, keep_col):
    kept = [at[MASKS + 4 * at[Y_AT] + g].astype(F32) for g in range(4)]
    for g in range(4):
        rows = slice(g * SPATIAL, (g + 1) * SPATIAL)
        dy[rows, :] = (cot[rows, :].astype(F32) * kept[g]).astype(BF)
        keep_col[rows, :] = jnp.full((SPATIAL, 1), kept[g])


def attend_forward_body(first, at, *refs):
    if first:
        x, gain, shift, wm, wp, keep, h1, w, qkv, o, logs = refs
        for r in range(0, SEQ, 96):
            scaled, _ = normalize(x[r : r + 96, :].astype(F32))
            h1[r : r + 96, :] = (scaled * gain[0:1, :] + shift[0:1, :]).astype(BF)
    else:
        h1, wm, wp, keep, w, qkv, o, logs = refs
    for g in range(12):
        w[64 * g : 64 * g + 32, :] = wm[32 * g : 32 * g + 32, :]
        w[64 * g + 32 : 64 * g + 64, :] = wp[32 * g : 32 * g + 32, :]
    bias = (wm[384:385, :] + wp[385:386, :])[:, : 3 * LW].astype(F32)
    for r in range(0, SEQ, ROWS):
        qkv[r : r + ROWS, :] = (nt(h1[r : r + ROWS, :], w[0 : 3 * LW, :]) + bias).astype(BF)
    mask = ((1.0 - keep[...]) * NEG).astype(BF)
    ones = jnp.ones((SEQ, 1), BF)
    rest = jnp.zeros((SEQ, HD - 1), BF)
    for h in range(LH):
        a = HD * h
        keys = jnp.concatenate([qkv[:, LW + a : LW + a + HD], mask, rest], axis=1)
        queries = jnp.concatenate(
            [qkv[:, a : a + HD] * jnp.asarray(SCALE, BF), ones, rest], axis=1
        )
        scores = nt(queries, keys)
        peak = jnp.max(scores, axis=-1, keepdims=True)
        expos = jnp.exp(scores - peak)
        total = jnp.sum(expos, axis=-1, keepdims=True)
        probs = (expos * (1.0 / total)).astype(BF)
        o[:, a : a + HD] = nn(probs, qkv[:, 2 * LW + a : 2 * LW + a + HD]).astype(BF)
        logs[:, h : h + 1] = peak + jnp.log(total)


def attend_forward(first, scalars, lead, wm, wp, keep):
    outs = [((D, D), BF), ((SEQ, 3 * LW), BF), ((SEQ, LW), BF), ((SEQ, 128), F32)]
    if first:
        outs = [((SEQ, D), BF)] + outs
    return call(
        functools.partial(attend_forward_body, first),
        outs,
        scalars,
        *lead,
        wm,
        wp,
        keep,
        specs={0: OWN_ROWS} if first else None,
        micros=8,
        name="attend_forward",
    )


def middle_body(at, *refs):
    x, bias, gain, shift = refs[:4]
    outs_of = refs[4:8]
    weights = refs[8:12]
    mid, h2 = refs[12:]
    for r in range(0, SEQ, ROWS):
        total = x[r : r + ROWS, :].astype(F32) + bias[...].astype(F32)
        for k in range(4):
            total = total + nn(outs_of[k][r : r + ROWS, :], weights[k][...])
        mid[r : r + ROWS, :] = total
        scaled, _ = normalize(total)
        h2[r : r + ROWS, :] = (scaled * gain[1:2, :] + shift[1:2, :]).astype(BF)


def feed_body(at, h2o, h2p, dyo, dyp, shards, grads, mo, mp, dho, dhp, ubias, *scratch):
    h2, dy, wu, wd, act, dhid, accm, acch = scratch
    owners = [lax.rem(at[Y_AT] + 4 - k, 4) for k in range(4)]
    h2[0:SEQ, :] = h2o[...]
    h2[SEQ:, :] = h2p[...]
    dy[0:SEQ, :] = dyo[...]
    dy[SEQ:, :] = dyp[...]
    block = 2 * SEQ
    for pair in range(2):
        one, two = (shards.at[owners[ORDER[2 * pair + s]]] for s in range(2))
        wu[0:HALF_FF, :] = one[0:HALF_FF, :]
        wu[HALF_FF:, :] = two[0:HALF_FF, :]
        wd[0:HALF_FF, :] = one[HALF_FF : 2 * HALF_FF, :]
        wd[HALF_FF:, :] = two[HALF_FF : 2 * HALF_FF, :]
        bias = jnp.concatenate(
            [one[768:784, 0:HALF_FF][0:1], two[768:784, 0:HALF_FF][0:1]], axis=1
        ).astype(F32)
        ubias[pair] = jnp.zeros((8, D), F32)

        @pl.loop(0, 2 * SEQ // block)
        def _(i):
            rows = pl.ds(pl.multiple_of(i * block, block), block)
            hid = nt(h2[rows, :], wu[...]) + bias
            cdf = 0.5 + 0.5 * lax.erf(hid * np.float32(0.7071067811865476))
            active = (hid * cdf).astype(BF)
            slope = cdf + hid * (
                jnp.exp(hid * hid * np.float32(-0.5)) * np.float32(0.3989422804014327)
            )
            act[rows, :] = active
            hid_grad = (nt(dy[rows, :], wd[...]) * slope).astype(BF)
            dhid[rows, :] = hid_grad
            ubias[pair, 0:1, :] += colsum(hid_grad.astype(F32))
            down = nn(active, wd[...])
            back = nn(hid_grad, wu[...])
            if pair == 0:
                accm[rows, :] = down
                acch[rows, :] = back
            else:
                accm[rows, :] += down
                acch[rows, :] += back

        for s in range(2):
            k = ORDER[2 * pair + s]
            cols = slice(s * HALF_FF, (s + 1) * HALF_FF)
            up_grad = tn(dhid[:, cols], h2[...])
            down_grad = tn(act[:, cols], dy[...])
            for q in range(8):
                rows = slice(48 * q, 48 * q + 48)
                grads[q, k] = up_grad[rows, :]
                grads[8 + q, k] = down_grad[rows, :]
    mo[...] = accm[0:SEQ, :]
    mp[...] = accm[SEQ:, :]
    dho[...] = acch[0:SEQ, :]
    dhp[...] = acch[SEQ:, :].astype(BF)


def feed(scalars, h2o, h2p, dyo, dyp, shards):
    big = (2 * SEQ, D)
    return call(
        feed_body,
        [
            ((16, 4, 48, D), F32),
            ((SEQ, D), F32),
            ((SEQ, D), F32),
            ((SEQ, D), F32),
            ((SEQ, D), BF),
            ((2, 8, D), F32),
        ],
        scalars,
        h2o,
        h2p,
        dyo,
        dyp,
        shards,
        scratch=[
            pltpu.VMEM(big, BF),
            pltpu.VMEM(big, BF),
            pltpu.VMEM((D, D), BF),
            pltpu.VMEM((D, D), BF),
            pltpu.VMEM(big, BF),
            pltpu.VMEM(big, BF),
            pltpu.VMEM(big, F32),
            pltpu.VMEM(big, F32),
        ],
        micros=30,
        name="feed",
    )


def result_body(at, middle, down, other, bias, out):
    total = middle[...] + (down[...] + other[...] + bias[...].astype(F32))
    low = total.astype(BF)
    for q in range(4):
        out[q] = low


def spread_body(at, a, b, c, d, out):
    total = ((a[...] + b[...]) + (c[...] + d[...])).astype(out.dtype)
    for q in range(16):
        out[q] = total


def hidden_out_body(at, mine, theirs, up, down):
    for ref, core in ((mine, at[CORE]), (theirs, 1 - at[CORE])):
        start = pl.multiple_of(core * HALF_FF, HALF_FF)
        half = jnp.concatenate([ref[q] for q in range(8)], axis=0).astype(F32)
        up[:, pl.ds(start, HALF_FF)] = half.T
        for q in range(8):
            row = pl.multiple_of(start + 48 * q, 16)
            down[pl.ds(row, 48), :] = ref[8 + q].astype(F32)


def middle_back_body(at, *refs):
    dho, dhp, mid, gain, dy = refs[:5]
    outs_of = refs[5:9]
    weights = refs[9:13]
    dmid, gm, gp, small = refs[13:17]
    outs_grad = refs[17:21]
    da = refs[21]
    gain_sum = shift_sum = bias_sum = down_sum = jnp.zeros((1, D), F32)
    for r in range(0, SEQ, ROWS):
        at = slice(r, r + ROWS)
        grad = dho[at, :] + dhp[at, :].astype(F32)
        scaled, inverse = normalize(mid[at, :])
        out_grad = dy[at, :].astype(F32)
        total = out_grad + norm_back(grad, scaled, inverse, gain[1:2, :])
        dmid[at, :] = total
        low = total.astype(BF)
        da[at, :] = low
        gain_sum += colsum(grad * scaled)
        shift_sum += colsum(grad)
        bias_sum += colsum(low.astype(F32))
        down_sum += colsum(out_grad)
        for k in range(4):
            outs_grad[k][at, :] = nt(low, weights[k][...]).astype(BF)
    for k in range(4):
        weight_grad = tn(outs_of[k][...], da[...])
        for h in range(LH):
            gm[k, 32 * h : 32 * h + 32, :] = weight_grad[64 * h : 64 * h + 32, :]
            gp[k, 32 * h : 32 * h + 32, :] = weight_grad[64 * h + 32 : 64 * h + 64, :]
    small[...] = jnp.concatenate(
        [gain_sum, shift_sum, bias_sum, down_sum, jnp.zeros((4, D), F32)], axis=0
    )


def in_three(value):
    one = value.astype(BF)
    left = value - one.astype(F32)
    two = left.astype(BF)
    return [one, two, (left - two.astype(F32)).astype(BF)]


def attend_backward_body(sc, qkv, logs, o, do, keep, h1, dqkv, gm, gp, bias):
    mask = ((1.0 - keep[...]) * NEG).astype(BF)
    ones = jnp.ones((SEQ, 3), BF)
    rest = jnp.zeros((SEQ, HD - 4), BF)
    for h in range(LH):
        a = HD * h
        heads_grad = do[:, a : a + HD]
        inner = jnp.sum(
            heads_grad.astype(F32) * o[:, a : a + HD].astype(F32), axis=-1, keepdims=True
        )
        keys = qkv[:, LW + a : LW + a + HD]
        vals = qkv[:, 2 * LW + a : 2 * LW + a + HD]
        queries = qkv[:, a : a + HD] * jnp.asarray(SCALE, BF)
        logits = nt(
            jnp.concatenate([keys, ones, mask, rest], axis=1),
            jnp.concatenate(
                [queries] + in_three(-logs[:, h : h + 1]) + [ones[:, 0:1], rest], axis=1
            ),
        )
        probs = jnp.exp(logits)
        centred = nt(
            jnp.concatenate([vals, ones, ones[:, 0:1], rest], axis=1),
            jnp.concatenate(
                [heads_grad] + in_three(-inner) + [jnp.zeros((SEQ, 1), BF), rest], axis=1
            ),
        )
        score_grad = (probs * centred).astype(BF)
        dqkv[:, 2 * LW + a : 2 * LW + a + HD] = nn(probs.astype(BF), heads_grad).astype(BF)
        dqkv[:, LW + a : LW + a + HD] = nn(score_grad, queries).astype(BF)
        dqkv[:, a : a + HD] = (tn(score_grad, keys) * SCALE).astype(BF)
    bias[...] = jnp.broadcast_to(colsum(dqkv[...].astype(F32)), (8, 3 * LW))
    for t in range(3):
        weight_grad = tn(dqkv[:, LW * t : LW * t + LW], h1[...])
        for h in range(LH):
            g = 3 * t + h
            gm[32 * g : 32 * g + 32, :] = weight_grad[64 * h : 64 * h + 32, :]
            gp[32 * g : 32 * g + 32, :] = weight_grad[64 * h + 32 : 64 * h + 64, :]


def attend_backward(scalars, qkv, logs, o, do, keep, h1):
    return call(
        attend_backward_body,
        [((SEQ, 3 * LW), BF), ((288, D), F32), ((288, D), F32), ((8, 3 * LW), F32)],
        scalars,
        qkv,
        logs,
        o,
        do,
        keep,
        h1,
        micros=8,
        name="attend_backward",
    )


def first_back_body(sc, *refs):
    x, gain, dmid, small_two = refs[:4]
    dqkvs = refs[4:8]
    weights = refs[8:12]
    biases = refs[12:16]
    grad_in, small = refs[16:]
    gain_sum = shift_sum = jnp.zeros((1, D), F32)
    for r in range(0, SEQ, ROWS):
        at = slice(r, r + ROWS)
        grad = nn(dqkvs[0][at, :], weights[0][...])
        for k in range(1, 4):
            grad += nn(dqkvs[k][at, :], weights[k][...])
        scaled, inverse = normalize(x[at, :].astype(F32))
        total = dmid[at, :] + norm_back(grad, scaled, inverse, gain[0:1, :])
        grad_in[at, :] = total.astype(BF)
        gain_sum += colsum(grad * scaled)
        shift_sum += colsum(grad)
    rest = jnp.zeros((1, D - 3 * LW), F32)
    small[...] = jnp.concatenate(
        [gain_sum, shift_sum, small_two[0:4, :]]
        + [jnp.concatenate([biases[k][0:1, :], rest], axis=1) for k in range(4)]
        + [jnp.zeros((6, D), F32)],
        axis=0,
    )


def heads_send_body(ks, sc, *refs):
    mine, theirs = refs[0:4], refs[4:8]
    out_mine, out_theirs, send = refs[8:11]
    for p in range(16):
        parts = []
        for j, k in enumerate(ks):
            if p < 12:
                rows = slice(24 * p, 24 * p + 24)
                parts.append(mine[j][rows, :] + theirs[j][rows, :])
            else:
                rows = slice(24 * (p - 12), 24 * (p - 12) + 24)
                parts.append(out_mine[k, rows, :] + out_theirs[k, rows, :])
        send[p] = jnp.concatenate(parts, axis=0).astype(BF)


def heads_fold_body(sc, got, small, small_other, sums, *to_y):
    total = got[0].astype(F32)
    for q in range(1, 16):
        total += got[q].astype(F32)
    parts = [total[24 * j : 24 * j + 24] for j in range(4)]
    common = small[0:6, :] + small_other[0:6, :]
    crossed = pltpu.roll(small_other[...], D - 32, 1)
    rest = jnp.zeros((1, D - HALF_FF), F32)
    for k in range(4):
        place = ORDER.index(k)
        lanes = slice((place % 2) * HALF_FF, (place % 2 + 1) * HALF_FF)
        hidden = jnp.concatenate([sums[place // 2, 0:1, lanes], rest], axis=1)
        heads_bias = small[6 + k : 7 + k, :] + crossed[6 + k : 7 + k, :]
        to_y[k][0:24, :] = parts[place]
        to_y[k][24:32, :] = jnp.concatenate([common, heads_bias, hidden], axis=0)


def heads_out_body(
    sc, mine, theirs, qkv_grad, out_grad, out_sum, down_sum, gains, biases, up_sum, qkv_sum, rows
):
    sums = []
    for ref, core in ((mine, sc[CORE]), (theirs, 1 - sc[CORE])):
        for p in range(16):
            for g in range(3):
                at = 24 * p + 8 * g
                row = pl.multiple_of(64 * (at // 32) + 32 * core + at % 32, 8)
                rows[pl.ds(row, 8), :] = ref[p, 8 * g : 8 * g + 8, :]
        total = ref[0, 24:32, :]
        for p in range(1, 16):
            total += ref[p, 24:32, :]
        sums.append(total)
    for t in range(3):
        qkv_grad[t] = rows[LW * t : LW * t + LW, :]
    out_grad[...] = rows[3 * LW :, :]
    own, other = sums
    gains[...] = jnp.concatenate([own[0:1], own[2:3]], axis=0)
    biases[...] = jnp.concatenate([own[1:2], own[3:4]], axis=0)
    out_sum[...] = own[4:5].reshape(D)
    down_sum[...] = own[5:6].reshape(D)
    low = (lax.broadcasted_iota(jnp.int32, (8, D), 1) % HD) < 32
    swap = sc[CORE] != 0
    hidden = (own[7:8, 0:HALF_FF], other[7:8, 0:HALF_FF])
    up_sum[...] = jnp.concatenate(
        [jnp.where(swap, hidden[1], hidden[0]), jnp.where(swap, hidden[0], hidden[1])], axis=1
    ).reshape(D)
    first = jnp.where(sc[CORE] == 0, own, other)
    second = jnp.where(sc[CORE] == 0, other, own)
    natural = jnp.where(low, first, pltpu.roll(second, 32, 1))[6:7]
    qkv_sum[...] = jnp.concatenate([natural[:, 0:LW], natural[:, 2 * LW : 3 * LW]], axis=0)


def along_y(value, step):
    return lax.ppermute(value, "y", [(i, (i + step) % 4) for i in range(4)])


def after(value, *done):
    return lax.optimization_barrier((value, *done))[0]


def other_core(value):
    return lax.ppermute(value, "c", [(0, 1), (1, 0)])


def per_device(
    tokens,
    qkv_weight,
    qkv_bias,
    out_weight,
    out_bias,
    up_weight,
    up_bias,
    down_weight,
    down_bias,
    norm_gains,
    norm_biases,
    cotangent,
    band_masks,
):
    core = lax.axis_index("c")
    here = lax.axis_index("y")
    at = jnp.concatenate(
        [
            jnp.stack([core, lax.axis_index("x"), lax.axis_index("z"), here]).astype(jnp.int32),
            band_masks.reshape(16),
        ]
    )
    four = range(4)
    mine, theirs, hidden = call(
        pack_body,
        [((400, D), BF), ((400, D), BF), ((784, D), BF)],
        jnp.zeros((1,), jnp.int32),
        jnp.swapaxes(qkv_weight, 1, 2),
        out_weight,
        qkv_bias,
        up_weight,
        down_weight,
        up_bias,
        scratch=[pltpu.VMEM((D, D), BF)],
        micros=5,
        name="pack",
    )
    heads_mine, heads_theirs = {0: mine}, {0: theirs}
    for s in (1, 3):
        heads_mine[s] = along_y(mine, s)
    relayed = [along_y(heads_mine[1][:200], 1), along_y(heads_mine[3][200:], 3)]
    shards = lax.all_gather(hidden, "y", axis=0, tiled=False)
    out_grad, keep_col = call(
        masks_body,
        [((SEQ, D), BF), ((SEQ, 1), F32)],
        at,
        cotangent,
        specs={0: OWN_ROWS},
        micros=2,
        name="masks",
    )
    out_grad_other = other_core(out_grad)

    weights, qkvs, outs_of, logs = {}, {}, {}, {}
    first_in, *rest = attend_forward(
        True, at, (tokens, norm_gains, norm_biases), heads_mine[0], heads_theirs[0], keep_col
    )
    weights[0], qkvs[0], outs_of[0], logs[0] = rest
    def forward(s, *done):
        weights[s], qkvs[s], outs_of[s], logs[s] = attend_forward(
            False, at, (after(first_in, *done),), heads_mine[s], heads_theirs[s], keep_col
        )

    for s in (1, 3):
        heads_theirs[s] = other_core(after(heads_mine[s], qkvs[0]))
    forward(1, qkvs[0])
    forward(3, qkvs[1])
    heads_mine[2] = jnp.concatenate(after(relayed, qkvs[1]), axis=0)
    heads_theirs[2] = other_core(heads_mine[2])
    forward(2, qkvs[3])
    middle, second_in = call(
        middle_body,
        [((SEQ, D), F32), ((SEQ, D), BF)],
        at,
        tokens,
        out_bias[None],
        norm_gains,
        norm_biases,
        *[outs_of[k] for k in four],
        *[weights[k] for k in four],
        specs={0: OWN_ROWS} | {8 + k: OUT_ROWS for k in four},
        micros=4,
        name="middle",
    )
    second_other = other_core(second_in)
    hidden_grads, down_own, down_other, back_own, back_other, up_sums = feed(
        at, second_in, second_other, out_grad, out_grad_other, shards
    )
    back_received = other_core(back_other)
    hidden_pieces = lax.psum_scatter(
        hidden_grads.reshape(16, 4 * 48, D), ("x", "z"), scatter_dimension=0, tiled=False
    ).reshape(4, 48, D)
    down_received = other_core(down_other)

    middle_grad, out_gm, out_gp, small_two, *outs_grad = call(
        middle_back_body,
        [((SEQ, D), F32), ((4, 96, D), F32), ((4, 96, D), F32), ((8, D), F32)]
        + [((SEQ, LW), BF)] * 4,
        at,
        back_own,
        back_received,
        middle,
        norm_gains,
        out_grad,
        *[outs_of[k] for k in four],
        *[weights[k] for k in four],
        specs={9 + k: OUT_ROWS for k in four},
        scratch=[pltpu.VMEM((SEQ, D), BF)],
        micros=7,
        name="middle_back",
    )
    out_received = other_core(out_gp)
    (result_copies,) = call(
        result_body,
        [((4, SEQ, D), BF)],
        at,
        middle,
        down_own,
        down_received,
        down_bias[None],
        micros=2,
        name="result_rows",
    )
    result = lax.all_to_all(result_copies, "y", 0, 0, tiled=True).reshape(4 * SEQ, D)
    dqkvs, gms, gps, bias_sums = {}, {}, {}, {}

    def backward(s, *done):
        heads_grad = after(outs_grad[s], *done)
        dqkvs[s], gms[s], gp, bias_sums[s] = attend_backward(
            at, qkvs[s], logs[s], outs_of[s], heads_grad, keep_col, first_in
        )
        gps[s] = other_core(gp)

    def heads_send(ks, *done):
        (send,) = call(
            functools.partial(heads_send_body, ks),
            [((16, 96, D), BF)],
            at,
            *[gms[k] for k in ks],
            *[gps[k] for k in ks],
            after(out_gm, *done),
            out_received,
            micros=4,
            name="heads_send",
        )
        return send

    backward(0, result_copies)
    backward(1, dqkvs[0])
    backward(3, dqkvs[1], gps[0])
    backward(2, dqkvs[3])
    grad_own, small = call(
        first_back_body,
        [((SEQ, D), BF), ((16, D), F32)],
        at,
        tokens,
        norm_gains,
        after(middle_grad, dqkvs[2]),
        small_two,
        *[dqkvs[k] for k in four],
        *[weights[k] for k in four],
        *[bias_sums[k] for k in four],
        specs={0: OWN_ROWS} | {8 + k: QKV_ROWS for k in four},
        micros=8,
        name="first_back",
    )
    small_other = other_core(small)
    hidden_pieces, small_other = lax.optimization_barrier((hidden_pieces, small_other))
    (hidden_copies,) = call(
        spread_body,
        [((16, 48, D), BF)],
        at,
        hidden_pieces[0],
        *[along_y(hidden_pieces[s], -s) for s in (1, 2, 3)],
        micros=2,
        name="hidden_spread",
    )
    send, result = lax.optimization_barrier((heads_send(ORDER, small), result))
    heads_got = lax.all_to_all(send, ("x", "z"), 0, 0, tiled=True)
    input_grad = lax.all_gather(grad_own, "y", axis=0, tiled=True).astype(F32)
    to_y = call(
        heads_fold_body,
        [((32, D), F32)] * 4,
        at,
        heads_got,
        small,
        small_other,
        up_sums,
        micros=3,
        name="heads_fold",
    )
    hidden_half = lax.all_to_all(after(hidden_copies, heads_got), ("x", "z"), 0, 0, tiled=True)
    (heads_copies,) = call(
        spread_body,
        [((16, 32, D), F32)],
        at,
        to_y[0],
        *[along_y(to_y[s], -s) for s in (1, 2, 3)],
        micros=2,
        name="heads_spread",
    )
    heads_half = lax.all_to_all(heads_copies, ("x", "z"), 0, 0, tiled=True)
    up_weight_grad, down_weight_grad = call(
        hidden_out_body,
        [((D, D), F32), ((D, D), F32)],
        at,
        hidden_half,
        other_core(hidden_half),
        micros=4,
        name="hidden_out",
    )
    keep_rows = jnp.repeat(band_masks, SPATIAL, axis=1).reshape(-1, 1)
    heads_half_sent, input_grad, up_weight_grad, down_weight_grad, result = (
        lax.optimization_barrier(
            (
                heads_half,
                input_grad,
                up_weight_grad,
                down_weight_grad,
                jnp.where(keep_rows > 0, result, jnp.asarray(0, BF)),
            )
        )
    )
    heads_half_other = other_core(heads_half_sent)
    qkv_grad, out_weight_grad, out_sum, down_sum, gains, biases, up_sum, qkv_sum = call(
        heads_out_body,
        [
            ((3, LW, D), F32),
            ((LW, D), F32),
            ((D,), F32),
            ((D,), F32),
            ((2, D), F32),
            ((2, D), F32),
            ((D,), F32),
            ((2, LW), F32),
        ],
        at,
        heads_half,
        heads_half_other,
        scratch=[pltpu.VMEM((D, D), F32)],
        micros=4,
        name="heads_out",
    )
    return (
        result,
        input_grad,
        jnp.swapaxes(qkv_grad, 1, 2),
        qkv_sum,
        out_weight_grad,
        out_sum,
        up_weight_grad,
        up_sum,
        down_weight_grad,
        down_sum,
        gains,
        biases,
    )


def solution(mesh):
    inner = Mesh(np.array(mesh.devices).reshape(4, 4, 2, 4), ("x", "z", "c", "y"))
    dp = ("x", "z", "c")
    in_specs = (
        P(dp, None),
        P(None, None, "y"),
        P(None, "y"),
        P("y", None),
        P(),
        P(None, "y"),
        P("y"),
        P("y", None),
        P(),
        P(),
        P(),
        P(dp, None),
        P(dp, None),
    )
    out_specs = (
        P(dp, None),
        P(dp, None),
        P(None, None, "y"),
        P(None, "y"),
        P("y", None),
        P(),
        P(None, "y"),
        P("y"),
        P("y", None),
        P(),
        P(),
        P(),
    )
    return jax.shard_map(
        per_device, mesh=inner, in_specs=in_specs, out_specs=out_specs, check_vma=False
    )
```

```python
import functools

import jax
import jax.numpy as jnp
import numpy as np
from jax import lax
from jax.experimental import pallas as pl
from jax.experimental.pallas import tpu as pltpu
from jax.sharding import Mesh, PartitionSpec as P

BF = jnp.bfloat16
F32 = jnp.float32
SEQ = 576
SPATIAL = 144
D = 768
HD = 64
LH = 3
LW = 192
HALF_FF = 384
ROWS = 192
VMEM = 56 * 2**20
NEG = -1e30
PER_MICRO = 1e6
SCALE = HD**-0.5
ORDER = (0, 1, 3, 2)


def nt(a, b):
    return lax.dot_general(a, b, (((1,), (1,)), ((), ())), preferred_element_type=F32)


def nn(a, b):
    return lax.dot_general(a, b, (((1,), (0,)), ((), ())), preferred_element_type=F32)


def tn(a, b):
    return lax.dot_general(a, b, (((0,), (0,)), ((), ())), preferred_element_type=F32)


def normalize(value):
    centred = value - jnp.mean(value, axis=-1, keepdims=True)
    inverse = lax.rsqrt(jnp.mean(centred * centred, axis=-1, keepdims=True) + 1e-05)
    return centred * inverse, inverse


def norm_back(grad_out, scaled, inverse, gain):
    scaled_grad = grad_out * gain
    centre = jnp.mean(scaled_grad, axis=-1, keepdims=True)
    along = jnp.mean(scaled_grad * scaled, axis=-1, keepdims=True)
    return inverse * (scaled_grad - centre - scaled * along)


def colsum(value):
    return jnp.sum(value, axis=0, keepdims=True)


def call(body, outs, scalars, *args, scratch=(), specs=None, micros=1.0, name=None):
    shapes = [jax.ShapeDtypeStruct(s, d) for s, d in outs]
    moved = sum(int(np.prod(a.shape)) * a.dtype.itemsize for a in list(args) + shapes)
    return pl.pallas_call(
        body,
        grid_spec=pltpu.PrefetchScalarGridSpec(
            num_scalar_prefetch=1,
            grid=(1,),
            in_specs=[
                (specs or {}).get(i, pl.BlockSpec(memory_space=pltpu.VMEM))
                for i in range(len(args))
            ],
            out_specs=[pl.BlockSpec(memory_space=pltpu.VMEM) for _ in shapes],
            scratch_shapes=list(scratch),
        ),
        out_shape=shapes,
        compiler_params=pltpu.CompilerParams(vmem_limit_bytes=VMEM),
        cost_estimate=pl.CostEstimate(
            flops=int(micros * PER_MICRO), bytes_accessed=moved // 1024, transcendentals=0
        ),
        name=name,
    )(scalars, *args)


OWN_ROWS = pl.BlockSpec((SEQ, D), lambda i, at: (at[3], 0))
OUT_ROWS = pl.BlockSpec((LW, D), lambda i, at: (3, 0))
QKV_ROWS = pl.BlockSpec((3 * LW, D), lambda i, at: (0, 0))
CORE, X_AT, Z_AT, Y_AT, MASKS = 0, 1, 2, 3, 4


def pack_body(
    at,
    qkv_weight,
    out_weight,
    qkv_bias,
    up_weight,
    down_weight,
    up_bias,
    mine,
    theirs,
    hidden,
    rows,
):
    core = lax.axis_index("c")
    for t in range(3):
        rows[LW * t : LW * t + LW, :] = qkv_weight[t]
    rows[3 * LW :, :] = out_weight[...]
    lane = lax.broadcasted_iota(jnp.int32, (8, D), 1)
    low = (lane % HD) < 32
    given = qkv_bias[...].astype(F32)
    none = jnp.zeros((1, LW), F32)
    bias = jnp.concatenate([given[0:1], none, given[1:2], none], axis=1)
    bias = jnp.broadcast_to(bias, (8, D))
    parts = (
        jnp.where(low, bias, 0.0),
        jnp.where(low, pltpu.roll(bias, D - 32, 1), 0.0),
    )

    def fill(ref, half):
        for g in range(12):
            ref[32 * g : 32 * g + 32, :] = rows[64 * g + 32 * half : 64 * g + 32 * half + 32, :]
        part = parts[half]
        shifted = pltpu.roll(part, 32, 1)
        ref[384:400, :] = jnp.concatenate(
            [part[0:1], shifted[0:1], jnp.zeros((14, D), F32)], axis=0
        ).astype(BF)

    @pl.when(core == 0)
    def _():
        fill(mine, 0)
        fill(theirs, 1)

    @pl.when(core != 0)
    def _():
        fill(mine, 1)
        fill(theirs, 0)

    start = pl.multiple_of(core * HALF_FF, HALF_FF)
    hidden[0:HALF_FF, :] = up_weight[:, pl.ds(start, HALF_FF)].T
    hidden[HALF_FF : 2 * HALF_FF, :] = down_weight[pl.ds(start, HALF_FF), :]
    up_row = up_bias[...].astype(F32).reshape(1, D)
    up_part = jnp.where(core == 0, up_row[:, 0:HALF_FF], up_row[:, HALF_FF:])
    hidden[2 * HALF_FF : 2 * HALF_FF + 16, :] = jnp.concatenate(
        [
            jnp.concatenate([up_part, jnp.zeros((1, D - HALF_FF), F32)], axis=1),
            jnp.zeros((15, D), F32),
        ],
        axis=0,
    ).astype(BF)


def masks_body(at, cot, dy, keep_col):
    kept = [at[MASKS + 4 * at[Y_AT] + g].astype(F32) for g in range(4)]
    for g in range(4):
        rows = slice(g * SPATIAL, (g + 1) * SPATIAL)
        dy[rows, :] = (cot[rows, :].astype(F32) * kept[g]).astype(BF)
        keep_col[rows, :] = jnp.full((SPATIAL, 1), kept[g])


def attend_forward_body(first, at, *refs):
    if first:
        x, gain, shift, wm, wp, keep, h1, w, qkv, o, logs = refs
        for r in range(0, SEQ, 96):
            scaled, _ = normalize(x[r : r + 96, :].astype(F32))
            h1[r : r + 96, :] = (scaled * gain[0:1, :] + shift[0:1, :]).astype(BF)
    else:
        h1, wm, wp, keep, w, qkv, o, logs = refs
    for g in range(12):
        w[64 * g : 64 * g + 32, :] = wm[32 * g : 32 * g + 32, :]
        w[64 * g + 32 : 64 * g + 64, :] = wp[32 * g : 32 * g + 32, :]
    bias = (wm[384:385, :] + wp[385:386, :])[:, : 3 * LW].astype(F32)
    for r in range(0, SEQ, ROWS):
        qkv[r : r + ROWS, :] = (nt(h1[r : r + ROWS, :], w[0 : 3 * LW, :]) + bias).astype(BF)
    mask = ((1.0 - keep[...]) * NEG).astype(BF)
    ones = jnp.ones((SEQ, 1), BF)
    rest = jnp.zeros((SEQ, HD - 1), BF)
    for h in range(LH):
        a = HD * h
        keys = jnp.concatenate([qkv[:, LW + a : LW + a + HD], mask, rest], axis=1)
        queries = jnp.concatenate(
            [qkv[:, a : a + HD] * jnp.asarray(SCALE, BF), ones, rest], axis=1
        )
        scores = nt(queries, keys)
        peak = jnp.max(scores, axis=-1, keepdims=True)
        expos = jnp.exp(scores - peak)
        total = jnp.sum(expos, axis=-1, keepdims=True)
        probs = (expos * (1.0 / total)).astype(BF)
        o[:, a : a + HD] = nn(probs, qkv[:, 2 * LW + a : 2 * LW + a + HD]).astype(BF)
        logs[:, h : h + 1] = peak + jnp.log(total)


def attend_forward(first, scalars, lead, wm, wp, keep):
    outs = [((D, D), BF), ((SEQ, 3 * LW), BF), ((SEQ, LW), BF), ((SEQ, 128), F32)]
    if first:
        outs = [((SEQ, D), BF)] + outs
    return call(
        functools.partial(attend_forward_body, first),
        outs,
        scalars,
        *lead,
        wm,
        wp,
        keep,
        specs={0: OWN_ROWS} if first else None,
        micros=8,
        name="attend_forward",
    )


def middle_body(at, *refs):
    x, bias, gain, shift = refs[:4]
    outs_of = refs[4:8]
    weights = refs[8:12]
    mid, h2 = refs[12:]
    for r in range(0, SEQ, ROWS):
        total = x[r : r + ROWS, :].astype(F32) + bias[...].astype(F32)
        for k in range(4):
            total = total + nn(outs_of[k][r : r + ROWS, :], weights[k][...])
        mid[r : r + ROWS, :] = total
        scaled, _ = normalize(total)
        h2[r : r + ROWS, :] = (scaled * gain[1:2, :] + shift[1:2, :]).astype(BF)


def feed_body(at, h2o, h2p, dyo, dyp, shards, grads, mo, mp, dho, dhp, ubias, *scratch):
    h2, dy, wu, wd, act, dhid, accm, acch = scratch
    owners = [lax.rem(at[Y_AT] + 4 - k, 4) for k in range(4)]
    h2[0:SEQ, :] = h2o[...]
    h2[SEQ:, :] = h2p[...]
    dy[0:SEQ, :] = dyo[...]
    dy[SEQ:, :] = dyp[...]
    block = 2 * SEQ
    for pair in range(2):
        one, two = (shards.at[owners[ORDER[2 * pair + s]]] for s in range(2))
        wu[0:HALF_FF, :] = one[0:HALF_FF, :]
        wu[HALF_FF:, :] = two[0:HALF_FF, :]
        wd[0:HALF_FF, :] = one[HALF_FF : 2 * HALF_FF, :]
        wd[HALF_FF:, :] = two[HALF_FF : 2 * HALF_FF, :]
        bias = jnp.concatenate(
            [one[768:784, 0:HALF_FF][0:1], two[768:784, 0:HALF_FF][0:1]], axis=1
        ).astype(F32)
        ubias[pair] = jnp.zeros((8, D), F32)

        @pl.loop(0, 2 * SEQ // block)
        def _(i):
            rows = pl.ds(pl.multiple_of(i * block, block), block)
            hid = nt(h2[rows, :], wu[...]) + bias
            cdf = 0.5 + 0.5 * lax.erf(hid * np.float32(0.7071067811865476))
            active = (hid * cdf).astype(BF)
            slope = cdf + hid * (
                jnp.exp(hid * hid * np.float32(-0.5)) * np.float32(0.3989422804014327)
            )
            act[rows, :] = active
            hid_grad = (nt(dy[rows, :], wd[...]) * slope).astype(BF)
            dhid[rows, :] = hid_grad
            ubias[pair, 0:1, :] += colsum(hid_grad.astype(F32))
            down = nn(active, wd[...])
            back = nn(hid_grad, wu[...])
            if pair == 0:
                accm[rows, :] = down
                acch[rows, :] = back
            else:
                accm[rows, :] += down
                acch[rows, :] += back

        for s in range(2):
            k = ORDER[2 * pair + s]
            cols = slice(s * HALF_FF, (s + 1) * HALF_FF)
            up_grad = tn(dhid[:, cols], h2[...])
            down_grad = tn(act[:, cols], dy[...])
            for q in range(8):
                rows = slice(48 * q, 48 * q + 48)
                grads[q, k] = up_grad[rows, :]
                grads[8 + q, k] = down_grad[rows, :]
    mo[...] = accm[0:SEQ, :]
    mp[...] = accm[SEQ:, :]
    dho[...] = acch[0:SEQ, :]
    dhp[...] = acch[SEQ:, :].astype(BF)


def feed(scalars, h2o, h2p, dyo, dyp, shards):
    big = (2 * SEQ, D)
    return call(
        feed_body,
        [
            ((16, 4, 48, D), F32),
            ((SEQ, D), F32),
            ((SEQ, D), F32),
            ((SEQ, D), F32),
            ((SEQ, D), BF),
            ((2, 8, D), F32),
        ],
        scalars,
        h2o,
        h2p,
        dyo,
        dyp,
        shards,
        scratch=[
            pltpu.VMEM(big, BF),
            pltpu.VMEM(big, BF),
            pltpu.VMEM((D, D), BF),
            pltpu.VMEM((D, D), BF),
            pltpu.VMEM(big, BF),
            pltpu.VMEM(big, BF),
            pltpu.VMEM(big, F32),
            pltpu.VMEM(big, F32),
        ],
        micros=30,
        name="feed",
    )


def result_body(at, middle, down, other, bias, out):
    total = middle[...] + (down[...] + other[...] + bias[...].astype(F32))
    low = total.astype(BF)
    for q in range(4):
        out[q] = low


def spread_body(at, a, b, c, d, out):
    total = ((a[...] + b[...]) + (c[...] + d[...])).astype(out.dtype)
    for q in range(16):
        out[q] = total


def hidden_out_body(at, mine, theirs, up, down):
    for ref, core in ((mine, at[CORE]), (theirs, 1 - at[CORE])):
        start = pl.multiple_of(core * HALF_FF, HALF_FF)
        half = jnp.concatenate([ref[q] for q in range(8)], axis=0).astype(F32)
        up[:, pl.ds(start, HALF_FF)] = half.T
        for q in range(8):
            row = pl.multiple_of(start + 48 * q, 16)
            down[pl.ds(row, 48), :] = ref[8 + q].astype(F32)


def middle_back_body(at, *refs):
    dho, dhp, mid, gain, dy = refs[:5]
    outs_of = refs[5:9]
    weights = refs[9:13]
    dmid, gm, gp, small = refs[13:17]
    outs_grad = refs[17:21]
    da = refs[21]
    gain_sum = shift_sum = bias_sum = down_sum = jnp.zeros((1, D), F32)
    for r in range(0, SEQ, ROWS):
        at = slice(r, r + ROWS)
        grad = dho[at, :] + dhp[at, :].astype(F32)
        scaled, inverse = normalize(mid[at, :])
        out_grad = dy[at, :].astype(F32)
        total = out_grad + norm_back(grad, scaled, inverse, gain[1:2, :])
        dmid[at, :] = total
        low = total.astype(BF)
        da[at, :] = low
        gain_sum += colsum(grad * scaled)
        shift_sum += colsum(grad)
        bias_sum += colsum(low.astype(F32))
        down_sum += colsum(out_grad)
        for k in range(4):
            outs_grad[k][at, :] = nt(low, weights[k][...]).astype(BF)
    for k in range(4):
        weight_grad = tn(outs_of[k][...], da[...])
        for h in range(LH):
            gm[k, 32 * h : 32 * h + 32, :] = weight_grad[64 * h : 64 * h + 32, :]
            gp[k, 32 * h : 32 * h + 32, :] = weight_grad[64 * h + 32 : 64 * h + 64, :]
    small[...] = jnp.concatenate(
        [gain_sum, shift_sum, bias_sum, down_sum, jnp.zeros((4, D), F32)], axis=0
    )


def in_three(value):
    one = value.astype(BF)
    left = value - one.astype(F32)
    two = left.astype(BF)
    return [one, two, (left - two.astype(F32)).astype(BF)]


def attend_backward_body(sc, qkv, logs, o, do, keep, h1, dqkv, gm, gp, bias):
    mask = ((1.0 - keep[...]) * NEG).astype(BF)
    ones = jnp.ones((SEQ, 3), BF)
    rest = jnp.zeros((SEQ, HD - 4), BF)
    for h in range(LH):
        a = HD * h
        heads_grad = do[:, a : a + HD]
        inner = jnp.sum(
            heads_grad.astype(F32) * o[:, a : a + HD].astype(F32), axis=-1, keepdims=True
        )
        keys = qkv[:, LW + a : LW + a + HD]
        vals = qkv[:, 2 * LW + a : 2 * LW + a + HD]
        queries = qkv[:, a : a + HD] * jnp.asarray(SCALE, BF)
        logits = nt(
            jnp.concatenate([keys, ones, mask, rest], axis=1),
            jnp.concatenate(
                [queries] + in_three(-logs[:, h : h + 1]) + [ones[:, 0:1], rest], axis=1
            ),
        )
        probs = jnp.exp(logits)
        centred = nt(
            jnp.concatenate([vals, ones, ones[:, 0:1], rest], axis=1),
            jnp.concatenate(
                [heads_grad] + in_three(-inner) + [jnp.zeros((SEQ, 1), BF), rest], axis=1
            ),
        )
        score_grad = (probs * centred).astype(BF)
        dqkv[:, 2 * LW + a : 2 * LW + a + HD] = nn(probs.astype(BF), heads_grad).astype(BF)
        dqkv[:, LW + a : LW + a + HD] = nn(score_grad, queries).astype(BF)
        dqkv[:, a : a + HD] = (tn(score_grad, keys) * SCALE).astype(BF)
    bias[...] = jnp.broadcast_to(colsum(dqkv[...].astype(F32)), (8, 3 * LW))
    weight_grad = tn(dqkv[...], h1[...])
    for g in range(3 * LH):
        gm[32 * g : 32 * g + 32, :] = weight_grad[64 * g : 64 * g + 32, :]
        gp[32 * g : 32 * g + 32, :] = weight_grad[64 * g + 32 : 64 * g + 64, :]


def attend_backward(scalars, qkv, logs, o, do, keep, h1):
    return call(
        attend_backward_body,
        [((SEQ, 3 * LW), BF), ((288, D), F32), ((288, D), F32), ((8, 3 * LW), F32)],
        scalars,
        qkv,
        logs,
        o,
        do,
        keep,
        h1,
        micros=8,
        name="attend_backward",
    )


def first_back_body(sc, *refs):
    x, gain, dmid, small_two = refs[:4]
    dqkvs = refs[4:8]
    weights = refs[8:12]
    biases = refs[12:16]
    grad_in, small = refs[16:]
    gain_sum = shift_sum = jnp.zeros((1, D), F32)
    for r in range(0, SEQ, ROWS):
        at = slice(r, r + ROWS)
        grad = nn(dqkvs[0][at, :], weights[0][...])
        for k in range(1, 4):
            grad += nn(dqkvs[k][at, :], weights[k][...])
        scaled, inverse = normalize(x[at, :].astype(F32))
        total = dmid[at, :] + norm_back(grad, scaled, inverse, gain[0:1, :])
        grad_in[at, :] = total.astype(BF)
        gain_sum += colsum(grad * scaled)
        shift_sum += colsum(grad)
    rest = jnp.zeros((1, D - 3 * LW), F32)
    small[...] = jnp.concatenate(
        [gain_sum, shift_sum, small_two[0:4, :]]
        + [jnp.concatenate([biases[k][0:1, :], rest], axis=1) for k in range(4)]
        + [jnp.zeros((6, D), F32)],
        axis=0,
    )


def heads_send_body(ks, sc, *refs):
    mine, theirs = refs[0:4], refs[4:8]
    out_mine, out_theirs, send = refs[8:11]
    for p in range(16):
        parts = []
        for j, k in enumerate(ks):
            if p < 12:
                rows = slice(24 * p, 24 * p + 24)
                parts.append(mine[j][rows, :] + theirs[j][rows, :])
            else:
                rows = slice(24 * (p - 12), 24 * (p - 12) + 24)
                parts.append(out_mine[k, rows, :] + out_theirs[k, rows, :])
        send[p] = jnp.concatenate(parts, axis=0).astype(BF)


def heads_fold_body(sc, got, small, small_other, sums, *to_y):
    total = got[0].astype(F32)
    for q in range(1, 16):
        total += got[q].astype(F32)
    parts = [total[24 * j : 24 * j + 24] for j in range(4)]
    common = small[0:6, :] + small_other[0:6, :]
    crossed = pltpu.roll(small_other[...], D - 32, 1)
    rest = jnp.zeros((1, D - HALF_FF), F32)
    for k in range(4):
        place = ORDER.index(k)
        lanes = slice((place % 2) * HALF_FF, (place % 2 + 1) * HALF_FF)
        hidden = jnp.concatenate([sums[place // 2, 0:1, lanes], rest], axis=1)
        heads_bias = small[6 + k : 7 + k, :] + crossed[6 + k : 7 + k, :]
        to_y[k][0:24, :] = parts[place]
        to_y[k][24:32, :] = jnp.concatenate([common, heads_bias, hidden], axis=0)


def heads_out_body(
    sc, mine, theirs, qkv_grad, out_grad, out_sum, down_sum, gains, biases, up_sum, qkv_sum, rows
):
    sums = []
    for ref, core in ((mine, sc[CORE]), (theirs, 1 - sc[CORE])):
        for p in range(16):
            for g in range(3):
                at = 24 * p + 8 * g
                row = pl.multiple_of(64 * (at // 32) + 32 * core + at % 32, 8)
                rows[pl.ds(row, 8), :] = ref[p, 8 * g : 8 * g + 8, :]
        total = ref[0, 24:32, :]
        for p in range(1, 16):
            total += ref[p, 24:32, :]
        sums.append(total)
    for t in range(3):
        qkv_grad[t] = rows[LW * t : LW * t + LW, :]
    out_grad[...] = rows[3 * LW :, :]
    own, other = sums
    gains[...] = jnp.concatenate([own[0:1], own[2:3]], axis=0)
    biases[...] = jnp.concatenate([own[1:2], own[3:4]], axis=0)
    out_sum[...] = own[4:5].reshape(D)
    down_sum[...] = own[5:6].reshape(D)
    low = (lax.broadcasted_iota(jnp.int32, (8, D), 1) % HD) < 32
    swap = sc[CORE] != 0
    hidden = (own[7:8, 0:HALF_FF], other[7:8, 0:HALF_FF])
    up_sum[...] = jnp.concatenate(
        [jnp.where(swap, hidden[1], hidden[0]), jnp.where(swap, hidden[0], hidden[1])], axis=1
    ).reshape(D)
    first = jnp.where(sc[CORE] == 0, own, other)
    second = jnp.where(sc[CORE] == 0, other, own)
    natural = jnp.where(low, first, pltpu.roll(second, 32, 1))[6:7]
    qkv_sum[...] = jnp.concatenate([natural[:, 0:LW], natural[:, 2 * LW : 3 * LW]], axis=0)


def along_y(value, step):
    return lax.ppermute(value, "y", [(i, (i + step) % 4) for i in range(4)])


def after(value, *done):
    return lax.optimization_barrier((value, *done))[0]


def other_core(value):
    return lax.ppermute(value, "c", [(0, 1), (1, 0)])


def per_device(
    tokens,
    qkv_weight,
    qkv_bias,
    out_weight,
    out_bias,
    up_weight,
    up_bias,
    down_weight,
    down_bias,
    norm_gains,
    norm_biases,
    cotangent,
    band_masks,
):
    core = lax.axis_index("c")
    here = lax.axis_index("y")
    at = jnp.concatenate(
        [
            jnp.stack([core, lax.axis_index("x"), lax.axis_index("z"), here]).astype(jnp.int32),
            band_masks.reshape(16),
        ]
    )
    four = range(4)
    mine, theirs, hidden = call(
        pack_body,
        [((400, D), BF), ((400, D), BF), ((784, D), BF)],
        jnp.zeros((1,), jnp.int32),
        jnp.swapaxes(qkv_weight, 1, 2),
        out_weight,
        qkv_bias,
        up_weight,
        down_weight,
        up_bias,
        scratch=[pltpu.VMEM((D, D), BF)],
        micros=5,
        name="pack",
    )
    heads_mine, heads_theirs = {0: mine}, {0: theirs}
    for s in (1, 3):
        heads_mine[s] = along_y(mine, s)
    relayed = [along_y(heads_mine[1][:200], 1), along_y(heads_mine[3][200:], 3)]
    shards = lax.all_gather(hidden, "y", axis=0, tiled=False)
    out_grad, keep_col = call(
        masks_body,
        [((SEQ, D), BF), ((SEQ, 1), F32)],
        at,
        cotangent,
        specs={0: OWN_ROWS},
        micros=2,
        name="masks",
    )
    out_grad_other = other_core(out_grad)

    weights, qkvs, outs_of, logs = {}, {}, {}, {}
    first_in, *rest = attend_forward(
        True, at, (tokens, norm_gains, norm_biases), heads_mine[0], heads_theirs[0], keep_col
    )
    weights[0], qkvs[0], outs_of[0], logs[0] = rest
    def forward(s, *done):
        weights[s], qkvs[s], outs_of[s], logs[s] = attend_forward(
            False, at, (after(first_in, *done),), heads_mine[s], heads_theirs[s], keep_col
        )

    for s in (1, 3):
        heads_theirs[s] = other_core(after(heads_mine[s], qkvs[0]))
    forward(1, qkvs[0])
    forward(3, qkvs[1])
    heads_mine[2] = jnp.concatenate(after(relayed, qkvs[1]), axis=0)
    heads_theirs[2] = other_core(heads_mine[2])
    forward(2, qkvs[3])
    middle, second_in = call(
        middle_body,
        [((SEQ, D), F32), ((SEQ, D), BF)],
        at,
        tokens,
        out_bias[None],
        norm_gains,
        norm_biases,
        *[outs_of[k] for k in four],
        *[weights[k] for k in four],
        specs={0: OWN_ROWS} | {8 + k: OUT_ROWS for k in four},
        micros=4,
        name="middle",
    )
    second_other = other_core(second_in)
    hidden_grads, down_own, down_other, back_own, back_other, up_sums = feed(
        at, second_in, second_other, out_grad, out_grad_other, shards
    )
    back_received = other_core(back_other)
    hidden_pieces = lax.psum_scatter(
        hidden_grads.reshape(16, 4 * 48, D), ("x", "z"), scatter_dimension=0, tiled=False
    ).reshape(4, 48, D)
    down_received = other_core(after(down_other, back_received))

    middle_grad, out_gm, out_gp, small_two, *outs_grad = call(
        middle_back_body,
        [((SEQ, D), F32), ((4, 96, D), F32), ((4, 96, D), F32), ((8, D), F32)]
        + [((SEQ, LW), BF)] * 4,
        at,
        back_own,
        back_received,
        middle,
        norm_gains,
        out_grad,
        *[outs_of[k] for k in four],
        *[weights[k] for k in four],
        specs={9 + k: OUT_ROWS for k in four},
        scratch=[pltpu.VMEM((SEQ, D), BF)],
        micros=7,
        name="middle_back",
    )
    out_received = other_core(out_gp)
    (result_copies,) = call(
        result_body,
        [((4, SEQ, D), BF)],
        at,
        middle,
        after(down_own, small_two),
        down_received,
        down_bias[None],
        micros=2,
        name="result_rows",
    )
    result = lax.all_to_all(result_copies, "y", 0, 0, tiled=True).reshape(4 * SEQ, D)
    dqkvs, gms, gps, bias_sums = {}, {}, {}, {}

    def backward(s, *done):
        heads_grad = after(outs_grad[s], *done)
        dqkvs[s], gms[s], gp, bias_sums[s] = attend_backward(
            at, qkvs[s], logs[s], outs_of[s], heads_grad, keep_col, first_in
        )
        gps[s] = other_core(gp)

    def heads_send(ks, *done):
        (send,) = call(
            functools.partial(heads_send_body, ks),
            [((16, 96, D), BF)],
            at,
            *[gms[k] for k in ks],
            *[gps[k] for k in ks],
            after(out_gm, *done),
            out_received,
            micros=4,
            name="heads_send",
        )
        return send

    backward(0, result_copies)
    backward(1, dqkvs[0])
    backward(3, dqkvs[1], gps[0])
    backward(2, dqkvs[3])
    grad_own, small = call(
        first_back_body,
        [((SEQ, D), BF), ((16, D), F32)],
        at,
        tokens,
        norm_gains,
        after(middle_grad, dqkvs[2]),
        small_two,
        *[dqkvs[k] for k in four],
        *[weights[k] for k in four],
        *[bias_sums[k] for k in four],
        specs={0: OWN_ROWS} | {8 + k: QKV_ROWS for k in four},
        micros=8,
        name="first_back",
    )
    small_other = other_core(small)
    hidden_pieces, small_other = lax.optimization_barrier((hidden_pieces, small_other))
    (hidden_copies,) = call(
        spread_body,
        [((16, 48, D), BF)],
        at,
        hidden_pieces[0],
        *[along_y(hidden_pieces[s], -s) for s in (1, 2, 3)],
        micros=2,
        name="hidden_spread",
    )
    send, result = lax.optimization_barrier((heads_send(ORDER, small), result))
    heads_got = lax.all_to_all(send, ("x", "z"), 0, 0, tiled=True)
    input_grad = lax.all_gather(grad_own, "y", axis=0, tiled=True).astype(F32)
    to_y = call(
        heads_fold_body,
        [((32, D), F32)] * 4,
        at,
        heads_got,
        small,
        small_other,
        up_sums,
        micros=3,
        name="heads_fold",
    )
    hidden_half = lax.all_to_all(after(hidden_copies, heads_got), ("x", "z"), 0, 0, tiled=True)
    (heads_copies,) = call(
        spread_body,
        [((16, 32, D), F32)],
        at,
        to_y[0],
        *[along_y(to_y[s], -s) for s in (1, 2, 3)],
        micros=2,
        name="heads_spread",
    )
    heads_half = lax.all_to_all(heads_copies, ("x", "z"), 0, 0, tiled=True)
    up_weight_grad, down_weight_grad = call(
        hidden_out_body,
        [((D, D), F32), ((D, D), F32)],
        at,
        hidden_half,
        other_core(hidden_half),
        micros=4,
        name="hidden_out",
    )
    keep_rows = jnp.repeat(band_masks, SPATIAL, axis=1).reshape(-1, 1)
    heads_half_sent, input_grad, up_weight_grad, down_weight_grad, result = (
        lax.optimization_barrier(
            (
                heads_half,
                input_grad,
                up_weight_grad,
                down_weight_grad,
                jnp.where(keep_rows > 0, result, jnp.asarray(0, BF)),
            )
        )
    )
    heads_half_other = other_core(heads_half_sent)
    qkv_grad, out_weight_grad, out_sum, down_sum, gains, biases, up_sum, qkv_sum = call(
        heads_out_body,
        [
            ((3, LW, D), F32),
            ((LW, D), F32),
            ((D,), F32),
            ((D,), F32),
            ((2, D), F32),
            ((2, D), F32),
            ((D,), F32),
            ((2, LW), F32),
        ],
        at,
        heads_half,
        heads_half_other,
        scratch=[pltpu.VMEM((D, D), F32)],
        micros=4,
        name="heads_out",
    )
    return (
        result,
        input_grad,
        jnp.swapaxes(qkv_grad, 1, 2),
        qkv_sum,
        out_weight_grad,
        out_sum,
        up_weight_grad,
        up_sum,
        down_weight_grad,
        down_sum,
        gains,
        biases,
    )


def solution(mesh):
    inner = Mesh(np.array(mesh.devices).reshape(4, 4, 2, 4), ("x", "z", "c", "y"))
    dp = ("x", "z", "c")
    in_specs = (
        P(dp, None),
        P(None, None, "y"),
        P(None, "y"),
        P("y", None),
        P(),
        P(None, "y"),
        P("y"),
        P("y", None),
        P(),
        P(),
        P(),
        P(dp, None),
        P(dp, None),
    )
    out_specs = (
        P(dp, None),
        P(dp, None),
        P(None, None, "y"),
        P(None, "y"),
        P("y", None),
        P(),
        P(None, "y"),
        P("y"),
        P("y", None),
        P(),
        P(),
        P(),
    )
    return jax.shard_map(
        per_device, mesh=inner, in_specs=in_specs, out_specs=out_specs, check_vma=False
    )
```

```python
import functools

import jax
import jax.numpy as jnp
import numpy as np
from jax import lax
from jax.experimental import pallas as pl
from jax.experimental.pallas import tpu as pltpu
from jax.sharding import Mesh, PartitionSpec as P

BF = jnp.bfloat16
F32 = jnp.float32
SEQ = 576
SPATIAL = 144
D = 768
HD = 64
LH = 3
LW = 192
HALF_FF = 384
ROWS = 192
VMEM = 56 * 2**20
NEG = -1e30
PER_MICRO = 1e6
SCALE = HD**-0.5
ORDER = (0, 1, 3, 2)


def nt(a, b):
    return lax.dot_general(a, b, (((1,), (1,)), ((), ())), preferred_element_type=F32)


def nn(a, b):
    return lax.dot_general(a, b, (((1,), (0,)), ((), ())), preferred_element_type=F32)


def tn(a, b):
    return lax.dot_general(a, b, (((0,), (0,)), ((), ())), preferred_element_type=F32)


def normalize(value):
    centred = value - jnp.mean(value, axis=-1, keepdims=True)
    inverse = lax.rsqrt(jnp.mean(centred * centred, axis=-1, keepdims=True) + 1e-05)
    return centred * inverse, inverse


def norm_back(grad_out, scaled, inverse, gain):
    scaled_grad = grad_out * gain
    centre = jnp.mean(scaled_grad, axis=-1, keepdims=True)
    along = jnp.mean(scaled_grad * scaled, axis=-1, keepdims=True)
    return inverse * (scaled_grad - centre - scaled * along)


def colsum(value):
    return jnp.sum(value, axis=0, keepdims=True)


def call(body, outs, scalars, *args, scratch=(), specs=None, micros=1.0, name=None):
    shapes = [jax.ShapeDtypeStruct(s, d) for s, d in outs]
    moved = sum(int(np.prod(a.shape)) * a.dtype.itemsize for a in list(args) + shapes)
    return pl.pallas_call(
        body,
        grid_spec=pltpu.PrefetchScalarGridSpec(
            num_scalar_prefetch=1,
            grid=(1,),
            in_specs=[
                (specs or {}).get(i, pl.BlockSpec(memory_space=pltpu.VMEM))
                for i in range(len(args))
            ],
            out_specs=[pl.BlockSpec(memory_space=pltpu.VMEM) for _ in shapes],
            scratch_shapes=list(scratch),
        ),
        out_shape=shapes,
        compiler_params=pltpu.CompilerParams(vmem_limit_bytes=VMEM),
        cost_estimate=pl.CostEstimate(
            flops=int(micros * PER_MICRO), bytes_accessed=moved // 1024, transcendentals=0
        ),
        name=name,
    )(scalars, *args)


OWN_ROWS = pl.BlockSpec((SEQ, D), lambda i, at: (at[3], 0))
OUT_ROWS = pl.BlockSpec((LW, D), lambda i, at: (3, 0))
QKV_ROWS = pl.BlockSpec((3 * LW, D), lambda i, at: (0, 0))
CORE, X_AT, Z_AT, Y_AT, MASKS = 0, 1, 2, 3, 4


def pack_body(
    at,
    qkv_weight,
    out_weight,
    qkv_bias,
    up_weight,
    down_weight,
    up_bias,
    mine,
    theirs,
    hidden,
    rows,
):
    core = lax.axis_index("c")
    for t in range(3):
        rows[LW * t : LW * t + LW, :] = qkv_weight[t]
    rows[3 * LW :, :] = out_weight[...]
    lane = lax.broadcasted_iota(jnp.int32, (8, D), 1)
    low = (lane % HD) < 32
    given = qkv_bias[...].astype(F32)
    none = jnp.zeros((1, LW), F32)
    bias = jnp.concatenate([given[0:1], none, given[1:2], none], axis=1)
    bias = jnp.broadcast_to(bias, (8, D))
    parts = (
        jnp.where(low, bias, 0.0),
        jnp.where(low, pltpu.roll(bias, D - 32, 1), 0.0),
    )

    def fill(ref, half):
        for g in range(12):
            ref[32 * g : 32 * g + 32, :] = rows[64 * g + 32 * half : 64 * g + 32 * half + 32, :]
        part = parts[half]
        shifted = pltpu.roll(part, 32, 1)
        ref[384:400, :] = jnp.concatenate(
            [part[0:1], shifted[0:1], jnp.zeros((14, D), F32)], axis=0
        ).astype(BF)

    @pl.when(core == 0)
    def _():
        fill(mine, 0)
        fill(theirs, 1)

    @pl.when(core != 0)
    def _():
        fill(mine, 1)
        fill(theirs, 0)

    start = pl.multiple_of(core * HALF_FF, HALF_FF)
    hidden[0:HALF_FF, :] = up_weight[:, pl.ds(start, HALF_FF)].T
    hidden[HALF_FF : 2 * HALF_FF, :] = down_weight[pl.ds(start, HALF_FF), :]
    up_row = up_bias[...].astype(F32).reshape(1, D)
    up_part = jnp.where(core == 0, up_row[:, 0:HALF_FF], up_row[:, HALF_FF:])
    hidden[2 * HALF_FF : 2 * HALF_FF + 16, :] = jnp.concatenate(
        [
            jnp.concatenate([up_part, jnp.zeros((1, D - HALF_FF), F32)], axis=1),
            jnp.zeros((15, D), F32),
        ],
        axis=0,
    ).astype(BF)


def masks_body(at, cot, dy, keep_col):
    kept = [at[MASKS + 4 * at[Y_AT] + g].astype(F32) for g in range(4)]
    for g in range(4):
        rows = slice(g * SPATIAL, (g + 1) * SPATIAL)
        dy[rows, :] = (cot[rows, :].astype(F32) * kept[g]).astype(BF)
        keep_col[rows, :] = jnp.full((SPATIAL, 1), kept[g])


def attend_forward_body(first, at, *refs):
    if first:
        x, gain, shift, wm, wp, keep, h1, w, qkv, o, logs = refs
        for r in range(0, SEQ, 96):
            scaled, _ = normalize(x[r : r + 96, :].astype(F32))
            h1[r : r + 96, :] = (scaled * gain[0:1, :] + shift[0:1, :]).astype(BF)
    else:
        h1, wm, wp, keep, w, qkv, o, logs = refs
    for g in range(12):
        w[64 * g : 64 * g + 32, :] = wm[32 * g : 32 * g + 32, :]
        w[64 * g + 32 : 64 * g + 64, :] = wp[32 * g : 32 * g + 32, :]
    bias = (wm[384:385, :] + wp[385:386, :])[:, : 3 * LW].astype(F32)
    for r in range(0, SEQ, ROWS):
        qkv[r : r + ROWS, :] = (nt(h1[r : r + ROWS, :], w[0 : 3 * LW, :]) + bias).astype(BF)
    mask = ((1.0 - keep[...]) * NEG).astype(BF)
    ones = jnp.ones((SEQ, 1), BF)
    rest = jnp.zeros((SEQ, HD - 1), BF)
    for h in range(LH):
        a = HD * h
        keys = jnp.concatenate([qkv[:, LW + a : LW + a + HD], mask, rest], axis=1)
        queries = jnp.concatenate(
            [qkv[:, a : a + HD] * jnp.asarray(SCALE, BF), ones, rest], axis=1
        )
        scores = nt(queries, keys)
        peak = jnp.max(scores, axis=-1, keepdims=True)
        expos = jnp.exp(scores - peak)
        total = jnp.sum(expos, axis=-1, keepdims=True)
        probs = (expos * (1.0 / total)).astype(BF)
        o[:, a : a + HD] = nn(probs, qkv[:, 2 * LW + a : 2 * LW + a + HD]).astype(BF)
        logs[:, h : h + 1] = peak + jnp.log(total)


def attend_forward(first, scalars, lead, wm, wp, keep):
    outs = [((D, D), BF), ((SEQ, 3 * LW), BF), ((SEQ, LW), BF), ((SEQ, 128), F32)]
    if first:
        outs = [((SEQ, D), BF)] + outs
    return call(
        functools.partial(attend_forward_body, first),
        outs,
        scalars,
        *lead,
        wm,
        wp,
        keep,
        specs={0: OWN_ROWS} if first else None,
        micros=8,
        name="attend_forward",
    )


def middle_body(at, *refs):
    x, bias, gain, shift = refs[:4]
    outs_of = refs[4:8]
    weights = refs[8:12]
    mid, h2 = refs[12:]
    for r in range(0, SEQ, ROWS):
        total = x[r : r + ROWS, :].astype(F32) + bias[...].astype(F32)
        for k in range(4):
            total = total + nn(outs_of[k][r : r + ROWS, :], weights[k][...])
        mid[r : r + ROWS, :] = total
        scaled, _ = normalize(total)
        h2[r : r + ROWS, :] = (scaled * gain[1:2, :] + shift[1:2, :]).astype(BF)


def feed_body(at, h2o, h2p, dyo, dyp, shards, grads, mo, mp, dho, dhp, ubias, *scratch):
    h2, dy, wu, wd, act, dhid, accm, acch = scratch
    owners = [lax.rem(at[Y_AT] + 4 - k, 4) for k in range(4)]
    h2[0:SEQ, :] = h2o[...]
    h2[SEQ:, :] = h2p[...]
    dy[0:SEQ, :] = dyo[...]
    dy[SEQ:, :] = dyp[...]
    block = 2 * SEQ
    for pair in range(2):
        one, two = (shards.at[owners[ORDER[2 * pair + s]]] for s in range(2))
        wu[0:HALF_FF, :] = one[0:HALF_FF, :]
        wu[HALF_FF:, :] = two[0:HALF_FF, :]
        wd[0:HALF_FF, :] = one[HALF_FF : 2 * HALF_FF, :]
        wd[HALF_FF:, :] = two[HALF_FF : 2 * HALF_FF, :]
        bias = jnp.concatenate(
            [one[768:784, 0:HALF_FF][0:1], two[768:784, 0:HALF_FF][0:1]], axis=1
        ).astype(F32)
        ubias[pair] = jnp.zeros((8, D), F32)

        @pl.loop(0, 2 * SEQ // block)
        def _(i):
            rows = pl.ds(pl.multiple_of(i * block, block), block)
            hid = nt(h2[rows, :], wu[...]) + bias
            cdf = 0.5 + 0.5 * lax.erf(hid * np.float32(0.7071067811865476))
            active = (hid * cdf).astype(BF)
            slope = cdf + hid * (
                jnp.exp(hid * hid * np.float32(-0.5)) * np.float32(0.3989422804014327)
            )
            act[rows, :] = active
            hid_grad = (nt(dy[rows, :], wd[...]) * slope).astype(BF)
            dhid[rows, :] = hid_grad
            ubias[pair, 0:1, :] += colsum(hid_grad.astype(F32))
            down = nn(active, wd[...])
            back = nn(hid_grad, wu[...])
            if pair == 0:
                accm[rows, :] = down
                acch[rows, :] = back
            else:
                accm[rows, :] += down
                acch[rows, :] += back

        for s in range(2):
            k = ORDER[2 * pair + s]
            cols = slice(s * HALF_FF, (s + 1) * HALF_FF)
            up_grad = tn(dhid[:, cols], h2[...])
            down_grad = tn(act[:, cols], dy[...])
            for q in range(8):
                rows = slice(48 * q, 48 * q + 48)
                grads[q, k] = up_grad[rows, :]
                grads[8 + q, k] = down_grad[rows, :]
    mo[...] = accm[0:SEQ, :]
    mp[...] = accm[SEQ:, :]
    dho[...] = acch[0:SEQ, :]
    dhp[...] = acch[SEQ:, :].astype(BF)


def feed(scalars, h2o, h2p, dyo, dyp, shards):
    big = (2 * SEQ, D)
    return call(
        feed_body,
        [
            ((16, 4, 48, D), F32),
            ((SEQ, D), F32),
            ((SEQ, D), F32),
            ((SEQ, D), F32),
            ((SEQ, D), BF),
            ((2, 8, D), F32),
        ],
        scalars,
        h2o,
        h2p,
        dyo,
        dyp,
        shards,
        scratch=[
            pltpu.VMEM(big, BF),
            pltpu.VMEM(big, BF),
            pltpu.VMEM((D, D), BF),
            pltpu.VMEM((D, D), BF),
            pltpu.VMEM(big, BF),
            pltpu.VMEM(big, BF),
            pltpu.VMEM(big, F32),
            pltpu.VMEM(big, F32),
        ],
        micros=30,
        name="feed",
    )


def result_body(at, middle, down, other, bias, out):
    total = middle[...] + (down[...] + other[...] + bias[...].astype(F32))
    low = total.astype(BF)
    for q in range(4):
        out[q] = low


def spread_body(at, a, b, c, d, out):
    total = ((a[...] + b[...]) + (c[...] + d[...])).astype(out.dtype)
    for q in range(16):
        out[q] = total


def hidden_out_body(at, mine, theirs, up, down):
    for ref, core in ((mine, at[CORE]), (theirs, 1 - at[CORE])):
        start = pl.multiple_of(core * HALF_FF, HALF_FF)
        half = jnp.concatenate([ref[q] for q in range(8)], axis=0).astype(F32)
        up[:, pl.ds(start, HALF_FF)] = half.T
        for q in range(8):
            row = pl.multiple_of(start + 48 * q, 16)
            down[pl.ds(row, 48), :] = ref[8 + q].astype(F32)


def middle_back_body(at, *refs):
    dho, dhp, mid, gain, dy = refs[:5]
    outs_of = refs[5:9]
    weights = refs[9:13]
    dmid, gm, gp, small = refs[13:17]
    outs_grad = refs[17:21]
    da = refs[21]
    gain_sum = shift_sum = bias_sum = down_sum = jnp.zeros((1, D), F32)
    for r in range(0, SEQ, ROWS):
        at = slice(r, r + ROWS)
        grad = dho[at, :] + dhp[at, :].astype(F32)
        scaled, inverse = normalize(mid[at, :])
        out_grad = dy[at, :].astype(F32)
        total = out_grad + norm_back(grad, scaled, inverse, gain[1:2, :])
        dmid[at, :] = total
        low = total.astype(BF)
        da[at, :] = low
        gain_sum += colsum(grad * scaled)
        shift_sum += colsum(grad)
        bias_sum += colsum(low.astype(F32))
        down_sum += colsum(out_grad)
        for k in range(4):
            outs_grad[k][at, :] = nt(low, weights[k][...]).astype(BF)
    for k in range(4):
        weight_grad = tn(outs_of[k][...], da[...])
        for h in range(LH):
            gm[k, 32 * h : 32 * h + 32, :] = weight_grad[64 * h : 64 * h + 32, :]
            gp[k, 32 * h : 32 * h + 32, :] = weight_grad[64 * h + 32 : 64 * h + 64, :]
    small[...] = jnp.concatenate(
        [gain_sum, shift_sum, bias_sum, down_sum, jnp.zeros((4, D), F32)], axis=0
    )


def in_three(value):
    one = value.astype(BF)
    left = value - one.astype(F32)
    two = left.astype(BF)
    return [one, two, (left - two.astype(F32)).astype(BF)]


def attend_backward_body(sc, qkv, logs, o, do, keep, h1, dqkv, gm, gp, bias):
    mask = ((1.0 - keep[...]) * NEG).astype(BF)
    ones = jnp.ones((SEQ, 3), BF)
    rest = jnp.zeros((SEQ, HD - 4), BF)
    for h in range(LH):
        a = HD * h
        heads_grad = do[:, a : a + HD]
        inner = jnp.sum(
            heads_grad.astype(F32) * o[:, a : a + HD].astype(F32), axis=-1, keepdims=True
        )
        keys = qkv[:, LW + a : LW + a + HD]
        vals = qkv[:, 2 * LW + a : 2 * LW + a + HD]
        queries = qkv[:, a : a + HD] * jnp.asarray(SCALE, BF)
        logits = nt(
            jnp.concatenate([keys, ones, mask, rest], axis=1),
            jnp.concatenate(
                [queries] + in_three(-logs[:, h : h + 1]) + [ones[:, 0:1], rest], axis=1
            ),
        )
        probs = jnp.exp(logits)
        centred = nt(
            jnp.concatenate([vals, ones, ones[:, 0:1], rest], axis=1),
            jnp.concatenate(
                [heads_grad] + in_three(-inner) + [jnp.zeros((SEQ, 1), BF), rest], axis=1
            ),
        )
        score_grad = (probs * centred).astype(BF)
        dqkv[:, 2 * LW + a : 2 * LW + a + HD] = nn(probs.astype(BF), heads_grad).astype(BF)
        dqkv[:, LW + a : LW + a + HD] = nn(score_grad, queries).astype(BF)
        dqkv[:, a : a + HD] = (tn(score_grad, keys) * SCALE).astype(BF)
    bias[...] = jnp.broadcast_to(colsum(dqkv[...].astype(F32)), (8, 3 * LW))
    weight_grad = tn(dqkv[...], h1[...])
    for g in range(3 * LH):
        gm[32 * g : 32 * g + 32, :] = weight_grad[64 * g : 64 * g + 32, :]
        gp[32 * g : 32 * g + 32, :] = weight_grad[64 * g + 32 : 64 * g + 64, :]


def attend_backward(scalars, qkv, logs, o, do, keep, h1):
    return call(
        attend_backward_body,
        [((SEQ, 3 * LW), BF), ((288, D), F32), ((288, D), F32), ((8, 3 * LW), F32)],
        scalars,
        qkv,
        logs,
        o,
        do,
        keep,
        h1,
        micros=8,
        name="attend_backward",
    )


def first_back_body(sc, *refs):
    x, gain, dmid, small_two = refs[:4]
    dqkvs = refs[4:8]
    weights = refs[8:12]
    biases = refs[12:16]
    grad_in, small = refs[16:]
    gain_sum = shift_sum = jnp.zeros((1, D), F32)
    for r in range(0, SEQ, ROWS):
        at = slice(r, r + ROWS)
        grad = nn(dqkvs[0][at, :], weights[0][...])
        for k in range(1, 4):
            grad += nn(dqkvs[k][at, :], weights[k][...])
        scaled, inverse = normalize(x[at, :].astype(F32))
        total = dmid[at, :] + norm_back(grad, scaled, inverse, gain[0:1, :])
        grad_in[at, :] = total.astype(BF)
        gain_sum += colsum(grad * scaled)
        shift_sum += colsum(grad)
    rest = jnp.zeros((1, D - 3 * LW), F32)
    small[...] = jnp.concatenate(
        [gain_sum, shift_sum, small_two[0:4, :]]
        + [jnp.concatenate([biases[k][0:1, :], rest], axis=1) for k in range(4)]
        + [jnp.zeros((6, D), F32)],
        axis=0,
    )


def heads_send_body(ks, sc, *refs):
    mine, theirs = refs[0:4], refs[4:8]
    out_mine, out_theirs, send = refs[8:11]
    for p in range(16):
        parts = []
        for j, k in enumerate(ks):
            if p < 12:
                rows = slice(24 * p, 24 * p + 24)
                parts.append(mine[j][rows, :] + theirs[j][rows, :])
            else:
                rows = slice(24 * (p - 12), 24 * (p - 12) + 24)
                parts.append(out_mine[k, rows, :] + out_theirs[k, rows, :])
        send[p] = jnp.concatenate(parts, axis=0).astype(BF)


def heads_fold_body(sc, got, small, small_other, sums, *to_y):
    total = got[0].astype(F32)
    for q in range(1, 16):
        total += got[q].astype(F32)
    parts = [total[24 * j : 24 * j + 24] for j in range(4)]
    common = small[0:6, :] + small_other[0:6, :]
    crossed = pltpu.roll(small_other[...], D - 32, 1)
    rest = jnp.zeros((1, D - HALF_FF), F32)
    for k in range(4):
        place = ORDER.index(k)
        lanes = slice((place % 2) * HALF_FF, (place % 2 + 1) * HALF_FF)
        hidden = jnp.concatenate([sums[place // 2, 0:1, lanes], rest], axis=1)
        heads_bias = small[6 + k : 7 + k, :] + crossed[6 + k : 7 + k, :]
        to_y[k][0:24, :] = parts[place]
        to_y[k][24:32, :] = jnp.concatenate([common, heads_bias, hidden], axis=0)


def heads_out_body(
    sc, mine, theirs, qkv_grad, out_grad, out_sum, down_sum, gains, biases, up_sum, qkv_sum, rows
):
    sums = []
    for ref, core in ((mine, sc[CORE]), (theirs, 1 - sc[CORE])):
        for p in range(16):
            for g in range(3):
                at = 24 * p + 8 * g
                row = pl.multiple_of(64 * (at // 32) + 32 * core + at % 32, 8)
                rows[pl.ds(row, 8), :] = ref[p, 8 * g : 8 * g + 8, :]
        total = ref[0, 24:32, :]
        for p in range(1, 16):
            total += ref[p, 24:32, :]
        sums.append(total)
    for t in range(3):
        qkv_grad[t] = rows[LW * t : LW * t + LW, :]
    out_grad[...] = rows[3 * LW :, :]
    own, other = sums
    gains[...] = jnp.concatenate([own[0:1], own[2:3]], axis=0)
    biases[...] = jnp.concatenate([own[1:2], own[3:4]], axis=0)
    out_sum[...] = own[4:5].reshape(D)
    down_sum[...] = own[5:6].reshape(D)
    low = (lax.broadcasted_iota(jnp.int32, (8, D), 1) % HD) < 32
    swap = sc[CORE] != 0
    hidden = (own[7:8, 0:HALF_FF], other[7:8, 0:HALF_FF])
    up_sum[...] = jnp.concatenate(
        [jnp.where(swap, hidden[1], hidden[0]), jnp.where(swap, hidden[0], hidden[1])], axis=1
    ).reshape(D)
    first = jnp.where(sc[CORE] == 0, own, other)
    second = jnp.where(sc[CORE] == 0, other, own)
    natural = jnp.where(low, first, pltpu.roll(second, 32, 1))[6:7]
    qkv_sum[...] = jnp.concatenate([natural[:, 0:LW], natural[:, 2 * LW : 3 * LW]], axis=0)


def along_y(value, step):
    return lax.ppermute(value, "y", [(i, (i + step) % 4) for i in range(4)])


def after(value, *done):
    return lax.optimization_barrier((value, *done))[0]


def other_core(value):
    return lax.ppermute(value, "c", [(0, 1), (1, 0)])


def per_device(
    tokens,
    qkv_weight,
    qkv_bias,
    out_weight,
    out_bias,
    up_weight,
    up_bias,
    down_weight,
    down_bias,
    norm_gains,
    norm_biases,
    cotangent,
    band_masks,
):
    core = lax.axis_index("c")
    here = lax.axis_index("y")
    at = jnp.concatenate(
        [
            jnp.stack([core, lax.axis_index("x"), lax.axis_index("z"), here]).astype(jnp.int32),
            band_masks.reshape(16),
        ]
    )
    four = range(4)
    mine, theirs, hidden = call(
        pack_body,
        [((400, D), BF), ((400, D), BF), ((784, D), BF)],
        jnp.zeros((1,), jnp.int32),
        jnp.swapaxes(qkv_weight, 1, 2),
        out_weight,
        qkv_bias,
        up_weight,
        down_weight,
        up_bias,
        scratch=[pltpu.VMEM((D, D), BF)],
        micros=5,
        name="pack",
    )
    heads_mine, heads_theirs = {0: mine}, {0: theirs}
    for s in (1, 3):
        heads_mine[s] = along_y(mine, s)
    relayed = [along_y(heads_mine[1][:200], 1), along_y(heads_mine[3][200:], 3)]
    shards = lax.all_gather(hidden, "y", axis=0, tiled=False)
    out_grad, keep_col = call(
        masks_body,
        [((SEQ, D), BF), ((SEQ, 1), F32)],
        at,
        cotangent,
        specs={0: OWN_ROWS},
        micros=2,
        name="masks",
    )
    out_grad_other = other_core(out_grad)

    weights, qkvs, outs_of, logs = {}, {}, {}, {}
    first_in, *rest = attend_forward(
        True, at, (tokens, norm_gains, norm_biases), heads_mine[0], heads_theirs[0], keep_col
    )
    weights[0], qkvs[0], outs_of[0], logs[0] = rest
    def forward(s, *done):
        weights[s], qkvs[s], outs_of[s], logs[s] = attend_forward(
            False, at, (after(first_in, *done),), heads_mine[s], heads_theirs[s], keep_col
        )

    for s in (1, 3):
        heads_theirs[s] = other_core(after(heads_mine[s], qkvs[0]))
    forward(1, qkvs[0])
    forward(3, qkvs[1])
    heads_mine[2] = jnp.concatenate(after(relayed, qkvs[1]), axis=0)
    heads_theirs[2] = other_core(heads_mine[2])
    forward(2, qkvs[3])
    middle, second_in = call(
        middle_body,
        [((SEQ, D), F32), ((SEQ, D), BF)],
        at,
        tokens,
        out_bias[None],
        norm_gains,
        norm_biases,
        *[outs_of[k] for k in four],
        *[weights[k] for k in four],
        specs={0: OWN_ROWS} | {8 + k: OUT_ROWS for k in four},
        micros=4,
        name="middle",
    )
    second_other = other_core(second_in)
    hidden_grads, down_own, down_other, back_own, back_other, up_sums = feed(
        at, second_in, second_other, out_grad, out_grad_other, shards
    )
    back_received = other_core(back_other)
    hidden_pieces = lax.psum_scatter(
        hidden_grads.reshape(16, 4 * 48, D), ("x", "z"), scatter_dimension=0, tiled=False
    ).reshape(4, 48, D)
    down_received = other_core(after(down_other, back_received))

    middle_grad, out_gm, out_gp, small_two, *outs_grad = call(
        middle_back_body,
        [((SEQ, D), F32), ((4, 96, D), F32), ((4, 96, D), F32), ((8, D), F32)]
        + [((SEQ, LW), BF)] * 4,
        at,
        back_own,
        back_received,
        middle,
        norm_gains,
        out_grad,
        *[outs_of[k] for k in four],
        *[weights[k] for k in four],
        specs={9 + k: OUT_ROWS for k in four},
        scratch=[pltpu.VMEM((SEQ, D), BF)],
        micros=7,
        name="middle_back",
    )
    out_received = other_core(out_gp)
    (result_copies,) = call(
        result_body,
        [((4, SEQ, D), BF)],
        at,
        middle,
        after(down_own, small_two),
        down_received,
        down_bias[None],
        micros=2,
        name="result_rows",
    )
    result = lax.all_to_all(result_copies, "y", 0, 0, tiled=True).reshape(4 * SEQ, D)
    dqkvs, gms, gps, bias_sums = {}, {}, {}, {}

    def backward(s, *done):
        heads_grad = after(outs_grad[s], *done)
        dqkvs[s], gms[s], gp, bias_sums[s] = attend_backward(
            at, qkvs[s], logs[s], outs_of[s], heads_grad, keep_col, first_in
        )
        gps[s] = other_core(gp)

    def heads_send(ks, *done):
        (send,) = call(
            functools.partial(heads_send_body, ks),
            [((16, 96, D), BF)],
            at,
            *[gms[k] for k in ks],
            *[gps[k] for k in ks],
            after(out_gm, *done),
            out_received,
            micros=4,
            name="heads_send",
        )
        return send

    backward(0, result_copies)
    backward(1, dqkvs[0])
    backward(3, dqkvs[1], gps[0])
    backward(2, dqkvs[3])
    grad_own, small = call(
        first_back_body,
        [((SEQ, D), BF), ((16, D), F32)],
        at,
        tokens,
        norm_gains,
        after(middle_grad, dqkvs[2]),
        small_two,
        *[dqkvs[k] for k in four],
        *[weights[k] for k in four],
        *[bias_sums[k] for k in four],
        specs={0: OWN_ROWS} | {8 + k: QKV_ROWS for k in four},
        micros=8,
        name="first_back",
    )
    small_other = other_core(small)
    hidden_pieces, small_other = lax.optimization_barrier((hidden_pieces, small_other))
    (hidden_copies,) = call(
        spread_body,
        [((16, 48, D), BF)],
        at,
        hidden_pieces[0],
        *[along_y(hidden_pieces[s], -s) for s in (1, 2, 3)],
        micros=2,
        name="hidden_spread",
    )
    send, result = lax.optimization_barrier((heads_send(ORDER, small), result))
    heads_got = lax.all_to_all(send, ("x", "z"), 0, 0, tiled=True)
    input_grad = lax.all_gather(grad_own, "y", axis=0, tiled=True).astype(F32)
    to_y = call(
        heads_fold_body,
        [((32, D), F32)] * 4,
        at,
        heads_got,
        small,
        small_other,
        up_sums,
        micros=3,
        name="heads_fold",
    )
    hidden_half = lax.all_to_all(after(hidden_copies, *to_y), ("x", "z"), 0, 0, tiled=True)
    (heads_copies,) = call(
        spread_body,
        [((16, 32, D), F32)],
        at,
        to_y[0],
        *[along_y(to_y[s], -s) for s in (1, 2, 3)],
        micros=2,
        name="heads_spread",
    )
    heads_half = lax.all_to_all(heads_copies, ("x", "z"), 0, 0, tiled=True)
    up_weight_grad, down_weight_grad = call(
        hidden_out_body,
        [((D, D), F32), ((D, D), F32)],
        at,
        hidden_half,
        other_core(hidden_half),
        micros=4,
        name="hidden_out",
    )
    keep_rows = jnp.repeat(band_masks, SPATIAL, axis=1).reshape(-1, 1)
    heads_half_sent, input_grad, up_weight_grad, down_weight_grad, result = (
        lax.optimization_barrier(
            (
                heads_half,
                input_grad,
                up_weight_grad,
                down_weight_grad,
                jnp.where(keep_rows > 0, result, jnp.asarray(0, BF)),
            )
        )
    )
    heads_half_other = other_core(heads_half_sent)
    qkv_grad, out_weight_grad, out_sum, down_sum, gains, biases, up_sum, qkv_sum = call(
        heads_out_body,
        [
            ((3, LW, D), F32),
            ((LW, D), F32),
            ((D,), F32),
            ((D,), F32),
            ((2, D), F32),
            ((2, D), F32),
            ((D,), F32),
            ((2, LW), F32),
        ],
        at,
        heads_half,
        heads_half_other,
        scratch=[pltpu.VMEM((D, D), F32)],
        micros=4,
        name="heads_out",
    )
    return (
        result,
        input_grad,
        jnp.swapaxes(qkv_grad, 1, 2),
        qkv_sum,
        out_weight_grad,
        out_sum,
        up_weight_grad,
        up_sum,
        down_weight_grad,
        down_sum,
        gains,
        biases,
    )


def solution(mesh):
    inner = Mesh(np.array(mesh.devices).reshape(4, 4, 2, 4), ("x", "z", "c", "y"))
    dp = ("x", "z", "c")
    in_specs = (
        P(dp, None),
        P(None, None, "y"),
        P(None, "y"),
        P("y", None),
        P(),
        P(None, "y"),
        P("y"),
        P("y", None),
        P(),
        P(),
        P(),
        P(dp, None),
        P(dp, None),
    )
    out_specs = (
        P(dp, None),
        P(dp, None),
        P(None, None, "y"),
        P(None, "y"),
        P("y", None),
        P(),
        P(None, "y"),
        P("y"),
        P("y", None),
        P(),
        P(),
        P(),
    )
    return jax.shard_map(
        per_device, mesh=inner, in_specs=in_specs, out_specs=out_specs, check_vma=False
    )
```
